32 devices in a mesh: groups: 2 (over y), space: 4 (over z), batch: 4 (over x, core).
Axes of the slice: x: 2, y: 2, z: 4, core: 2. Of those that a mesh axis runs over, the one named last changes fastest.
Arguments:
- fields: bfloat16 [8, 32, 64, 128], P(('groups', 'batch'), 'space'), parts along dimension 0, may hold values from -36 to 36
- land: int32 [32, 64], P('space'), may hold values 0 or 1
- conv_in: bfloat16 [9, 128, 128], replicated, may hold values from -0.1875 to 0.1875
- conv_out: bfloat16 [9, 128, 128], replicated, may hold values from -0.1875 to 0.1875
- batchnorm_gain: float32 [128], replicated, may hold values from 0.25 to 1.75
- batchnorm_offset: float32 [128], replicated, may hold values from -3 to 3
- target_grad: bfloat16 [8, 32, 64, 128], P(('groups', 'batch'), 'space'), parts along dimension 0, may hold values from -6 to 6
Outputs:
- output: bfloat16 [8, 32, 64, 128], P(('groups', 'batch'), 'space'), parts along dimension 0
- grad_in: float32 [18, 128, 128], P('groups', None, 'batch'), parts along dimension 0
- grad_out: float32 [18, 128, 128], P('groups', None, 'batch'), parts along dimension 0
- gain_gradient: float32 [256], P('groups'), parts along dimension 0
- offset_gradient: float32 [256], P('groups'), parts along dimension 0
The draws below stay inside these ranges and needn't reach their ends.
There are 2 independent parts, one for each index of `groups`. The reference program is written for one: setup_inputs(seed, part) draws one part's arguments, and reference() takes and returns one part's arrays. A program takes and returns all parts, laid end to end along the dimension named above; an argument that names none is the same for every part. Nothing has to cross between parts.
All inputs are finite; a program needn't handle non-finite values. No bound on the sum of `land` on one device may be relied on, other than what follows from the above.
Results may differ from the reference program's by a relative error of at most 0.025.
Values may be sent and summed in bfloat16 or wider, within the bound.
A program may use at most 64 MiB of HBM per device.

```python
import jax
import jax.numpy as jnp
from jax import lax

CH = 128
LAT = 64
NX = 32
SAMPLES = 4


def draw_fields(key, part):
    first_key, second_key = jax.random.split(key, 2)
    shape = (SAMPLES, NX, LAT, CH)
    longitude = jnp.arange(NX, dtype=jnp.float32)[None, :, None, None]
    sample_pos = jnp.arange(SAMPLES, dtype=jnp.float32)[:, None, None, None]
    rough = jnp.exp(jax.random.uniform(second_key, (SAMPLES, NX, LAT, 1), jnp.float32, -0.8, 0.8))
    scales = (0.5 + 1.5 * longitude / NX) * (0.5 + 1.5 * sample_pos / SAMPLES) * rough
    base = jax.random.truncated_normal(first_key, -4.0, 4.0, shape, jnp.float32)
    return (base * scales).astype(jnp.bfloat16)


def with_ends(values, own_key, smallest, largest):
    place = [jax.random.randint(jax.random.fold_in(own_key, axis), (), 0, length) for axis, length in enumerate(values.shape)]
    widest = values.shape.index(max(values.shape))
    next_to = place[:widest] + [(place[widest] + 1) % values.shape[widest]] + place[widest + 1:]
    return values.at[tuple(place)].set(smallest).at[tuple(next_to)].set(largest)


def with_spikes(values, rng, source, target, blocks, factor):
    owner, partner = [(jnp.arange(values.shape[axis_at]) // (values.shape[axis_at] // blocks)).reshape([-1 if axis == axis_at else 1 for axis in range(values.ndim)]) for axis_at in (source, target)]
    chosen = jax.random.permutation(rng, blocks)[partner]
    strong = (owner == chosen) | (owner == (partner + blocks // 2) % blocks)
    return jnp.where(strong, factor * values, values)


def block_levels(key, shape, shards, least, largest):
    gain = 1.0
    for axis_at, parts in shards:
        steps = jax.random.uniform(jax.random.fold_in(jax.random.fold_in(key, 6), axis_at), (parts,), jnp.float32, least / len(shards), largest / len(shards))
        gain = gain * jnp.repeat(jnp.exp(steps), shape[axis_at] // parts).reshape((-1,) + (1,) * (len(shape) - 1 - axis_at))
    return gain


def centred(key, extent, deviation, most, cuts=(), held_as=jnp.bfloat16):
    values = jax.random.normal(key, extent, jnp.float32) * deviation
    if len(cuts) > 0:
        values = block_levels(key, extent, cuts, -0.22, 0.18) * values
    return jnp.clip(values, min=-most, max=most).astype(held_as)


def gaussian_with(key, extent, scale, limit, pieces, heavy, kind=jnp.bfloat16):
    drawn = scale * jax.random.normal(key, extent, jnp.float32)
    if pieces:
        drawn = drawn * block_levels(key, extent, pieces, -0.22, 0.18)
    return jnp.clip(with_spikes(drawn, jax.random.fold_in(key, 3), *heavy), -limit, limit).astype(kind)


def setup_inputs(seed: int = 0, part: int = 0) -> dict:
    splits = jax.random.split(jax.random.key(seed), 8)
    part_splits = jax.random.split(jax.random.fold_in(splits[7], part), 8)
    return {
        "fields": draw_fields(jax.random.fold_in(jax.random.fold_in(splits[7], part), 71), part),
        "land": with_ends((jax.random.randint(splits[1], (NX, LAT), 0, 4) < 3).astype(jnp.int32), jax.random.fold_in(splits[1], 1), 0, 1),
        "conv_in": centred(splits[2], (9, CH, CH), (9 * CH) ** -0.5, 0.1875),
        "conv_out": centred(splits[3], (9, CH, CH), (9 * CH) ** -0.5, 0.1875),
        "batchnorm_gain": jnp.clip(1.0 + 0.15 * jax.random.normal(splits[4], (CH,), jnp.float32), 0.25, 1.75),
        "batchnorm_offset": centred(splits[5], (CH,), 0.5, 3.0, (), jnp.float32),
        "target_grad": gaussian_with(part_splits[6], (SAMPLES, NX, LAT, CH), 1.0, 6.0, ((0, 4), (1, 4)), (0, 3, 4, 2.0)),
    }


def pad_field(field):
    ghost = jnp.flip(field[:, :, -1:, :], axis=1)
    south = jnp.zeros_like(field[:, :, :1, :])
    extended = jnp.concatenate([south, field, ghost], axis=2)
    return jnp.concatenate([extended[:, -1:], extended, extended[:, :1]], axis=1)

def convolve(padded, weights, lon, lat):
    chans = padded.shape[3]
    total = jnp.zeros((padded.shape[0] * lon * lat, weights.shape[2]), jnp.float32)
    for tap in range(9):
        first, second = (tap // 3, tap % 3)
        piece = padded[:, first:first + lon, second:second + lat, :].reshape(-1, chans)
        total = total + jnp.dot(piece, weights[tap], preferred_element_type=jnp.float32)
    return total.reshape(padded.shape[0], lon, lat, weights.shape[2])

def adjoint_conv(padded, weights, lon, lat):
    chans = padded.shape[3]
    ghost_row = padded[:, :, lat + 1, :]
    cleared = padded.at[:, :, lat + 1, :].set(jnp.zeros_like(ghost_row))
    total = jnp.zeros((padded.shape[0] * lon * lat, weights.shape[1]), jnp.float32)
    for tap in range(9):
        first, second = (tap // 3, tap % 3)
        piece = cleared[:, 2 - first:2 - first + lon, 2 - second:2 - second + lat, :].reshape(-1, chans)
        total = total + jnp.dot(piece, weights[tap].T, preferred_element_type=jnp.float32)
    total = total.reshape(padded.shape[0], lon, lat, weights.shape[1])
    extra = jnp.zeros((padded.shape[0] * lon, weights.shape[1]), jnp.float32)
    for first in range(3):
        piece = ghost_row[:, first:first + lon, :].reshape(-1, chans)
        extra = extra + jnp.dot(piece, weights[3 * first + 2].T, preferred_element_type=jnp.float32)
    extra = extra.reshape(padded.shape[0], lon, weights.shape[1])
    return total.at[:, :, lat - 1, :].add(extra)

def tap_grads(padded, grad, lon, lat):
    chans = padded.shape[3]
    flat = grad.reshape(-1, grad.shape[3])
    result = []
    for tap in range(9):
        first, second = (tap // 3, tap % 3)
        piece = padded[:, first:first + lon, second:second + lat, :].reshape(-1, chans)
        result.append(lax.dot_general(piece, flat, (((0,), (0,)), ((), ())), preferred_element_type=jnp.float32))
    return jnp.stack(result, axis=0)

def gelu_value(value):
    inner = 0.7978845608 * (value + 0.044715 * value * value * value)
    return 0.5 * value * (1.0 + jnp.tanh(inner))

def gelu_slope(value):
    inner = 0.7978845608 * (value + 0.044715 * value * value * value)
    hyper = jnp.tanh(inner)
    return 0.5 * (1.0 + hyper) + 0.5 * value * (1.0 - hyper * hyper) * 0.7978845608 * (1.0 + 3.0 * 0.044715 * value * value)

def reference(fields, land, conv_in, conv_out, batchnorm_gain, batchnorm_offset, target_grad):
    lon, lat = (fields.shape[1], fields.shape[2])
    ocean_mask = land.astype(jnp.float32)[None, :, :, None]
    masked = fields * ocean_mask.astype(jnp.bfloat16)
    padded_in = pad_field(masked)
    first = convolve(padded_in, conv_in, lon, lat).astype(jnp.bfloat16)
    first_features = first.astype(jnp.float32)
    element_count = jnp.sum(land.astype(jnp.float32)) * fields.shape[0]
    channel_mean = lax.optimization_barrier(jnp.sum(first_features * ocean_mask, axis=(0, 1, 2))) / element_count
    var = lax.optimization_barrier(jnp.sum(first_features * first_features * ocean_mask, axis=(0, 1, 2))) / element_count - channel_mean * channel_mean
    inverse_deviation = lax.rsqrt(var + 1e-05)
    normalized_input = (first_features - channel_mean) * inverse_deviation
    preactivation = batchnorm_gain * normalized_input + batchnorm_offset
    act = (gelu_value(preactivation) * ocean_mask).astype(jnp.bfloat16)
    padded_act = pad_field(act)
    output = (convolve(padded_act, conv_out, lon, lat) * ocean_mask).astype(jnp.bfloat16)
    dout = (target_grad.astype(jnp.float32) * ocean_mask * lax.rsqrt(element_count)).astype(jnp.bfloat16)
    grad_out = tap_grads(padded_act, dout, lon, lat)
    dact = adjoint_conv(pad_field(dout), conv_out, lon, lat)
    preactivation_gradient = dact * ocean_mask * gelu_slope(preactivation)
    offset_gradient = lax.optimization_barrier(jnp.sum(preactivation_gradient, axis=(0, 1, 2)))
    gain_gradient = lax.optimization_barrier(jnp.sum(preactivation_gradient * normalized_input, axis=(0, 1, 2)))
    first_layer_gradient = (ocean_mask * batchnorm_gain * inverse_deviation * (preactivation_gradient - (offset_gradient + normalized_input * gain_gradient) / element_count)).astype(jnp.bfloat16)
    grad_in = tap_grads(padded_in, first_layer_gradient, lon, lat)
    return (output, grad_in, grad_out, gain_gradient, offset_gradient)
```

```python
import functools

import jax
import jax.numpy as jnp
from jax import lax
from jax.experimental import pallas as pl
from jax.experimental.pallas import tpu as pltpu
from jax.sharding import PartitionSpec as P

F32 = jnp.float32
BF16 = jnp.bfloat16


def gelu_parts(value):
    inner = 0.7978845608 * (value + 0.044715 * value * value * value)
    hyper = jnp.tanh(inner)
    act = 0.5 * value * (1.0 + hyper)
    slope = 0.5 * (1.0 + hyper) + 0.5 * value * (1.0 - hyper * hyper) * 0.7978845608 * (
        1.0 + 3.0 * 0.044715 * value * value
    )
    return act, slope


def kernel(
    nz, nb, lon, lat, ch, units,
    fields, land, w_in, w_out, gain, offset, target,
    output, grad_in, grad_out, gain_gradient, offset_gradient,
    mask, first, dact, dpre, s_in, s_act, s_dout, w_back, dout_t,
    rows1, head1, tail1, west1, east1,
    rows2, head2, tail2, west2, east2,
    stats1, stats2,
    part_a, pair_a, half_a, cross_a, mine_a, ring_a, full_a,
    part_b, pair_b, half_b, cross_b, mine_b, ring_b, full_b,
    row_sems, col_sems, stat_sems, pair_sems, cross_sems, ring_sems, full_sems,
):
    nd = nz * nb
    nx = nb // 2
    cells = lon * lat
    z = lax.axis_index("space")
    b = lax.axis_index("batch")
    me = z * nb + b
    core = lax.rem(b, 2)
    col = b // 2
    other = 1 - core

    def device(zz, bb):
        return {"space": zz, "batch": bb}

    def copy(src, dst, send, recv, zz, bb):
        return pltpu.make_async_remote_copy(
            src_ref=src, dst_ref=dst, send_sem=send, recv_sem=recv,
            device_id=device(zz, bb), device_id_type=pl.DeviceIdType.MESH,
        )

    def over(count, fn):
        def step(k, carry):
            fn(k)
            return carry
        lax.fori_loop(1, count, step, 0)

    def row_copy(which, buf, slot, zz):
        return copy(buf.at[slot], buf.at[slot], row_sems.at[which, 0, zz],
                    row_sems.at[which, 1, slot], zz, b)

    def send_rows(which, buf):
        over(nz, lambda k: row_copy(which, buf, z, lax.rem(z + k, nz)).start())

    def recv_rows(which, buf):
        def one(k):
            src = lax.rem(z + k, nz)
            row_copy(which, buf, src, src).wait_recv()
        over(nz, one)

    def drain_rows(which, buf):
        over(nz, lambda k: row_copy(which, buf, z, lax.rem(z + k, nz)).wait_send())

    up = lax.rem(z + 1, nz)
    down = lax.rem(z + nz - 1, nz)

    def col_copies(which, head, tail, west, east):
        return (
            copy(head, east, col_sems.at[which, 0, 0], col_sems.at[which, 1, 0], down, b),
            copy(tail, west, col_sems.at[which, 0, 1], col_sems.at[which, 1, 1], up, b),
        )

    def stat_copy(which, buf, slot, peer):
        return copy(buf.at[slot], buf.at[slot], stat_sems.at[which, 0, peer],
                    stat_sems.at[which, 1, slot], peer // nb, lax.rem(peer, nb))

    def send_stats(which, buf):
        over(nd, lambda k: stat_copy(which, buf, me, lax.rem(me + k, nd)).start())

    def recv_stats(which, buf):
        def one(k):
            src = lax.rem(me + k, nd)
            stat_copy(which, buf, src, src).wait_recv()
        over(nd, one)

    def drain_stats(which, buf):
        over(nd, lambda k: stat_copy(which, buf, me, lax.rem(me + k, nd)).wait_send())

    barrier = pltpu.get_barrier_semaphore()

    def greet(k):
        peer = lax.rem(me + k, nd)
        pl.semaphore_signal(barrier, inc=1, device_id=device(peer // nb, lax.rem(peer, nb)),
                            device_id_type=pl.DeviceIdType.MESH)
    over(nd, greet)

    row_id = lax.broadcasted_iota(jnp.int32, (lat, ch), 0)
    zero_row = jnp.zeros((1, ch), F32)

    land_f = land[...].astype(F32)
    diagonal = lax.broadcasted_iota(jnp.int32, (lat, lat), 0) == lax.broadcasted_iota(
        jnp.int32, (lat, lat), 1)
    spread = jnp.concatenate(
        [jnp.where(diagonal, land_f[i:i + 1, :], 0.0) for i in range(lon)], axis=0)
    mask[...] = jnp.dot(spread.astype(BF16), jnp.ones((lat, ch), BF16), preferred_element_type=F32)

    def at(i):
        return pl.ds(i * lat, lat)

    def shift_up(v, ghost):
        return jnp.concatenate([v[1:], ghost], axis=0)

    def shift_down(v):
        return jnp.concatenate([zero_row, v[:-1]], axis=0)

    def put(s, i, v, lane):
        s[i, :, lane * ch:(lane + 1) * ch] = v.astype(BF16)

    masked = [fields[0, i].astype(F32) * mask[at(i)] for i in range(lon)]
    seen = [target[0, i].astype(F32) * mask[at(i)] for i in range(lon)]
    halves = []
    for h in range(2):
        half = mask[h * cells // 2:(h + 1) * cells // 2]
        halves.append(jnp.broadcast_to(jnp.sum(half, axis=0, keepdims=True), (8, ch)))
    rows1[z] = jnp.concatenate(
        [v[lat - 1:] for v in masked] + [v[lat - 1:] for v in seen] + halves, axis=0).astype(BF16)
    head1[0:lat] = masked[0].astype(BF16)
    head1[lat:2 * lat] = seen[0].astype(BF16)
    tail1[0:lat] = masked[-1].astype(BF16)
    tail1[lat:2 * lat] = seen[-1].astype(BF16)

    pl.semaphore_wait(barrier, nd - 1)
    send_rows(0, rows1)
    cols1 = col_copies(0, head1, tail1, west1, east1)
    for c in cols1:
        c.start()

    for i in range(lon):
        put(s_in, i + 1, shift_down(masked[i]), 0)
        put(s_in, i + 1, masked[i], 1)
    for tap in range(9):
        f, s = tap // 3, tap % 3
        w = w_out[f, s * ch:(s + 1) * ch, :].astype(F32)
        w_back[f, s * ch:(s + 1) * ch, :] = w.T.astype(BF16)

    for c in cols1:
        c.wait_recv()
    recv_rows(0, rows1)

    opposite = nz - 1 - z
    beyond = lax.rem(nz - z, nz)
    before = lax.rem(2 * nz - 2 - z, nz)

    def ghosts(buf, start):
        facing = buf[opposite].astype(F32)
        left = buf[beyond].astype(F32)[start:start + 1]
        right = buf[before].astype(F32)[start + lon - 1:start + lon]
        return [left] + [facing[start + lon - 1 - i:start + lon - i] for i in range(lon)] + [right]

    ghost_in = ghosts(rows1, 0)
    edge_w = west1[0:lat].astype(F32)
    edge_e = east1[0:lat].astype(F32)
    for i, v in ((0, edge_w), (lon + 1, edge_e)):
        put(s_in, i, shift_down(v), 0)
        put(s_in, i, v, 1)
    for i in range(lon + 2):
        v = edge_w if i == 0 else edge_e if i == lon + 1 else (
            fields[0, i - 1].astype(F32) * mask[at(i - 1)])
        put(s_in, i, shift_up(v, ghost_in[i]), 2)

    def window(s, f):
        return s[f:f + lon].reshape(cells, 3 * ch)

    total = jnp.dot(window(s_in, 0), w_in[0], preferred_element_type=F32)
    total += jnp.dot(window(s_in, 1), w_in[1], preferred_element_type=F32)
    total += jnp.dot(window(s_in, 2), w_in[2], preferred_element_type=F32)
    rounded = total.astype(BF16).astype(F32)
    first[...] = rounded
    held = rounded * mask[...]
    stats1[me, 0:1] = jnp.sum(held, axis=0, keepdims=True)
    stats1[me, 1:2] = jnp.sum(held * rounded, axis=0, keepdims=True)
    send_stats(0, stats1)

    count = zero_row
    for k in range(nz):
        packet = rows1[k].astype(F32)
        count = count + packet[16:17] + packet[24:25]
    count = count * float(nb)
    scale = lax.rsqrt(count)

    def scaled(v):
        return (v * scale).astype(BF16).astype(F32)

    for i in range(lon + 2):
        if i == 0:
            v = west1[lat:2 * lat].astype(F32)
        elif i == lon + 1:
            v = east1[lat:2 * lat].astype(F32)
        else:
            v = target[0, i - 1].astype(F32) * mask[at(i - 1)]
        v = scaled(v)
        put(s_dout, i, shift_up(v, zero_row), 0)
        put(s_dout, i, v, 1)
        put(s_dout, i, shift_down(v), 2)
        if 0 < i <= lon and i % 2 == 0:
            pair = jnp.concatenate([earlier, v], axis=0)
            dout_t[:, (i - 2) * lat:i * lat] = pair.T.astype(BF16)
        earlier = v
    ghost_dout = [scaled(v) for v in ghosts(rows1, lon)]
    total = jnp.dot(window(s_dout, 2), w_back[0], preferred_element_type=F32)
    total += jnp.dot(window(s_dout, 1), w_back[1], preferred_element_type=F32)
    total += jnp.dot(window(s_dout, 0), w_back[2], preferred_element_type=F32)
    extra = jnp.zeros((2 * lon, ch), F32)
    for f in range(3):
        piece = jnp.concatenate(ghost_dout[f:f + lon] + [jnp.zeros((lon, ch), F32)], axis=0)
        extra += jnp.dot(piece.astype(BF16), w_back[f, 2 * ch:3 * ch, :], preferred_element_type=F32)
    for i in range(lon):
        dact[at(i)] = total[i * lat:(i + 1) * lat] + jnp.where(
            row_id == lat - 1, extra[i:i + 1], 0.0)

    recv_stats(0, stats1)

    def gathered(buf):
        acc = buf[0]
        for k in range(1, nd):
            acc = acc + buf[k]
        return acc

    acc = gathered(stats1)
    mean = acc[0:1] / count
    var = acc[1:2] / count - mean * mean
    inverse = lax.rsqrt(var + 1e-05)
    gains = gain[...]
    offsets = offset[...]

    sum_off = zero_row
    sum_gain = zero_row
    last = []
    for i in range(lon):
        xhat = (first[at(i)] - mean) * inverse
        act, slope = gelu_parts(gains * xhat + offsets)
        act = (act * mask[at(i)]).astype(BF16)
        d = dact[at(i)] * mask[at(i)] * slope
        dpre[at(i)] = d
        sum_off += jnp.sum(d, axis=0, keepdims=True)
        sum_gain += jnp.sum(d * xhat, axis=0, keepdims=True)
        s_act[i + 1, :, ch:2 * ch] = act
        last.append(act.astype(F32)[lat - 1:])
        if i == 0:
            head2[...] = act
        if i == lon - 1:
            tail2[...] = act
    stats2[me, 0:1] = sum_off
    stats2[me, 1:2] = sum_gain
    send_stats(1, stats2)
    rows2[z] = jnp.concatenate(last + [jnp.zeros((lon, ch), F32)], axis=0).astype(BF16)
    cols2 = col_copies(1, head2, tail2, west2, east2)
    for c in cols2:
        c.start()
    send_rows(1, rows2)

    for i in range(1, lon + 1):
        put(s_act, i, shift_down(s_act[i, :, ch:2 * ch].astype(F32)), 0)
    for c in cols2:
        c.wait_recv()
    recv_rows(1, rows2)
    ghost_act = ghosts(rows2, 0)
    s_act[0, :, ch:2 * ch] = west2[...]
    s_act[lon + 1, :, ch:2 * ch] = east2[...]
    for i in range(lon + 2):
        v = s_act[i, :, ch:2 * ch].astype(F32)
        if i == 0 or i == lon + 1:
            put(s_act, i, shift_down(v), 0)
        put(s_act, i, shift_up(v, ghost_act[i]), 2)

    share = ch // nb
    live = 9 * share
    padded = units * 16 * nz

    def tap_grad(s, d_t, part):
        for f in range(3):
            g = jnp.dot(d_t, window(s, f), preferred_element_type=F32).astype(BF16)
            for t in range(3):
                tap = 3 * f + t
                for k in range(nb):
                    part[k % 2, k // 2, tap * share:(tap + 1) * share, :] = (
                        g[k * share:(k + 1) * share, t * ch:(t + 1) * ch])
        if padded > live:
            for k in range(nb):
                part[k % 2, k // 2, live:padded, :] = jnp.zeros((padded - live, ch), BF16)

    def pair_copy(which, part, pair):
        return copy(part.at[other], pair, pair_sems.at[which, 0], pair_sems.at[which, 1],
                    z, 2 * col + other)

    def cross_copy(which, half, cross, slot, peer, x):
        return copy(half.at[peer], cross.at[slot], cross_sems.at[which, 0, peer],
                    cross_sems.at[which, 1, slot], z, 2 * x + core)

    def ring_copy(which, mine, ring, slot, peer):
        return copy(mine.at[peer], ring.at[slot], ring_sems.at[which, 0, peer],
                    ring_sems.at[which, 1, slot], peer, b)

    def full_copy(which, full, slot, peer):
        return copy(full.at[slot], full.at[slot], full_sems.at[which, 0, peer],
                    full_sems.at[which, 1, slot], peer, b)

    def after_pair(which, part, pair, half, cross):
        pair_copy(which, part, pair).wait_recv()
        for x in range(nx):
            half[x] = (part[core, x].astype(F32) + pair[x].astype(F32)).astype(BF16)

        def one(k):
            x = lax.rem(col + k, nx)
            cross_copy(which, half, cross, col, x, x).start()
        over(nx, one)

    def after_cross(which, half, cross, mine, ring):
        acc = half[col].astype(F32)
        for k in range(1, nx):
            x = lax.rem(col + k, nx)
            cross_copy(which, half, cross, x, x, x).wait_recv()
            acc = acc + cross[x].astype(F32)
        for k in range(nz):
            mine[k] = acc[k * units * 16:(k + 1) * units * 16].astype(BF16)

        def one(k):
            peer = lax.rem(z + k, nz)
            ring_copy(which, mine, ring, z, peer).start()
        over(nz, one)

    def after_ring(which, mine, ring, full):
        acc = mine[z].astype(F32)
        for k in range(1, nz):
            src = lax.rem(z + k, nz)
            ring_copy(which, mine, ring, src, src).wait_recv()
            acc = acc + ring[src].astype(F32)
        full[z] = acc.astype(BF16)

        def one(k):
            full_copy(which, full, z, lax.rem(z + k, nz)).start()
        over(nz, one)

    def after_full(which, full, out):
        def one(k):
            src = lax.rem(z + k, nz)
            full_copy(which, full, src, src).wait_recv()
        over(nz, one)
        out[...] = full[...].reshape(padded, ch)[0:live].astype(F32)

    def drain(which, part, pair, half, cross, mine, ring, full):
        pair_copy(which, part, pair).wait_send()

        def one_x(k):
            x = lax.rem(col + k, nx)
            cross_copy(which, half, cross, col, x, x).wait_send()
        over(nx, one_x)

        def one_z(k):
            peer = lax.rem(z + k, nz)
            ring_copy(which, mine, ring, z, peer).wait_send()
            full_copy(which, full, z, peer).wait_send()
        over(nz, one_z)

    tap_grad(s_act, dout_t[...], part_a)
    pair_copy(0, part_a, pair_a).start()

    recv_stats(1, stats2)
    acc = gathered(stats2)
    off_total = acc[0:1]
    gain_total = acc[1:2]
    offset_gradient[...] = off_total
    gain_gradient[...] = gain_total
    for i in range(0, lon, 2):
        pieces = []
        for j in (i, i + 1):
            xhat = (first[at(j)] - mean) * inverse
            pieces.append(mask[at(j)] * gains * inverse * (
                dpre[at(j)] - (off_total + xhat * gain_total) / count))
        pair = jnp.concatenate(pieces, axis=0)
        dout_t[:, i * lat:(i + 2) * lat] = pair.T.astype(BF16)
    tap_grad(s_in, dout_t[...], part_b)
    pair_copy(1, part_b, pair_b).start()

    after_pair(0, part_a, pair_a, half_a, cross_a)
    after_pair(1, part_b, pair_b, half_b, cross_b)

    total = jnp.dot(window(s_act, 0), w_out[0], preferred_element_type=F32)
    total += jnp.dot(window(s_act, 1), w_out[1], preferred_element_type=F32)
    total += jnp.dot(window(s_act, 2), w_out[2], preferred_element_type=F32)
    output[0] = (total * mask[...]).astype(BF16).reshape(lon, lat, ch)

    after_cross(0, half_a, cross_a, mine_a, ring_a)
    after_cross(1, half_b, cross_b, mine_b, ring_b)
    after_ring(0, mine_a, ring_a, full_a)
    after_ring(1, mine_b, ring_b, full_b)
    after_full(0, full_a, grad_out)
    after_full(1, full_b, grad_in)

    for c in cols1 + cols2:
        c.wait_send()
    drain_rows(0, rows1)
    drain_rows(1, rows2)
    drain_stats(0, stats1)
    drain_stats(1, stats2)
    drain(0, part_a, pair_a, half_a, cross_a, mine_a, ring_a, full_a)
    drain(1, part_b, pair_b, half_b, cross_b, mine_b, ring_b, full_b)


def body(nz, nb, fields, land, conv_in, conv_out, gain, offset, target):
    lon, lat, ch = fields.shape[1:]
    nd = nz * nb
    nx = nb // 2
    share = ch // nb
    units = -(-(9 * share // 16) // nz)
    padded = units * 16 * nz
    vm = pltpu.VMEM
    reduction = [
        vm((2, nx, padded, ch), BF16),
        vm((nx, padded, ch), BF16),
        vm((nx, padded, ch), BF16),
        vm((nx, padded, ch), BF16),
        vm((nz, units * 16, ch), BF16),
        vm((nz, units * 16, ch), BF16),
        vm((nz, units * 16, ch), BF16),
    ]
    dma = pltpu.SemaphoreType.DMA
    scratch = [
        vm((lon * lat, ch), F32),
        vm((lon * lat, ch), F32),
        vm((lon * lat, ch), F32),
        vm((lon * lat, ch), F32),
        vm((lon + 2, lat, 3 * ch), BF16),
        vm((lon + 2, lat, 3 * ch), BF16),
        vm((lon + 2, lat, 3 * ch), BF16),
        vm((3, 3 * ch, ch), BF16),
        vm((ch, lon * lat), BF16),
        vm((nz, 32, ch), BF16),
        vm((2 * lat, ch), BF16), vm((2 * lat, ch), BF16),
        vm((2 * lat, ch), BF16), vm((2 * lat, ch), BF16),
        vm((nz, 16, ch), BF16),
        vm((lat, ch), BF16), vm((lat, ch), BF16),
        vm((lat, ch), BF16), vm((lat, ch), BF16),
        vm((nd, 8, ch), F32),
        vm((nd, 8, ch), F32),
        *reduction,
        *reduction,
        dma((2, 2, nz)),
        dma((2, 2, 2)),
        dma((2, 2, nd)),
        dma((2, 2)),
        dma((2, 2, nx)),
        dma((2, 2, nz)),
        dma((2, 2, nz)),
    ]
    spec = pl.BlockSpec(memory_space=pltpu.VMEM)
    out, grad_in, grad_out, gain_gradient, offset_gradient = pl.pallas_call(
        functools.partial(kernel, nz, nb, lon, lat, ch, units),
        out_shape=(
            jax.ShapeDtypeStruct(fields.shape, BF16),
            jax.ShapeDtypeStruct((9 * share, ch), F32),
            jax.ShapeDtypeStruct((9 * share, ch), F32),
            jax.ShapeDtypeStruct((1, ch), F32),
            jax.ShapeDtypeStruct((1, ch), F32),
        ),
        in_specs=[spec] * 7,
        out_specs=(spec,) * 5,
        scratch_shapes=scratch,
        compiler_params=pltpu.CompilerParams(
            collective_id=0, has_side_effects=True, vmem_limit_bytes=40 * 1024 * 1024
        ),
    )(
        fields, land,
        conv_in.reshape(3, 3 * ch, ch), conv_out.reshape(3, 3 * ch, ch),
        gain.reshape(1, ch), offset.reshape(1, ch), target,
    )

    def taps(g):
        return g.reshape(9, share, ch).transpose(0, 2, 1)

    return (out, taps(grad_in), taps(grad_out),
            gain_gradient.reshape(ch), offset_gradient.reshape(ch))


def solution(mesh):
    in_specs = (
        P(("groups", "batch"), "space", None, None),
        P("space", None),
        P(),
        P(),
        P(),
        P(),
        P(("groups", "batch"), "space", None, None),
    )
    out_specs = (
        P(("groups", "batch"), "space", None, None),
        P("groups", None, "batch"),
        P("groups", None, "batch"),
        P("groups"),
        P("groups"),
    )
    step = functools.partial(body, mesh.shape["space"], mesh.shape["batch"])
    return jax.shard_map(step, mesh=mesh, in_specs=in_specs, out_specs=out_specs, check_vma=False)
```

```python
import functools

import jax
import jax.numpy as jnp
from jax import lax
from jax.experimental import pallas as pl
from jax.experimental.pallas import tpu as pltpu
from jax.sharding import PartitionSpec as P

F32 = jnp.float32
BF16 = jnp.bfloat16


def gelu_parts(value):
    inner = 0.7978845608 * (value + 0.044715 * value * value * value)
    hyper = jnp.tanh(inner)
    act = 0.5 * value * (1.0 + hyper)
    slope = 0.5 * (1.0 + hyper) + 0.5 * value * (1.0 - hyper * hyper) * 0.7978845608 * (
        1.0 + 3.0 * 0.044715 * value * value
    )
    return act, slope


def kernel(
    nz, nb, lon, lat, ch, units,
    fields_h, land_h, w_in_h, w_out_h, gain_h, offset_h, target_h,
    output_h, grad_in_h, grad_out_h, gain_gradient_h, offset_gradient_h,
    output, grad_in, grad_out, gain_gradient, offset_gradient,
    fields, land, w_in, w_out, gain, offset, target,
    mask, first, dact, dpre, s_in, s_act, s_dout, w_back, dout_t,
    rows1, rows2, heads, tails, wests, easts,
    stats1, stats2,
    part_a, pair_a, half_a, cross_a, mine_a, ring_a, full_a,
    part_b, pair_b, half_b, cross_b, mine_b, ring_b, full_b,
    load_sems, store_sems, row_sems, col_sems, stat_sems, pair_sems, cross_sems, ring_sems, full_sems,
):
    nd = nz * nb
    nx = nb // 2
    cells = lon * lat
    z = lax.axis_index("space")
    b = lax.axis_index("batch")
    me = z * nb + b
    core = lax.rem(b, 2)
    col = b // 2
    other = 1 - core

    def device(zz, bb):
        return {"space": zz, "batch": bb}

    def copy(src, dst, send, recv, zz, bb):
        return pltpu.make_async_remote_copy(
            src_ref=src, dst_ref=dst, send_sem=send, recv_sem=recv,
            device_id=device(zz, bb), device_id_type=pl.DeviceIdType.MESH,
        )

    def over(count, fn):
        if count <= 16:
            for k in range(1, count):
                fn(k)
            return

        def step(k, carry):
            fn(k)
            return carry
        lax.fori_loop(1, count, step, 0)

    def row_copy(which, buf, slot, zz):
        return copy(buf.at[slot], buf.at[slot], row_sems.at[which, 0, zz],
                    row_sems.at[which, 1, slot], zz, b)

    def send_rows(which, buf):
        over(nz, lambda k: row_copy(which, buf, z, lax.rem(z + k, nz)).start())

    def recv_rows(which, buf):
        def one(k):
            src = lax.rem(z + k, nz)
            row_copy(which, buf, src, src).wait_recv()
        over(nz, one)

    def drain_rows(which, buf):
        over(nz, lambda k: row_copy(which, buf, z, lax.rem(z + k, nz)).wait_send())

    up = lax.rem(z + 1, nz)
    down = lax.rem(z + nz - 1, nz)

    def col_copies(which):
        return (
            copy(heads.at[which], easts.at[which], col_sems.at[which, 0, 0], col_sems.at[which, 1, 0], down, b),
            copy(tails.at[which], wests.at[which], col_sems.at[which, 0, 1], col_sems.at[which, 1, 1], up, b),
        )

    def stat_copy(which, buf, slot, peer):
        return copy(buf.at[slot], buf.at[slot], stat_sems.at[which, 0, peer],
                    stat_sems.at[which, 1, slot], peer // nb, lax.rem(peer, nb))

    def send_stats(which, buf):
        over(nd, lambda k: stat_copy(which, buf, me, lax.rem(me + k, nd)).start())

    def recv_stats(which, buf):
        def one(k):
            src = lax.rem(me + k, nd)
            stat_copy(which, buf, src, src).wait_recv()
        over(nd, one)

    def drain_stats(which, buf):
        over(nd, lambda k: stat_copy(which, buf, me, lax.rem(me + k, nd)).wait_send())

    loads = [
        pltpu.make_async_copy(src, dst, load_sems.at[k])
        for k, (src, dst) in enumerate((
            (land_h, land), (fields_h, fields), (target_h, target), (w_in_h, w_in),
            (w_out_h, w_out), (gain_h, gain), (offset_h, offset)))
    ]
    for load in loads:
        load.start()
    stores = [
        pltpu.make_async_copy(src, dst, store_sems.at[k])
        for k, (src, dst) in enumerate((
            (output, output_h), (grad_in, grad_in_h), (grad_out, grad_out_h),
            (gain_gradient, gain_gradient_h), (offset_gradient, offset_gradient_h)))
    ]

    barrier = pltpu.get_barrier_semaphore()

    def greet(k):
        peer = lax.rem(me + k, nd)
        pl.semaphore_signal(barrier, inc=1, device_id=device(peer // nb, lax.rem(peer, nb)),
                            device_id_type=pl.DeviceIdType.MESH)
    over(nd, greet)

    row_id = lax.broadcasted_iota(jnp.int32, (lat, ch), 0)
    zero_row = jnp.zeros((1, ch), F32)

    loads[0].wait()
    land_f = land[...].astype(F32)
    diagonal = lax.broadcasted_iota(jnp.int32, (lat, lat), 0) == lax.broadcasted_iota(
        jnp.int32, (lat, lat), 1)
    spread = jnp.concatenate(
        [jnp.where(diagonal, land_f[i:i + 1, :], 0.0) for i in range(lon)], axis=0)
    mask[...] = jnp.dot(spread.astype(BF16), jnp.ones((lat, ch), BF16), preferred_element_type=F32)

    def at(i):
        return pl.ds(i * lat, lat)

    def shift_up(v, ghost):
        return jnp.concatenate([v[1:], ghost], axis=0)

    def shift_down(v):
        return jnp.concatenate([zero_row, v[:-1]], axis=0)

    def put(s, i, v, lane):
        s[i, :, lane * ch:(lane + 1) * ch] = v.astype(BF16)

    loads[1].wait()
    loads[2].wait()
    masked = [fields[0, i].astype(F32) * mask[at(i)] for i in range(lon)]
    seen = [target[0, i].astype(F32) * mask[at(i)] for i in range(lon)]
    halves = []
    for h in range(2):
        half = mask[h * cells // 2:(h + 1) * cells // 2]
        halves.append(jnp.broadcast_to(jnp.sum(half, axis=0, keepdims=True), (8, ch)))
    rows1[z] = jnp.concatenate(
        [v[lat - 1:] for v in masked] + [v[lat - 1:] for v in seen] + halves, axis=0).astype(BF16)
    for k, v in enumerate((masked, seen)):
        heads[k] = v[0].astype(BF16)
        tails[k] = v[-1].astype(BF16)

    cols1 = col_copies(0)
    cols_t = col_copies(1)
    pl.semaphore_wait(barrier, nd - 1)
    for c in cols1:
        c.start()
    send_rows(0, rows1)
    for c in cols_t:
        c.start()

    for i in range(lon):
        put(s_in, i + 1, shift_down(masked[i]), 0)
        put(s_in, i + 1, masked[i], 1)
        put(s_in, i + 1, shift_up(masked[i], zero_row), 2)
    for i in (0, lon + 1):
        s_in[i] = jnp.zeros((lat, 3 * ch), BF16)

    def window(s, f):
        return s[f:f + lon].reshape(cells, 3 * ch)

    def conv(s, w, order=(0, 1, 2)):
        acc = jnp.dot(window(s, order[0]), w[0], preferred_element_type=F32)
        acc += jnp.dot(window(s, order[1]), w[1], preferred_element_type=F32)
        return acc + jnp.dot(window(s, order[2]), w[2], preferred_element_type=F32)

    def fold_part(rows, w):
        acc = jnp.zeros((2 * lon, ch), F32)
        for f in range(3):
            piece = jnp.concatenate(rows[f:f + lon] + [jnp.zeros((lon, ch), F32)], axis=0)
            acc += jnp.dot(piece.astype(BF16), w[f, 2 * ch:3 * ch, :], preferred_element_type=F32)
        return acc

    def north(v, row):
        return v + jnp.where(row_id == lat - 1, row, 0.0)

    loads[3].wait()
    first[...] = conv(s_in, w_in)
    for load in loads[4:]:
        load.wait()

    for c in cols1:
        c.wait_recv()
    recv_rows(0, rows1)

    opposite = nz - 1 - z
    beyond = lax.rem(nz - z, nz)
    before = lax.rem(2 * nz - 2 - z, nz)

    def ghosts(buf, start):
        facing = buf[opposite].astype(F32)
        left = buf[beyond].astype(F32)[start:start + 1]
        right = buf[before].astype(F32)[start + lon - 1:start + lon]
        return [left] + [facing[start + lon - 1 - i:start + lon - i] for i in range(lon)] + [right]

    ghost_in = ghosts(rows1, 0)
    for i, v in ((0, wests[0].astype(F32)), (lon + 1, easts[0].astype(F32))):
        put(s_in, i, shift_down(v), 0)
        put(s_in, i, v, 1)
        put(s_in, i, shift_up(v, ghost_in[i]), 2)
    from_west = jnp.dot(s_in[0], w_in[0], preferred_element_type=F32)
    from_east = jnp.dot(s_in[lon + 1], w_in[2], preferred_element_type=F32)
    extra = fold_part([zero_row] + ghost_in[1:lon + 1] + [zero_row], w_in)
    sum_1 = jnp.zeros((lat, ch), F32)
    sum_2 = jnp.zeros((lat, ch), F32)
    for i in range(lon):
        v = north(first[at(i)], extra[i:i + 1])
        if i == 0:
            v = v + from_west
        if i == lon - 1:
            v = v + from_east
        v = v.astype(BF16).astype(F32)
        first[at(i)] = v
        held = v * mask[at(i)]
        sum_1 += held
        sum_2 += held * v
    stats1[me, 0:1] = jnp.sum(sum_1, axis=0, keepdims=True)
    stats1[me, 1:2] = jnp.sum(sum_2, axis=0, keepdims=True)
    send_stats(0, stats1)

    for tap in range(9):
        f, t = tap // 3, tap % 3
        w = w_out[f, t * ch:(t + 1) * ch, :].astype(F32)
        w_back[f, t * ch:(t + 1) * ch, :] = w.T.astype(BF16)
    count = zero_row
    for k in range(nz):
        packet = rows1[k].astype(F32)
        count = count + packet[16:17] + packet[24:25]
    count = count * float(nb)
    scale = lax.rsqrt(count)

    def scaled(v):
        return (v * scale).astype(BF16).astype(F32)

    for c in cols_t:
        c.wait_recv()
    for i in range(lon + 2):
        if i == 0:
            v = wests[1].astype(F32)
        elif i == lon + 1:
            v = easts[1].astype(F32)
        else:
            v = target[0, i - 1].astype(F32) * mask[at(i - 1)]
        v = scaled(v)
        put(s_dout, i, shift_up(v, zero_row), 0)
        put(s_dout, i, v, 1)
        put(s_dout, i, shift_down(v), 2)
        if 0 < i <= lon and i % 2 == 0:
            pair = jnp.concatenate([earlier, v], axis=0)
            dout_t[:, (i - 2) * lat:i * lat] = pair.T.astype(BF16)
        earlier = v
    ghost_dout = [scaled(v) for v in ghosts(rows1, lon)]
    total = conv(s_dout, w_back, (2, 1, 0))
    extra = fold_part(ghost_dout, w_back)
    for i in range(lon):
        dact[at(i)] = north(total[i * lat:(i + 1) * lat], extra[i:i + 1])
    for i in range(lon):
        v = s_in[i + 1, :, ch:2 * ch].astype(F32)
        put(s_in, i + 1, shift_up(v, ghost_in[i + 1]), 2)

    recv_stats(0, stats1)

    def gathered(buf):
        acc = buf[0]
        for k in range(1, nd):
            acc = acc + buf[k]
        return acc

    acc = gathered(stats1)
    mean = acc[0:1] / count
    var = acc[1:2] / count - mean * mean
    inverse = lax.rsqrt(var + 1e-05)
    gains = gain[...]
    offsets = offset[...]

    sum_off = zero_row
    sum_gain = zero_row
    last = []
    for i in range(lon):
        xhat = (first[at(i)] - mean) * inverse
        act, slope = gelu_parts(gains * xhat + offsets)
        act = (act * mask[at(i)]).astype(BF16)
        d = dact[at(i)] * mask[at(i)] * slope
        dpre[at(i)] = d
        sum_off += jnp.sum(d, axis=0, keepdims=True)
        sum_gain += jnp.sum(d * xhat, axis=0, keepdims=True)
        s_act[i + 1, :, ch:2 * ch] = act
        last.append(act.astype(F32)[lat - 1:])
        if i == 0:
            heads[2] = act
        if i == lon - 1:
            tails[2] = act
    stats2[me, 0:1] = sum_off
    stats2[me, 1:2] = sum_gain
    send_stats(1, stats2)
    rows2[z] = jnp.concatenate(last + [jnp.zeros((lon, ch), F32)], axis=0).astype(BF16)
    cols2 = col_copies(2)
    for c in cols2:
        c.start()
    send_rows(1, rows2)

    for i in range(1, lon + 1):
        put(s_act, i, shift_down(s_act[i, :, ch:2 * ch].astype(F32)), 0)
    for c in cols2:
        c.wait_recv()
    recv_rows(1, rows2)
    ghost_act = ghosts(rows2, 0)
    s_act[0, :, ch:2 * ch] = wests[2]
    s_act[lon + 1, :, ch:2 * ch] = easts[2]
    for i in range(lon + 2):
        v = s_act[i, :, ch:2 * ch].astype(F32)
        if i == 0 or i == lon + 1:
            put(s_act, i, shift_down(v), 0)
        put(s_act, i, shift_up(v, ghost_act[i]), 2)

    share = ch // nb
    live = 9 * share
    padded = units * 16 * nz

    def rows_of(f):
        return pl.ds(3 * f * share, 3 * share)

    def tap_grad(which, s, d_t, part, pair):
        for f in range(3):
            g = jnp.dot(d_t, window(s, f), preferred_element_type=F32).astype(BF16)
            for t in range(3):
                tap = 3 * f + t
                for k in range(nb):
                    part[k % 2, k // 2, tap * share:(tap + 1) * share, :] = (
                        g[k * share:(k + 1) * share, t * ch:(t + 1) * ch])
            pair_copy(which, f, part, pair).start()

    def pair_copy(which, f, part, pair):
        return copy(part.at[other, :, rows_of(f)], pair.at[:, rows_of(f)],
                    pair_sems.at[which, 0, f], pair_sems.at[which, 1, f], z, 2 * col + other)

    def cross_copy(which, f, half, cross, slot, peer, x):
        return copy(half.at[peer, rows_of(f)], cross.at[slot, rows_of(f)],
                    cross_sems.at[which, 0, f, peer], cross_sems.at[which, 1, f, slot],
                    z, 2 * x + core)

    def ring_copy(which, mine, ring, slot, peer):
        return copy(mine.at[peer], ring.at[slot], ring_sems.at[which, 0, peer],
                    ring_sems.at[which, 1, slot], peer, b)

    def full_copy(which, full, slot, peer):
        return copy(full.at[slot], full.at[slot], full_sems.at[which, 0, peer],
                    full_sems.at[which, 1, slot], peer, b)

    def after_pair(which, part, pair, half, cross):
        for f in range(3):
            pair_copy(which, f, part, pair).wait_recv()
            for x in range(nx):
                half[x, rows_of(f)] = (
                    part[core, x, rows_of(f)].astype(F32) + pair[x, rows_of(f)].astype(F32)
                ).astype(BF16)

            def one(k):
                x = lax.rem(col + k, nx)
                cross_copy(which, f, half, cross, col, x, x).start()
            over(nx, one)

    def after_cross(which, half, cross, mine, ring):
        acc = half[col].astype(F32)
        for k in range(1, nx):
            x = lax.rem(col + k, nx)
            for f in range(3):
                cross_copy(which, f, half, cross, x, x, x).wait_recv()
            acc = acc + cross[x].astype(F32)
        if padded > live:
            acc = jnp.concatenate([acc, jnp.zeros((padded - live, ch), F32)], axis=0)
        for k in range(nz):
            mine[k] = acc[k * units * 16:(k + 1) * units * 16].astype(BF16)

        def one(k):
            peer = lax.rem(z + k, nz)
            ring_copy(which, mine, ring, z, peer).start()
        over(nz, one)

    def after_ring(which, mine, ring, full):
        acc = mine[z].astype(F32)
        for k in range(1, nz):
            src = lax.rem(z + k, nz)
            ring_copy(which, mine, ring, src, src).wait_recv()
            acc = acc + ring[src].astype(F32)
        full[z] = acc.astype(BF16)

        def one(k):
            full_copy(which, full, z, lax.rem(z + k, nz)).start()
        over(nz, one)

    def after_full(which, full, out):
        def one(k):
            src = lax.rem(z + k, nz)
            full_copy(which, full, src, src).wait_recv()
        over(nz, one)
        out[...] = full[...].reshape(padded, ch)[0:live].astype(F32)

    def drain(which, part, pair, half, cross, mine, ring, full):
        for f in range(3):
            pair_copy(which, f, part, pair).wait_send()

            def one_x(k):
                x = lax.rem(col + k, nx)
                cross_copy(which, f, half, cross, col, x, x).wait_send()
            over(nx, one_x)

        def one_z(k):
            peer = lax.rem(z + k, nz)
            ring_copy(which, mine, ring, z, peer).wait_send()
            full_copy(which, full, z, peer).wait_send()
        over(nz, one_z)

    tap_grad(0, s_act, dout_t[...], part_a, pair_a)

    recv_stats(1, stats2)
    acc = gathered(stats2)
    off_total = acc[0:1]
    gain_total = acc[1:2]
    offset_gradient[...] = off_total
    gain_gradient[...] = gain_total
    stores[3].start()
    stores[4].start()
    for i in range(0, lon, 2):
        pieces = []
        for j in (i, i + 1):
            xhat = (first[at(j)] - mean) * inverse
            pieces.append(mask[at(j)] * gains * inverse * (
                dpre[at(j)] - (off_total + xhat * gain_total) / count))
        pair = jnp.concatenate(pieces, axis=0)
        dout_t[:, i * lat:(i + 2) * lat] = pair.T.astype(BF16)
    after_pair(0, part_a, pair_a, half_a, cross_a)
    tap_grad(1, s_in, dout_t[...], part_b, pair_b)
    after_cross(0, half_a, cross_a, mine_a, ring_a)
    after_pair(1, part_b, pair_b, half_b, cross_b)

    total = conv(s_act, w_out)
    output[0] = (total * mask[...]).astype(BF16).reshape(lon, lat, ch)
    stores[0].start()

    after_ring(0, mine_a, ring_a, full_a)
    after_cross(1, half_b, cross_b, mine_b, ring_b)
    after_ring(1, mine_b, ring_b, full_b)
    after_full(0, full_a, grad_out)
    stores[2].start()
    after_full(1, full_b, grad_in)
    stores[1].start()

    for c in cols1 + cols_t + cols2:
        c.wait_send()
    drain_rows(0, rows1)
    drain_rows(1, rows2)
    drain_stats(0, stats1)
    drain_stats(1, stats2)
    drain(0, part_a, pair_a, half_a, cross_a, mine_a, ring_a, full_a)
    drain(1, part_b, pair_b, half_b, cross_b, mine_b, ring_b, full_b)
    for store in stores:
        store.wait()


def writer(*refs):
    sems = refs[-1]
    copies = [pltpu.make_async_copy(refs[k], refs[5 + k], sems.at[k]) for k in range(5)]
    for c in copies:
        c.start()
    for c in copies:
        c.wait()


def body(nz, nb, fields, land, conv_in, conv_out, gain, offset, target):
    lon, lat, ch = fields.shape[1:]
    nd = nz * nb
    nx = nb // 2
    share = ch // nb
    units = -(-(9 * share // 16) // nz)
    padded = units * 16 * nz
    vm = pltpu.VMEM
    reduction = [
        vm((2, nx, 9 * share, ch), BF16),
        vm((nx, 9 * share, ch), BF16),
        vm((nx, 9 * share, ch), BF16),
        vm((nx, 9 * share, ch), BF16),
        vm((nz, units * 16, ch), BF16),
        vm((nz, units * 16, ch), BF16),
        vm((nz, units * 16, ch), BF16),
    ]
    dma = pltpu.SemaphoreType.DMA
    scratch = [
        vm(fields.shape, BF16),
        vm((9 * share, ch), F32),
        vm((9 * share, ch), F32),
        vm((1, ch), F32),
        vm((1, ch), F32),
        vm(fields.shape, BF16),
        vm(land.shape, jnp.int32),
        vm((3, 3 * ch, ch), BF16),
        vm((3, 3 * ch, ch), BF16),
        vm((1, ch), F32),
        vm((1, ch), F32),
        vm(target.shape, BF16),
        vm((lon * lat, ch), F32),
        vm((lon * lat, ch), F32),
        vm((lon * lat, ch), F32),
        vm((lon * lat, ch), F32),
        vm((lon + 2, lat, 3 * ch), BF16),
        vm((lon + 2, lat, 3 * ch), BF16),
        vm((lon + 2, lat, 3 * ch), BF16),
        vm((3, 3 * ch, ch), BF16),
        vm((ch, lon * lat), BF16),
        vm((nz, 32, ch), BF16),
        vm((nz, 16, ch), BF16),
        vm((3, lat, ch), BF16), vm((3, lat, ch), BF16),
        vm((3, lat, ch), BF16), vm((3, lat, ch), BF16),
        vm((nd, 2, ch), F32),
        vm((nd, 2, ch), F32),
        *reduction,
        *reduction,
        dma((7,)),
        dma((5,)),
        dma((2, 2, nz)),
        dma((3, 2, 2)),
        dma((2, 2, nd)),
        dma((2, 2, 3)),
        dma((2, 2, 3, nx)),
        dma((2, 2, nz)),
        dma((2, 2, nz)),
    ]
    anywhere = pl.BlockSpec(memory_space=pl.ANY)
    limit = 62 * 1024 * 1024
    results = pl.pallas_call(
        functools.partial(kernel, nz, nb, lon, lat, ch, units),
        out_shape=(
            jax.ShapeDtypeStruct(fields.shape, BF16),
            jax.ShapeDtypeStruct((9 * share, ch), F32),
            jax.ShapeDtypeStruct((9 * share, ch), F32),
            jax.ShapeDtypeStruct((1, ch), F32),
            jax.ShapeDtypeStruct((1, ch), F32),
        ),
        in_specs=[anywhere] * 7,
        out_specs=(anywhere,) * 5,
        scratch_shapes=scratch,
        compiler_params=pltpu.CompilerParams(
            collective_id=0, has_side_effects=True, vmem_limit_bytes=limit
        ),
    )(
        fields, land,
        conv_in.reshape(3, 3 * ch, ch), conv_out.reshape(3, 3 * ch, ch),
        gain.reshape(1, ch), offset.reshape(1, ch), target,
    )

    out, grad_in, grad_out, gain_gradient, offset_gradient = pl.pallas_call(
        writer,
        out_shape=tuple(jax.ShapeDtypeStruct(r.shape, r.dtype) for r in results),
        in_specs=[anywhere] * 5,
        out_specs=(anywhere,) * 5,
        scratch_shapes=[dma((5,))],
        compiler_params=pltpu.CompilerParams(vmem_limit_bytes=limit),
    )(*results)

    def taps(g):
        return g.reshape(9, share, ch).transpose(0, 2, 1)

    return (out, taps(grad_in), taps(grad_out),
            gain_gradient.reshape(ch), offset_gradient.reshape(ch))


def solution(mesh):
    in_specs = (
        P(("groups", "batch"), "space", None, None),
        P("space", None),
        P(),
        P(),
        P(),
        P(),
        P(("groups", "batch"), "space", None, None),
    )
    out_specs = (
        P(("groups", "batch"), "space", None, None),
        P("groups", None, "batch"),
        P("groups", None, "batch"),
        P("groups"),
        P("groups"),
    )
    step = functools.partial(body, mesh.shape["space"], mesh.shape["batch"])
    return jax.shard_map(step, mesh=mesh, in_specs=in_specs, out_specs=out_specs, check_vma=False)
```

```python
import functools

import jax
import jax.numpy as jnp
from jax import lax
from jax.experimental import pallas as pl
from jax.experimental.pallas import tpu as pltpu
from jax.sharding import PartitionSpec as P

F32 = jnp.float32
BF16 = jnp.bfloat16


def gelu_parts(value):
    inner = 0.7978845608 * (value + 0.044715 * value * value * value)
    hyper = jnp.tanh(inner)
    act = 0.5 * value * (1.0 + hyper)
    slope = 0.5 * (1.0 + hyper) + 0.5 * value * (1.0 - hyper * hyper) * 0.7978845608 * (
        1.0 + 3.0 * 0.044715 * value * value
    )
    return act, slope


def kernel(
    nz, nb, lon, lat, ch, units,
    fields_h, land_h, w_in_h, w_out_h, gain_h, offset_h, target_h,
    output_h, grad_in_h, grad_out_h, gain_gradient_h, offset_gradient_h,
    output, grad_in, grad_out, gain_gradient, offset_gradient,
    fields, land, w_in, w_out, gain, offset, target,
    mask, first, dact, dpre, s_in, s_act, s_dout, w_back, dout_t,
    rows1, rows2, heads, tails, wests, easts,
    by_batch, by_space,
    part_a, pair_a, half_a, cross_a, mine_a, ring_a, full_a,
    part_b, pair_b, half_b, cross_b, mine_b, ring_b, full_b,
    load_sems, store_sems, row_sems, col_sems, batch_sems, space_sems, pair_sems, cross_sems, ring_sems, full_sems,
):
    nx = nb // 2
    cells = lon * lat
    z = lax.axis_index("space")
    b = lax.axis_index("batch")
    core = lax.rem(b, 2)
    col = b // 2
    other = 1 - core

    def device(zz, bb):
        return {"space": zz, "batch": bb}

    def copy(src, dst, send, recv, zz, bb):
        return pltpu.make_async_remote_copy(
            src_ref=src, dst_ref=dst, send_sem=send, recv_sem=recv,
            device_id=device(zz, bb), device_id_type=pl.DeviceIdType.MESH,
        )

    def over(count, fn):
        if count <= 16:
            for k in range(1, count):
                fn(k)
            return

        def step(k, carry):
            fn(k)
            return carry
        lax.fori_loop(1, count, step, 0)

    def row_copy(which, buf, slot, zz):
        return copy(buf.at[slot], buf.at[slot], row_sems.at[which, 0, zz],
                    row_sems.at[which, 1, slot], zz, b)

    def send_rows(which, buf):
        over(nz, lambda k: row_copy(which, buf, z, lax.rem(z + k, nz)).start())

    def recv_rows(which, buf):
        def one(k):
            src = lax.rem(z + k, nz)
            row_copy(which, buf, src, src).wait_recv()
        over(nz, one)

    def drain_rows(which, buf):
        over(nz, lambda k: row_copy(which, buf, z, lax.rem(z + k, nz)).wait_send())

    up = lax.rem(z + 1, nz)
    down = lax.rem(z + nz - 1, nz)

    def col_copies(which):
        return (
            copy(heads.at[which], easts.at[which], col_sems.at[which, 0, 0], col_sems.at[which, 1, 0], down, b),
            copy(tails.at[which], wests.at[which], col_sems.at[which, 0, 1], col_sems.at[which, 1, 1], up, b),
        )

    def batch_copy(which, slot, peer):
        return copy(by_batch.at[which, slot], by_batch.at[which, slot],
                    batch_sems.at[which, 0, peer], batch_sems.at[which, 1, slot], z, peer)

    def space_copy(which, slot, peer):
        return copy(by_space.at[which, slot], by_space.at[which, slot],
                    space_sems.at[which, 0, peer], space_sems.at[which, 1, slot], peer, b)

    def send_stats(which):
        over(nb, lambda k: batch_copy(which, b, lax.rem(b + k, nb)).start())

    def recv_stats(which):
        def one_b(k):
            src = lax.rem(b + k, nb)
            batch_copy(which, src, src).wait_recv()
        over(nb, one_b)
        acc = by_batch[which, 0]
        for k in range(1, nb):
            acc = acc + by_batch[which, k]
        by_space[which, z] = acc
        over(nz, lambda k: space_copy(which, z, lax.rem(z + k, nz)).start())

        def one_z(k):
            src = lax.rem(z + k, nz)
            space_copy(which, src, src).wait_recv()
        over(nz, one_z)
        acc = by_space[which, 0]
        for k in range(1, nz):
            acc = acc + by_space[which, k]
        return acc

    def drain_stats(which):
        over(nb, lambda k: batch_copy(which, b, lax.rem(b + k, nb)).wait_send())
        over(nz, lambda k: space_copy(which, z, lax.rem(z + k, nz)).wait_send())

    loads = [
        pltpu.make_async_copy(src, dst, load_sems.at[k])
        for k, (src, dst) in enumerate((
            (land_h, land), (fields_h, fields), (target_h, target), (w_in_h, w_in),
            (w_out_h, w_out), (gain_h, gain), (offset_h, offset)))
    ]
    for load in loads:
        load.start()
    stores = [
        pltpu.make_async_copy(src, dst, store_sems.at[k])
        for k, (src, dst) in enumerate((
            (output, output_h), (grad_in, grad_in_h), (grad_out, grad_out_h),
            (gain_gradient, gain_gradient_h), (offset_gradient, offset_gradient_h)))
    ]

    barrier = pltpu.get_barrier_semaphore()

    def greet(zz, bb):
        pl.semaphore_signal(barrier, inc=1, device_id=device(zz, bb),
                            device_id_type=pl.DeviceIdType.MESH)
    over(nz, lambda k: greet(lax.rem(z + k, nz), b))
    over(nb, lambda k: greet(z, lax.rem(b + k, nb)))

    row_id = lax.broadcasted_iota(jnp.int32, (lat, ch), 0)
    zero_row = jnp.zeros((1, ch), F32)

    loads[0].wait()
    land_f = land[...].astype(F32)
    diagonal = lax.broadcasted_iota(jnp.int32, (lat, lat), 0) == lax.broadcasted_iota(
        jnp.int32, (lat, lat), 1)
    spread = jnp.concatenate(
        [jnp.where(diagonal, land_f[i:i + 1, :], 0.0) for i in range(lon)], axis=0)
    mask[...] = jnp.dot(spread.astype(BF16), jnp.ones((lat, ch), BF16), preferred_element_type=F32)

    def at(i):
        return pl.ds(i * lat, lat)

    def shift_up(v, ghost):
        return jnp.concatenate([v[1:], ghost], axis=0)

    def shift_down(v):
        return jnp.concatenate([zero_row, v[:-1]], axis=0)

    def put(s, i, v, lane):
        s[i, :, lane * ch:(lane + 1) * ch] = v.astype(BF16)

    loads[1].wait()
    loads[2].wait()
    masked = [fields[0, i].astype(F32) * mask[at(i)] for i in range(lon)]
    seen = [target[0, i].astype(F32) * mask[at(i)] for i in range(lon)]
    halves = []
    for h in range(2):
        half = mask[h * cells // 2:(h + 1) * cells // 2]
        halves.append(jnp.broadcast_to(jnp.sum(half, axis=0, keepdims=True), (8, ch)))
    rows1[z] = jnp.concatenate(
        [v[lat - 1:] for v in masked] + [v[lat - 1:] for v in seen] + halves, axis=0).astype(BF16)
    for k, v in enumerate((masked, seen)):
        heads[k] = v[0].astype(BF16)
        tails[k] = v[-1].astype(BF16)

    cols1 = col_copies(0)
    cols_t = col_copies(1)
    pl.semaphore_wait(barrier, nz + nb - 2)
    for c in cols1:
        c.start()
    send_rows(0, rows1)
    for c in cols_t:
        c.start()

    for i in range(lon):
        put(s_in, i + 1, shift_down(masked[i]), 0)
        put(s_in, i + 1, masked[i], 1)
        put(s_in, i + 1, shift_up(masked[i], zero_row), 2)
    for i in (0, lon + 1):
        s_in[i] = jnp.zeros((lat, 3 * ch), BF16)

    def window(s, f):
        return s[f:f + lon].reshape(cells, 3 * ch)

    def conv(s, w, order=(0, 1, 2)):
        acc = jnp.dot(window(s, order[0]), w[0], preferred_element_type=F32)
        acc += jnp.dot(window(s, order[1]), w[1], preferred_element_type=F32)
        return acc + jnp.dot(window(s, order[2]), w[2], preferred_element_type=F32)

    def fold_part(rows, w):
        acc = jnp.zeros((2 * lon, ch), F32)
        for f in range(3):
            piece = jnp.concatenate(rows[f:f + lon] + [jnp.zeros((lon, ch), F32)], axis=0)
            acc += jnp.dot(piece.astype(BF16), w[f, 2 * ch:3 * ch, :], preferred_element_type=F32)
        return acc

    def north(v, row):
        return v + jnp.where(row_id == lat - 1, row, 0.0)

    loads[3].wait()
    first[...] = conv(s_in, w_in)
    for load in loads[4:]:
        load.wait()

    for c in cols1:
        c.wait_recv()
    recv_rows(0, rows1)

    opposite = nz - 1 - z
    beyond = lax.rem(nz - z, nz)
    before = lax.rem(2 * nz - 2 - z, nz)

    def ghosts(buf, start):
        facing = buf[opposite].astype(F32)
        left = buf[beyond].astype(F32)[start:start + 1]
        right = buf[before].astype(F32)[start + lon - 1:start + lon]
        return [left] + [facing[start + lon - 1 - i:start + lon - i] for i in range(lon)] + [right]

    ghost_in = ghosts(rows1, 0)
    for i, v in ((0, wests[0].astype(F32)), (lon + 1, easts[0].astype(F32))):
        put(s_in, i, shift_down(v), 0)
        put(s_in, i, v, 1)
        put(s_in, i, shift_up(v, ghost_in[i]), 2)
    from_west = jnp.dot(s_in[0], w_in[0], preferred_element_type=F32)
    from_east = jnp.dot(s_in[lon + 1], w_in[2], preferred_element_type=F32)
    extra = fold_part([zero_row] + ghost_in[1:lon + 1] + [zero_row], w_in)
    sum_1 = jnp.zeros((lat, ch), F32)
    sum_2 = jnp.zeros((lat, ch), F32)
    for i in range(lon):
        v = north(first[at(i)], extra[i:i + 1])
        if i == 0:
            v = v + from_west
        if i == lon - 1:
            v = v + from_east
        v = v.astype(BF16).astype(F32)
        first[at(i)] = v
        held = v * mask[at(i)]
        sum_1 += held
        sum_2 += held * v
    by_batch[0, b, 0:1] = jnp.sum(sum_1, axis=0, keepdims=True)
    by_batch[0, b, 1:2] = jnp.sum(sum_2, axis=0, keepdims=True)
    send_stats(0)

    for tap in range(9):
        f, t = tap // 3, tap % 3
        w = w_out[f, t * ch:(t + 1) * ch, :].astype(F32)
        w_back[f, t * ch:(t + 1) * ch, :] = w.T.astype(BF16)
    count = zero_row
    for k in range(nz):
        packet = rows1[k].astype(F32)
        count = count + packet[16:17] + packet[24:25]
    count = count * float(nb)
    scale = lax.rsqrt(count)

    def scaled(v):
        return (v * scale).astype(BF16).astype(F32)

    for c in cols_t:
        c.wait_recv()
    for i in range(lon + 2):
        if i == 0:
            v = wests[1].astype(F32)
        elif i == lon + 1:
            v = easts[1].astype(F32)
        else:
            v = target[0, i - 1].astype(F32) * mask[at(i - 1)]
        v = scaled(v)
        put(s_dout, i, shift_up(v, zero_row), 0)
        put(s_dout, i, v, 1)
        put(s_dout, i, shift_down(v), 2)
        if 0 < i <= lon and i % 2 == 0:
            pair = jnp.concatenate([earlier, v], axis=0)
            dout_t[:, (i - 2) * lat:i * lat] = pair.T.astype(BF16)
        earlier = v
    ghost_dout = [scaled(v) for v in ghosts(rows1, lon)]
    total = conv(s_dout, w_back, (2, 1, 0))
    extra = fold_part(ghost_dout, w_back)
    for i in range(lon):
        dact[at(i)] = north(total[i * lat:(i + 1) * lat], extra[i:i + 1])
    for i in range(lon):
        v = s_in[i + 1, :, ch:2 * ch].astype(F32)
        put(s_in, i + 1, shift_up(v, ghost_in[i + 1]), 2)

    acc = recv_stats(0)
    mean = acc[0:1] / count
    var = acc[1:2] / count - mean * mean
    inverse = lax.rsqrt(var + 1e-05)
    gains = gain[...]
    offsets = offset[...]

    sum_off = zero_row
    sum_gain = zero_row
    last = []
    for i in range(lon):
        xhat = (first[at(i)] - mean) * inverse
        act, slope = gelu_parts(gains * xhat + offsets)
        act = (act * mask[at(i)]).astype(BF16)
        d = dact[at(i)] * mask[at(i)] * slope
        dpre[at(i)] = d
        sum_off += jnp.sum(d, axis=0, keepdims=True)
        sum_gain += jnp.sum(d * xhat, axis=0, keepdims=True)
        s_act[i + 1, :, ch:2 * ch] = act
        last.append(act.astype(F32)[lat - 1:])
        if i == 0:
            heads[2] = act
        if i == lon - 1:
            tails[2] = act
    by_batch[1, b, 0:1] = sum_off
    by_batch[1, b, 1:2] = sum_gain
    send_stats(1)
    rows2[z] = jnp.concatenate(last + [jnp.zeros((lon, ch), F32)], axis=0).astype(BF16)
    cols2 = col_copies(2)
    for c in cols2:
        c.start()
    send_rows(1, rows2)

    for i in range(1, lon + 1):
        put(s_act, i, shift_down(s_act[i, :, ch:2 * ch].astype(F32)), 0)
    for c in cols2:
        c.wait_recv()
    recv_rows(1, rows2)
    ghost_act = ghosts(rows2, 0)
    s_act[0, :, ch:2 * ch] = wests[2]
    s_act[lon + 1, :, ch:2 * ch] = easts[2]
    for i in range(lon + 2):
        v = s_act[i, :, ch:2 * ch].astype(F32)
        if i == 0 or i == lon + 1:
            put(s_act, i, shift_down(v), 0)
        put(s_act, i, shift_up(v, ghost_act[i]), 2)

    share = ch // nb
    live = 9 * share
    padded = units * 16 * nz

    def rows_of(f):
        return pl.ds(3 * f * share, 3 * share)

    def tap_grad(which, s, d_t, part, pair):
        for f in range(3):
            g = jnp.dot(d_t, window(s, f), preferred_element_type=F32).astype(BF16)
            for t in range(3):
                tap = 3 * f + t
                for k in range(nb):
                    part[k % 2, k // 2, tap * share:(tap + 1) * share, :] = (
                        g[k * share:(k + 1) * share, t * ch:(t + 1) * ch])
            pair_copy(which, f, part, pair).start()

    def pair_copy(which, f, part, pair):
        return copy(part.at[other, :, rows_of(f)], pair.at[:, rows_of(f)],
                    pair_sems.at[which, 0, f], pair_sems.at[which, 1, f], z, 2 * col + other)

    def cross_copy(which, f, half, cross, slot, peer, x):
        return copy(half.at[peer, rows_of(f)], cross.at[slot, rows_of(f)],
                    cross_sems.at[which, 0, f, peer], cross_sems.at[which, 1, f, slot],
                    z, 2 * x + core)

    def ring_copy(which, mine, ring, slot, peer):
        return copy(mine.at[peer], ring.at[slot], ring_sems.at[which, 0, peer],
                    ring_sems.at[which, 1, slot], peer, b)

    def full_copy(which, full, slot, peer):
        return copy(full.at[slot], full.at[slot], full_sems.at[which, 0, peer],
                    full_sems.at[which, 1, slot], peer, b)

    def after_pair(which, part, pair, half, cross):
        for f in range(3):
            pair_copy(which, f, part, pair).wait_recv()
            for x in range(nx):
                half[x, rows_of(f)] = (
                    part[core, x, rows_of(f)].astype(F32) + pair[x, rows_of(f)].astype(F32)
                ).astype(BF16)

            def one(k):
                x = lax.rem(col + k, nx)
                cross_copy(which, f, half, cross, col, x, x).start()
            over(nx, one)

    def after_cross(which, half, cross, mine, ring):
        acc = half[col].astype(F32)
        for k in range(1, nx):
            x = lax.rem(col + k, nx)
            for f in range(3):
                cross_copy(which, f, half, cross, x, x, x).wait_recv()
            acc = acc + cross[x].astype(F32)
        if padded > live:
            acc = jnp.concatenate([acc, jnp.zeros((padded - live, ch), F32)], axis=0)
        for k in range(nz):
            mine[k] = acc[k * units * 16:(k + 1) * units * 16].astype(BF16)

        def one(k):
            peer = lax.rem(z + k, nz)
            ring_copy(which, mine, ring, z, peer).start()
        over(nz, one)

    def after_ring(which, mine, ring, full):
        acc = mine[z].astype(F32)
        for k in range(1, nz):
            src = lax.rem(z + k, nz)
            ring_copy(which, mine, ring, src, src).wait_recv()
            acc = acc + ring[src].astype(F32)
        full[z] = acc.astype(BF16)

        def one(k):
            full_copy(which, full, z, lax.rem(z + k, nz)).start()
        over(nz, one)

    def after_full(which, full, out):
        def one(k):
            src = lax.rem(z + k, nz)
            full_copy(which, full, src, src).wait_recv()
        over(nz, one)
        out[...] = full[...].reshape(padded, ch)[0:live].astype(F32)

    def drain(which, part, pair, half, cross, mine, ring, full):
        for f in range(3):
            pair_copy(which, f, part, pair).wait_send()

            def one_x(k):
                x = lax.rem(col + k, nx)
                cross_copy(which, f, half, cross, col, x, x).wait_send()
            over(nx, one_x)

        def one_z(k):
            peer = lax.rem(z + k, nz)
            ring_copy(which, mine, ring, z, peer).wait_send()
            full_copy(which, full, z, peer).wait_send()
        over(nz, one_z)

    tap_grad(0, s_act, dout_t[...], part_a, pair_a)

    acc = recv_stats(1)
    off_total = acc[0:1]
    gain_total = acc[1:2]
    offset_gradient[...] = off_total
    gain_gradient[...] = gain_total
    stores[3].start()
    stores[4].start()
    for i in range(0, lon, 2):
        pieces = []
        for j in (i, i + 1):
            xhat = (first[at(j)] - mean) * inverse
            pieces.append(mask[at(j)] * gains * inverse * (
                dpre[at(j)] - (off_total + xhat * gain_total) / count))
        pair = jnp.concatenate(pieces, axis=0)
        dout_t[:, i * lat:(i + 2) * lat] = pair.T.astype(BF16)
    after_pair(0, part_a, pair_a, half_a, cross_a)
    tap_grad(1, s_in, dout_t[...], part_b, pair_b)
    after_cross(0, half_a, cross_a, mine_a, ring_a)
    after_pair(1, part_b, pair_b, half_b, cross_b)

    total = conv(s_act, w_out)
    output[0] = (total * mask[...]).astype(BF16).reshape(lon, lat, ch)
    stores[0].start()

    after_ring(0, mine_a, ring_a, full_a)
    after_cross(1, half_b, cross_b, mine_b, ring_b)
    after_ring(1, mine_b, ring_b, full_b)
    after_full(0, full_a, grad_out)
    stores[2].start()
    after_full(1, full_b, grad_in)
    stores[1].start()

    for c in cols1 + cols_t + cols2:
        c.wait_send()
    drain_rows(0, rows1)
    drain_rows(1, rows2)
    drain_stats(0)
    drain_stats(1)
    drain(0, part_a, pair_a, half_a, cross_a, mine_a, ring_a, full_a)
    drain(1, part_b, pair_b, half_b, cross_b, mine_b, ring_b, full_b)
    for store in stores:
        store.wait()


def writer(*refs):
    sources, results, held, sems = refs[:5], refs[5:10], refs[10:15], refs[15]
    loads = [pltpu.make_async_copy(sources[k], held[k], sems.at[0, k]) for k in range(5)]
    stores = [pltpu.make_async_copy(held[k], results[k], sems.at[1, k]) for k in range(5)]
    for c in loads:
        c.start()
    for load, store in zip(loads, stores):
        load.wait()
        store.start()
    for c in stores:
        c.wait()


def body(nz, nb, fields, land, conv_in, conv_out, gain, offset, target):
    lon, lat, ch = fields.shape[1:]
    nx = nb // 2
    share = ch // nb
    units = -(-(9 * share // 16) // nz)
    padded = units * 16 * nz
    vm = pltpu.VMEM
    reduction = [
        vm((2, nx, 9 * share, ch), BF16),
        vm((nx, 9 * share, ch), BF16),
        vm((nx, 9 * share, ch), BF16),
        vm((nx, 9 * share, ch), BF16),
        vm((nz, units * 16, ch), BF16),
        vm((nz, units * 16, ch), BF16),
        vm((nz, units * 16, ch), BF16),
    ]
    dma = pltpu.SemaphoreType.DMA
    scratch = [
        vm(fields.shape, BF16),
        vm((9 * share, ch), F32),
        vm((9 * share, ch), F32),
        vm((1, ch), F32),
        vm((1, ch), F32),
        vm(fields.shape, BF16),
        vm(land.shape, jnp.int32),
        vm((3, 3 * ch, ch), BF16),
        vm((3, 3 * ch, ch), BF16),
        vm((1, ch), F32),
        vm((1, ch), F32),
        vm(target.shape, BF16),
        vm((lon * lat, ch), F32),
        vm((lon * lat, ch), F32),
        vm((lon * lat, ch), F32),
        vm((lon * lat, ch), F32),
        vm((lon + 2, lat, 3 * ch), BF16),
        vm((lon + 2, lat, 3 * ch), BF16),
        vm((lon + 2, lat, 3 * ch), BF16),
        vm((3, 3 * ch, ch), BF16),
        vm((ch, lon * lat), BF16),
        vm((nz, 32, ch), BF16),
        vm((nz, 16, ch), BF16),
        vm((3, lat, ch), BF16), vm((3, lat, ch), BF16),
        vm((3, lat, ch), BF16), vm((3, lat, ch), BF16),
        vm((2, nb, 2, ch), F32),
        vm((2, nz, 2, ch), F32),
        *reduction,
        *reduction,
        dma((7,)),
        dma((5,)),
        dma((2, 2, nz)),
        dma((3, 2, 2)),
        dma((2, 2, nb)),
        dma((2, 2, nz)),
        dma((2, 2, 3)),
        dma((2, 2, 3, nx)),
        dma((2, 2, nz)),
        dma((2, 2, nz)),
    ]
    anywhere = pl.BlockSpec(memory_space=pl.ANY)
    limit = 62 * 1024 * 1024
    results = pl.pallas_call(
        functools.partial(kernel, nz, nb, lon, lat, ch, units),
        out_shape=(
            jax.ShapeDtypeStruct(fields.shape, BF16),
            jax.ShapeDtypeStruct((9 * share, ch), F32),
            jax.ShapeDtypeStruct((9 * share, ch), F32),
            jax.ShapeDtypeStruct((1, ch), F32),
            jax.ShapeDtypeStruct((1, ch), F32),
        ),
        in_specs=[anywhere] * 7,
        out_specs=(anywhere,) * 5,
        scratch_shapes=scratch,
        compiler_params=pltpu.CompilerParams(
            collective_id=0, has_side_effects=True, vmem_limit_bytes=limit
        ),
    )(
        fields, land,
        conv_in.reshape(3, 3 * ch, ch), conv_out.reshape(3, 3 * ch, ch),
        gain.reshape(1, ch), offset.reshape(1, ch), target,
    )

    out, grad_in, grad_out, gain_gradient, offset_gradient = pl.pallas_call(
        writer,
        out_shape=tuple(jax.ShapeDtypeStruct(r.shape, r.dtype) for r in results),
        in_specs=[anywhere] * 5,
        out_specs=(anywhere,) * 5,
        scratch_shapes=[vm(r.shape, r.dtype) for r in results] + [dma((2, 5))],
        compiler_params=pltpu.CompilerParams(vmem_limit_bytes=limit),
    )(*results)

    def taps(g):
        return g.reshape(9, share, ch).transpose(0, 2, 1)

    return (out, taps(grad_in), taps(grad_out),
            gain_gradient.reshape(ch), offset_gradient.reshape(ch))


def solution(mesh):
    in_specs = (
        P(("groups", "batch"), "space", None, None),
        P("space", None),
        P(),
        P(),
        P(),
        P(),
        P(("groups", "batch"), "space", None, None),
    )
    out_specs = (
        P(("groups", "batch"), "space", None, None),
        P("groups", None, "batch"),
        P("groups", None, "batch"),
        P("groups"),
        P("groups"),
    )
    step = functools.partial(body, mesh.shape["space"], mesh.shape["batch"])
    return jax.shard_map(step, mesh=mesh, in_specs=in_specs, out_specs=out_specs, check_vma=False)
```

```python
import functools

import jax
import jax.numpy as jnp
from jax import lax
from jax.experimental import pallas as pl
from jax.experimental.pallas import tpu as pltpu
from jax.sharding import PartitionSpec as P

F32 = jnp.float32
BF16 = jnp.bfloat16


def gelu_parts(value):
    inner = 0.7978845608 * (value + 0.044715 * value * value * value)
    hyper = jnp.tanh(inner)
    act = 0.5 * value * (1.0 + hyper)
    slope = 0.5 * (1.0 + hyper) + 0.5 * value * (1.0 - hyper * hyper) * 0.7978845608 * (
        1.0 + 3.0 * 0.044715 * value * value
    )
    return act, slope


def kernel(
    nz, nb, lon, lat, ch, units,
    fields_h, land_h, w_in_h, w_out_h, gain_h, offset_h, target_h,
    output_h, grad_in_h, grad_out_h, gain_gradient_h, offset_gradient_h,
    output, grad_in, grad_out, gain_gradient, offset_gradient,
    fields, land, w_in, w_out, gain, offset, target,
    mask, first, dact, dpre, s_in, s_act, s_dout, w_back, dout_t,
    rows1, rows2, heads, tails, wests, easts,
    stats, ghost_f, ghost_d, ghost_a, fold,
    part_a, pair_a, half_a, cross_a, mine_a, ring_a, full_a,
    part_b, pair_b, half_b, cross_b, mine_b, ring_b, full_b,
    load_sems, store_sems, row_sems, col_sems, stat_sems, pair_sems, cross_sems, ring_sems, full_sems,
):
    nd = nz * nb
    nx = nb // 2
    cells = lon * lat
    z = lax.axis_index("space")
    b = lax.axis_index("batch")
    me = z * nb + b
    core = lax.rem(b, 2)
    col = b // 2
    other = 1 - core

    def device(zz, bb):
        return {"space": zz, "batch": bb}

    def copy(src, dst, send, recv, zz, bb):
        return pltpu.make_async_remote_copy(
            src_ref=src, dst_ref=dst, send_sem=send, recv_sem=recv,
            device_id=device(zz, bb), device_id_type=pl.DeviceIdType.MESH,
        )

    def over(count, fn):
        if count <= 4:
            for k in range(1, count):
                fn(k)
            return

        def step(k, carry):
            fn(k)
            return carry
        lax.fori_loop(1, count, step, 0)

    def row_copy(which, buf, slot, zz):
        return copy(buf.at[slot], buf.at[slot], row_sems.at[which, 0, zz],
                    row_sems.at[which, 1, slot], zz, b)

    def send_rows(which, buf):
        over(nz, lambda k: row_copy(which, buf, z, lax.rem(z + k, nz)).start())

    def recv_rows(which, buf):
        def one(k):
            src = lax.rem(z + k, nz)
            row_copy(which, buf, src, src).wait_recv()
        over(nz, one)

    def drain_rows(which, buf):
        over(nz, lambda k: row_copy(which, buf, z, lax.rem(z + k, nz)).wait_send())

    up = lax.rem(z + 1, nz)
    down = lax.rem(z + nz - 1, nz)

    def col_copies(which):
        return (
            copy(heads.at[which], easts.at[which], col_sems.at[which, 0, 0], col_sems.at[which, 1, 0], down, b),
            copy(tails.at[which], wests.at[which], col_sems.at[which, 0, 1], col_sems.at[which, 1, 1], up, b),
        )

    def stat_copy(which, slot, peer):
        return copy(stats.at[which, slot], stats.at[which, slot], stat_sems.at[which, 0, peer],
                    stat_sems.at[which, 1, slot], peer // nb, lax.rem(peer, nb))

    def send_stats(which):
        over(nd, lambda k: stat_copy(which, me, lax.rem(me + k, nd)).start())

    def recv_stats(which):
        def one(k):
            src = lax.rem(me + k, nd)
            stat_copy(which, src, src).wait_recv()
        over(nd, one)
        acc = stats[which, 0]
        for k in range(1, nd):
            acc = acc + stats[which, k]
        return acc

    def drain_stats(which):
        over(nd, lambda k: stat_copy(which, me, lax.rem(me + k, nd)).wait_send())

    loads = [
        pltpu.make_async_copy(src, dst, load_sems.at[k])
        for k, (src, dst) in enumerate((
            (land_h, land), (fields_h, fields), (target_h, target), (w_in_h, w_in),
            (w_out_h, w_out), (gain_h, gain), (offset_h, offset)))
    ]
    for load in loads:
        load.start()
    stores = [
        pltpu.make_async_copy(src, dst, store_sems.at[k])
        for k, (src, dst) in enumerate((
            (output, output_h), (grad_in, grad_in_h), (grad_out, grad_out_h),
            (gain_gradient, gain_gradient_h), (offset_gradient, offset_gradient_h)))
    ]

    barrier = pltpu.get_barrier_semaphore()

    def greet(k):
        peer = lax.rem(me + k, nd)
        pl.semaphore_signal(barrier, inc=1, device_id=device(peer // nb, lax.rem(peer, nb)),
                            device_id_type=pl.DeviceIdType.MESH)
    over(nd, greet)

    row_id = lax.broadcasted_iota(jnp.int32, (lat, ch), 0)
    zero_row = jnp.zeros((1, ch), F32)

    loads[0].wait()
    land_f = land[...].astype(F32)
    diagonal = lax.broadcasted_iota(jnp.int32, (lat, lat), 0) == lax.broadcasted_iota(
        jnp.int32, (lat, lat), 1)
    spread = jnp.concatenate(
        [jnp.where(diagonal, land_f[i:i + 1, :], 0.0) for i in range(lon)], axis=0)
    mask[...] = jnp.dot(spread.astype(BF16), jnp.ones((lat, ch), BF16), preferred_element_type=F32)

    def at(i):
        return pl.ds(pl.multiple_of(i * lat, lat), lat)

    def loop(start, stop, fn):
        def step(i, carry):
            fn(i)
            return carry
        lax.fori_loop(start, stop, step, 0)

    def shift_up(v, ghost):
        return jnp.concatenate([v[1:], ghost], axis=0)

    def shift_down(v):
        return jnp.concatenate([zero_row, v[:-1]], axis=0)

    def put(s, i, v, lane):
        s[i, :, lane * ch:(lane + 1) * ch] = v.astype(BF16)

    loads[1].wait()
    loads[2].wait()
    def base(s, i, v):
        put(s, i, shift_down(v), 0)
        put(s, i, v, 1)
        put(s, i, shift_up(v, zero_row), 2)

    def mask_lon(i):
        base(s_in, i + 1, fields[0, i].astype(F32) * mask[at(i)])
        target[0, i] = (target[0, i].astype(F32) * mask[at(i)]).astype(BF16)
    loop(0, lon, mask_lon)

    halves = []
    for h in range(2):
        half = mask[h * cells // 2:(h + 1) * cells // 2]
        halves.append(jnp.broadcast_to(jnp.sum(half, axis=0, keepdims=True), (8, ch)))
    rows1[z] = jnp.concatenate(
        [s_in[i + 1, lat - 16:, ch:2 * ch].astype(F32)[15:] for i in range(lon)]
        + [target[0, i, lat - 16:].astype(F32)[15:] for i in range(lon)] + halves, axis=0
    ).astype(BF16)
    heads[0] = s_in[1, :, ch:2 * ch]
    tails[0] = s_in[lon, :, ch:2 * ch]
    heads[1] = target[0, 0]
    tails[1] = target[0, lon - 1]

    cols1 = col_copies(0)
    cols_t = col_copies(1)
    pl.semaphore_wait(barrier, nd - 1)
    for c in cols1:
        c.start()
    send_rows(0, rows1)
    for c in cols_t:
        c.start()

    for i in (0, lon + 1):
        s_in[i] = jnp.zeros((lat, 3 * ch), BF16)

    def window(s, f):
        return s[pl.ds(f, lon)].reshape(cells, 3 * ch)

    def conv(s, w, out, order=(0, 1, 2)):
        part_lon = lon // 2

        def half(h):
            acc = jnp.zeros((part_lon * lat, ch), F32)
            for f in range(3):
                piece = s[pl.ds(h * part_lon + order[f], part_lon)].reshape(part_lon * lat, 3 * ch)
                acc += jnp.dot(piece, w[f], preferred_element_type=F32)
            out[pl.ds(pl.multiple_of(h * part_lon * lat, part_lon * lat), part_lon * lat)] = acc
        loop(0, 2, half)

    def fold_part(rows, w):
        acc = jnp.zeros((2 * lon, ch), F32)
        for f in range(3):
            piece = jnp.concatenate(rows[f:f + lon] + [jnp.zeros((lon, ch), F32)], axis=0)
            acc += jnp.dot(piece.astype(BF16), w[f, 2 * ch:3 * ch, :], preferred_element_type=F32)
        return acc

    def north(v, row):
        return v + jnp.where(row_id == lat - 1, row, 0.0)

    loads[3].wait()
    conv(s_in, w_in, first)
    for load in loads[4:]:
        load.wait()

    for c in cols1:
        c.wait_recv()
    recv_rows(0, rows1)

    opposite = nz - 1 - z
    beyond = lax.rem(nz - z, nz)
    before = lax.rem(2 * nz - 2 - z, nz)

    def ghosts(buf, start):
        facing = buf[opposite].astype(F32)
        left = buf[beyond].astype(F32)[start:start + 1]
        right = buf[before].astype(F32)[start + lon - 1:start + lon]
        return [left] + [facing[start + lon - 1 - i:start + lon - i] for i in range(lon)] + [right]

    ghost_in = ghosts(rows1, 0)
    for i, v in ((0, wests[0].astype(F32)), (lon + 1, easts[0].astype(F32))):
        put(s_in, i, shift_down(v), 0)
        put(s_in, i, v, 1)
        put(s_in, i, shift_up(v, ghost_in[i]), 2)
    from_west = jnp.dot(s_in[0], w_in[0], preferred_element_type=F32)
    from_east = jnp.dot(s_in[lon + 1], w_in[2], preferred_element_type=F32)
    fold[0] = fold_part([zero_row] + ghost_in[1:lon + 1] + [zero_row], w_in)
    for i in range(lon + 2):
        ghost_f[i] = ghost_in[i]
    first[at(0)] += from_west
    first[at(lon - 1)] += from_east

    def first_lon(i, sums):
        v = north(first[at(i)], fold[0, pl.ds(i, 1)])
        v = v.astype(BF16).astype(F32)
        first[at(i)] = v
        held = v * mask[at(i)]
        return sums[0] + held, sums[1] + held * v
    zeros = jnp.zeros((lat, ch), F32)
    sum_1, sum_2 = lax.fori_loop(0, lon, first_lon, (zeros, zeros))
    stats[0, me, 0:1] = jnp.sum(sum_1, axis=0, keepdims=True)
    stats[0, me, 1:2] = jnp.sum(sum_2, axis=0, keepdims=True)
    send_stats(0)

    def turn(f):
        for t in range(3):
            w = w_out[f, t * ch:(t + 1) * ch, :].astype(F32)
            w_back[f, t * ch:(t + 1) * ch, :] = w.T.astype(BF16)
    loop(0, 3, turn)

    count = zero_row
    for k in range(nz):
        packet = rows1[k].astype(F32)
        count = count + packet[16:17] + packet[24:25]
    count = count * float(nb)
    scale = lax.rsqrt(count)

    def scaled(v):
        return (v * scale).astype(BF16).astype(F32)

    for c in cols_t:
        c.wait_recv()
    def base_dout(i, v):
        put(s_dout, i, shift_up(v, zero_row), 0)
        put(s_dout, i, v, 1)
        put(s_dout, i, shift_down(v), 2)

    def lanes(k):
        return pl.ds(pl.multiple_of(k * 2 * lat, 2 * lat), 2 * lat)

    def dout_pair(k):
        pair = [scaled(target[0, 2 * k + t].astype(F32)) for t in range(2)]
        for t in range(2):
            base_dout(2 * k + t + 1, pair[t])
        dout_t[:, lanes(k)] = jnp.concatenate(pair, axis=0).T.astype(BF16)
    loop(0, lon // 2, dout_pair)
    base_dout(0, scaled(wests[1].astype(F32)))
    base_dout(lon + 1, scaled(easts[1].astype(F32)))
    ghost_dout = [scaled(v) for v in ghosts(rows1, lon)]
    conv(s_dout, w_back, dact, (2, 1, 0))
    fold[1] = fold_part(ghost_dout, w_back)

    def finish_lon(i):
        dact[at(i)] = north(dact[at(i)], fold[1, pl.ds(i, 1)]) * mask[at(i)]
        v = s_in[i + 1, :, ch:2 * ch].astype(F32)
        put(s_in, i + 1, shift_up(v, ghost_f[i + 1]), 2)
    loop(0, lon, finish_lon)

    acc = recv_stats(0)
    mean = acc[0:1] / count
    var = acc[1:2] / count - mean * mean
    inverse = lax.rsqrt(var + 1e-05)
    gains = gain[...]
    offsets = offset[...]

    def act_lon(i, sums):
        xhat = (first[at(i)] - mean) * inverse
        act, slope = gelu_parts(gains * xhat + offsets)
        d = dact[at(i)] * slope
        dpre[at(i)] = d
        s_act[i + 1, :, ch:2 * ch] = (act * mask[at(i)]).astype(BF16)
        return sums[0] + d, sums[1] + d * xhat
    sum_1, sum_2 = lax.fori_loop(0, lon, act_lon, (zeros, zeros))
    sum_off = jnp.sum(sum_1, axis=0, keepdims=True)
    sum_gain = jnp.sum(sum_2, axis=0, keepdims=True)
    stats[1, me, 0:1] = sum_off
    stats[1, me, 1:2] = sum_gain
    send_stats(1)
    heads[2] = s_act[1, :, ch:2 * ch]
    tails[2] = s_act[lon, :, ch:2 * ch]
    last = [s_act[i + 1, lat - 16:, ch:2 * ch].astype(F32)[15:] for i in range(lon)]
    rows2[z] = jnp.concatenate(last + [jnp.zeros((lon, ch), F32)], axis=0).astype(BF16)
    cols2 = col_copies(2)
    for c in cols2:
        c.start()
    send_rows(1, rows2)

    for c in cols2:
        c.wait_recv()
    recv_rows(1, rows2)
    ghost_act = ghosts(rows2, 0)
    s_act[0, :, ch:2 * ch] = wests[2]
    s_act[lon + 1, :, ch:2 * ch] = easts[2]
    for i in range(lon + 2):
        ghost_a[i] = ghost_act[i]

    def act_shifts(i):
        v = s_act[i, :, ch:2 * ch].astype(F32)
        put(s_act, i, shift_down(v), 0)
        put(s_act, i, shift_up(v, ghost_a[i]), 2)
    loop(0, lon + 2, act_shifts)

    share = ch // nb
    live = 9 * share
    padded = units * 16 * nz

    def rows_of(f):
        return pl.ds(pl.multiple_of(3 * f * share, 16), 3 * share)

    def tap_grad(which, s, d_t, part, pair):
        def one_f(f):
            g = jnp.dot(d_t[...], window(s, f), preferred_element_type=F32).astype(BF16)
            for t in range(3):
                row = pl.ds(pl.multiple_of((3 * f + t) * share, 16), share)
                for k in range(nb):
                    part[k % 2, k // 2, row, :] = g[k * share:(k + 1) * share, t * ch:(t + 1) * ch]
            pair_copy(which, f, part, pair).start()
        loop(0, 3, one_f)

    def pair_copy(which, f, part, pair):
        return copy(part.at[other, :, rows_of(f)], pair.at[:, rows_of(f)],
                    pair_sems.at[which, 0, f], pair_sems.at[which, 1, f], z, 2 * col + other)

    def cross_copy(which, f, half, cross, slot, peer, x):
        return copy(half.at[peer, rows_of(f)], cross.at[slot, rows_of(f)],
                    cross_sems.at[which, 0, f, peer], cross_sems.at[which, 1, f, slot],
                    z, 2 * x + core)

    def ring_copy(which, mine, ring, slot, peer):
        return copy(mine.at[peer], ring.at[slot], ring_sems.at[which, 0, peer],
                    ring_sems.at[which, 1, slot], peer, b)

    def full_copy(which, full, slot, peer):
        return copy(full.at[slot], full.at[slot], full_sems.at[which, 0, peer],
                    full_sems.at[which, 1, slot], peer, b)

    def after_pair(which, part, pair, half, cross):
        def one_f(f):
            pair_copy(which, f, part, pair).wait_recv()
            for x in range(nx):
                half[x, rows_of(f)] = (
                    part[core, x, rows_of(f)].astype(F32) + pair[x, rows_of(f)].astype(F32)
                ).astype(BF16)

            def one(k):
                x = lax.rem(col + k, nx)
                cross_copy(which, f, half, cross, col, x, x).start()
            over(nx, one)
        loop(0, 3, one_f)

    def after_cross(which, half, cross, mine, ring):
        acc = half[col].astype(F32)
        for k in range(1, nx):
            x = lax.rem(col + k, nx)
            for f in range(3):
                cross_copy(which, f, half, cross, x, x, x).wait_recv()
            acc = acc + cross[x].astype(F32)
        if padded > live:
            acc = jnp.concatenate([acc, jnp.zeros((padded - live, ch), F32)], axis=0)
        for k in range(nz):
            mine[k] = acc[k * units * 16:(k + 1) * units * 16].astype(BF16)

        def one(k):
            peer = lax.rem(z + k, nz)
            ring_copy(which, mine, ring, z, peer).start()
        over(nz, one)

    def after_ring(which, mine, ring, full):
        acc = mine[z].astype(F32)
        for k in range(1, nz):
            src = lax.rem(z + k, nz)
            ring_copy(which, mine, ring, src, src).wait_recv()
            acc = acc + ring[src].astype(F32)
        full[z] = acc.astype(BF16)

        def one(k):
            full_copy(which, full, z, lax.rem(z + k, nz)).start()
        over(nz, one)

    def after_full(which, full, out):
        def one(k):
            src = lax.rem(z + k, nz)
            full_copy(which, full, src, src).wait_recv()
        over(nz, one)
        out[...] = full[...].reshape(padded, ch)[0:live].astype(F32)

    def drain(which, part, pair, half, cross, mine, ring, full):
        for f in range(3):
            pair_copy(which, f, part, pair).wait_send()

            def one_x(k):
                x = lax.rem(col + k, nx)
                cross_copy(which, f, half, cross, col, x, x).wait_send()
            over(nx, one_x)

        def one_z(k):
            peer = lax.rem(z + k, nz)
            ring_copy(which, mine, ring, z, peer).wait_send()
            full_copy(which, full, z, peer).wait_send()
        over(nz, one_z)

    tap_grad(0, s_act, dout_t, part_a, pair_a)

    acc = recv_stats(1)
    off_total = acc[0:1]
    gain_total = acc[1:2]
    offset_gradient[...] = off_total
    gain_gradient[...] = gain_total
    stores[3].start()
    stores[4].start()
    scale_in = gains * inverse
    off_mean = off_total / count
    gain_mean = gain_total / count

    def dfirst_pair(k):
        pieces = []
        for j in (2 * k, 2 * k + 1):
            xhat = (first[at(j)] - mean) * inverse
            pieces.append(mask[at(j)] * scale_in * (dpre[at(j)] - (off_mean + xhat * gain_mean)))
        dout_t[:, lanes(k)] = jnp.concatenate(pieces, axis=0).T.astype(BF16)
    loop(0, lon // 2, dfirst_pair)
    after_pair(0, part_a, pair_a, half_a, cross_a)
    tap_grad(1, s_in, dout_t, part_b, pair_b)
    after_cross(0, half_a, cross_a, mine_a, ring_a)
    after_pair(1, part_b, pair_b, half_b, cross_b)

    conv(s_act, w_out, dact)

    def out_lon(i):
        output[0, i] = (dact[at(i)] * mask[at(i)]).astype(BF16)
    loop(0, lon, out_lon)
    stores[0].start()

    after_ring(0, mine_a, ring_a, full_a)
    after_cross(1, half_b, cross_b, mine_b, ring_b)
    after_ring(1, mine_b, ring_b, full_b)
    after_full(0, full_a, grad_out)
    stores[2].start()
    after_full(1, full_b, grad_in)
    stores[1].start()

    for c in cols1 + cols_t + cols2:
        c.wait_send()
    drain_rows(0, rows1)
    drain_rows(1, rows2)
    drain_stats(0)
    drain_stats(1)
    drain(0, part_a, pair_a, half_a, cross_a, mine_a, ring_a, full_a)
    drain(1, part_b, pair_b, half_b, cross_b, mine_b, ring_b, full_b)
    for store in stores:
        store.wait()


def writer(*refs):
    sources, results, held, sems = refs[:5], refs[5:10], refs[10:15], refs[15]
    loads = [pltpu.make_async_copy(sources[k], held[k], sems.at[0, k]) for k in range(5)]
    stores = [pltpu.make_async_copy(held[k], results[k], sems.at[1, k]) for k in range(5)]
    for c in loads:
        c.start()
    for load, store in zip(loads, stores):
        load.wait()
        store.start()
    for c in stores:
        c.wait()


def body(nz, nb, fields, land, conv_in, conv_out, gain, offset, target):
    lon, lat, ch = fields.shape[1:]
    nd = nz * nb
    nx = nb // 2
    share = ch // nb
    units = -(-(9 * share // 16) // nz)
    padded = units * 16 * nz
    vm = pltpu.VMEM
    reduction = [
        vm((2, nx, 9 * share, ch), BF16),
        vm((nx, 9 * share, ch), BF16),
        vm((nx, 9 * share, ch), BF16),
        vm((nx, 9 * share, ch), BF16),
        vm((nz, units * 16, ch), BF16),
        vm((nz, units * 16, ch), BF16),
        vm((nz, units * 16, ch), BF16),
    ]
    dma = pltpu.SemaphoreType.DMA
    scratch = [
        vm(fields.shape, BF16),
        vm((9 * share, ch), F32),
        vm((9 * share, ch), F32),
        vm((1, ch), F32),
        vm((1, ch), F32),
        vm(fields.shape, BF16),
        vm(land.shape, jnp.int32),
        vm((3, 3 * ch, ch), BF16),
        vm((3, 3 * ch, ch), BF16),
        vm((1, ch), F32),
        vm((1, ch), F32),
        vm(target.shape, BF16),
        vm((lon * lat, ch), F32),
        vm((lon * lat, ch), F32),
        vm((lon * lat, ch), F32),
        vm((lon * lat, ch), F32),
        vm((lon + 2, lat, 3 * ch), BF16),
        vm((lon + 2, lat, 3 * ch), BF16),
        vm((lon + 2, lat, 3 * ch), BF16),
        vm((3, 3 * ch, ch), BF16),
        vm((ch, lon * lat), BF16),
        vm((nz, 32, ch), BF16),
        vm((nz, 16, ch), BF16),
        vm((3, lat, ch), BF16), vm((3, lat, ch), BF16),
        vm((3, lat, ch), BF16), vm((3, lat, ch), BF16),
        vm((2, nd, 2, ch), F32),
        vm((lon + 2, 1, ch), F32),
        vm((lon + 2, 1, ch), F32),
        vm((lon + 2, 1, ch), F32),
        vm((2, 2 * lon, ch), F32),
        *reduction,
        *reduction,
        dma((7,)),
        dma((5,)),
        dma((2, 2, nz)),
        dma((3, 2, 2)),
        dma((2, 2, nd)),
        dma((2, 2, 3)),
        dma((2, 2, 3, nx)),
        dma((2, 2, nz)),
        dma((2, 2, nz)),
    ]
    anywhere = pl.BlockSpec(memory_space=pl.ANY)
    limit = 62 * 1024 * 1024
    results = pl.pallas_call(
        functools.partial(kernel, nz, nb, lon, lat, ch, units),
        out_shape=(
            jax.ShapeDtypeStruct(fields.shape, BF16),
            jax.ShapeDtypeStruct((9 * share, ch), F32),
            jax.ShapeDtypeStruct((9 * share, ch), F32),
            jax.ShapeDtypeStruct((1, ch), F32),
            jax.ShapeDtypeStruct((1, ch), F32),
        ),
        in_specs=[anywhere] * 7,
        out_specs=(anywhere,) * 5,
        scratch_shapes=scratch,
        compiler_params=pltpu.CompilerParams(
            collective_id=0, has_side_effects=True, vmem_limit_bytes=limit
        ),
    )(
        fields, land,
        conv_in.reshape(3, 3 * ch, ch), conv_out.reshape(3, 3 * ch, ch),
        gain.reshape(1, ch), offset.reshape(1, ch), target,
    )

    out, grad_in, grad_out, gain_gradient, offset_gradient = pl.pallas_call(
        writer,
        out_shape=tuple(jax.ShapeDtypeStruct(r.shape, r.dtype) for r in results),
        in_specs=[anywhere] * 5,
        out_specs=(anywhere,) * 5,
        scratch_shapes=[vm(r.shape, r.dtype) for r in results] + [dma((2, 5))],
        compiler_params=pltpu.CompilerParams(vmem_limit_bytes=limit),
    )(*results)

    def taps(g):
        return g.reshape(9, share, ch).transpose(0, 2, 1)

    return (out, taps(grad_in), taps(grad_out),
            gain_gradient.reshape(ch), offset_gradient.reshape(ch))


def solution(mesh):
    in_specs = (
        P(("groups", "batch"), "space", None, None),
        P("space", None),
        P(),
        P(),
        P(),
        P(),
        P(("groups", "batch"), "space", None, None),
    )
    out_specs = (
        P(("groups", "batch"), "space", None, None),
        P("groups", None, "batch"),
        P("groups", None, "batch"),
        P("groups"),
        P("groups"),
    )
    step = functools.partial(body, mesh.shape["space"], mesh.shape["batch"])
    return jax.shard_map(step, mesh=mesh, in_specs=in_specs, out_specs=out_specs, check_vma=False)
```

```python
import functools

import jax
import jax.numpy as jnp
from jax import lax
from jax.experimental import pallas as pl
from jax.experimental.pallas import tpu as pltpu
from jax.sharding import PartitionSpec as P

F32 = jnp.float32
BF16 = jnp.bfloat16


def gelu_parts(value):
    inner = 0.7978845608 * (value + 0.044715 * value * value * value)
    hyper = jnp.tanh(inner)
    act = 0.5 * value * (1.0 + hyper)
    slope = 0.5 * (1.0 + hyper) + 0.5 * value * (1.0 - hyper * hyper) * 0.7978845608 * (
        1.0 + 3.0 * 0.044715 * value * value
    )
    return act, slope


def kernel(
    nz, nb, lon, lat, ch, units,
    fields_h, land_h, w_in_h, w_out_h, gain_h, offset_h, target_h,
    output_h, grad_in_h, grad_out_h, gain_gradient_h, offset_gradient_h,
    output, grad_in, grad_out, gain_gradient, offset_gradient,
    fields, land, w_in, w_out, gain, offset, target,
    mask, first, dact, dpre, s_in, s_act, s_dout, w_back, dout_t,
    rows1, rows2, heads, tails, wests, easts,
    stats, ghost_f, ghost_d, ghost_a, fold,
    acc_a, north_t,
    part_a, peer_a, mine_a, ring_a, full_a,
    part_b, peer_b, mine_b, ring_b, full_b,
    load_sems, store_sems, row_sems, col_sems, stat_sems, part_sems, ring_sems, full_sems,
):
    nd = nz * nb
    cells = lon * lat
    z = lax.axis_index("space")
    b = lax.axis_index("batch")
    me = z * nb + b

    def device(zz, bb):
        return {"space": zz, "batch": bb}

    def copy(src, dst, send, recv, zz, bb):
        return pltpu.make_async_remote_copy(
            src_ref=src, dst_ref=dst, send_sem=send, recv_sem=recv,
            device_id=device(zz, bb), device_id_type=pl.DeviceIdType.MESH,
        )

    def over(count, fn):
        if count <= 4:
            for k in range(1, count):
                fn(k)
            return

        def step(k, carry):
            fn(k)
            return carry
        lax.fori_loop(1, count, step, 0)

    def row_copy(which, buf, slot, zz):
        return copy(buf.at[slot], buf.at[slot], row_sems.at[which, 0, zz],
                    row_sems.at[which, 1, slot], zz, b)

    def send_rows(which, buf):
        over(nz, lambda k: row_copy(which, buf, z, lax.rem(z + k, nz)).start())

    def recv_rows(which, buf):
        def one(k):
            src = lax.rem(z + k, nz)
            row_copy(which, buf, src, src).wait_recv()
        over(nz, one)

    def drain_rows(which, buf):
        over(nz, lambda k: row_copy(which, buf, z, lax.rem(z + k, nz)).wait_send())

    up = lax.rem(z + 1, nz)
    down = lax.rem(z + nz - 1, nz)

    def col_copies(which):
        return (
            copy(heads.at[which], easts.at[which], col_sems.at[which, 0, 0], col_sems.at[which, 1, 0], down, b),
            copy(tails.at[which], wests.at[which], col_sems.at[which, 0, 1], col_sems.at[which, 1, 1], up, b),
        )

    def stat_copy(which, slot, peer):
        return copy(stats.at[which, slot], stats.at[which, slot], stat_sems.at[which, 0, peer],
                    stat_sems.at[which, 1, slot], peer // nb, lax.rem(peer, nb))

    def send_stats(which):
        over(nd, lambda k: stat_copy(which, me, lax.rem(me + k, nd)).start())

    def recv_stats(which):
        def one(k):
            src = lax.rem(me + k, nd)
            stat_copy(which, src, src).wait_recv()
        over(nd, one)
        acc = stats[which, 0]
        for k in range(1, nd):
            acc = acc + stats[which, k]
        return acc

    def drain_stats(which):
        over(nd, lambda k: stat_copy(which, me, lax.rem(me + k, nd)).wait_send())

    loads = [
        pltpu.make_async_copy(src, dst, load_sems.at[k])
        for k, (src, dst) in enumerate((
            (land_h, land), (fields_h, fields), (target_h, target), (w_in_h, w_in),
            (w_out_h, w_out), (gain_h, gain), (offset_h, offset)))
    ]
    for load in loads:
        load.start()
    stores = [
        pltpu.make_async_copy(src, dst, store_sems.at[k])
        for k, (src, dst) in enumerate((
            (output, output_h), (grad_in, grad_in_h), (grad_out, grad_out_h),
            (gain_gradient, gain_gradient_h), (offset_gradient, offset_gradient_h)))
    ]

    barrier = pltpu.get_barrier_semaphore()

    def greet(k):
        peer = lax.rem(me + k, nd)
        pl.semaphore_signal(barrier, inc=1, device_id=device(peer // nb, lax.rem(peer, nb)),
                            device_id_type=pl.DeviceIdType.MESH)
    over(nd, greet)

    row_id = lax.broadcasted_iota(jnp.int32, (lat, ch), 0)
    zero_row = jnp.zeros((1, ch), F32)

    loads[0].wait()
    land_f = land[...].astype(F32)
    diagonal = lax.broadcasted_iota(jnp.int32, (lat, lat), 0) == lax.broadcasted_iota(
        jnp.int32, (lat, lat), 1)
    spread = jnp.concatenate(
        [jnp.where(diagonal, land_f[i:i + 1, :], 0.0) for i in range(lon)], axis=0)
    mask[...] = jnp.dot(spread.astype(BF16), jnp.ones((lat, ch), BF16), preferred_element_type=F32)

    def at(i):
        return pl.ds(pl.multiple_of(i * lat, lat), lat)

    def loop(start, stop, fn):
        def step(i, carry):
            fn(i)
            return carry
        lax.fori_loop(start, stop, step, 0)

    def shift_up(v, ghost):
        return jnp.concatenate([v[1:], ghost], axis=0)

    def shift_down(v):
        return jnp.concatenate([zero_row, v[:-1]], axis=0)

    def put(s, i, v, lane):
        s[i, :, lane * ch:(lane + 1) * ch] = v.astype(BF16)

    loads[1].wait()
    def base(s, i, v):
        put(s, i, shift_down(v), 0)
        put(s, i, v, 1)
        put(s, i, shift_up(v, zero_row), 2)

    def mask_lon(i):
        base(s_in, i + 1, fields[0, i].astype(F32) * mask[at(i)])
    loop(0, lon, mask_lon)
    heads[0] = s_in[1, :, ch:2 * ch]
    tails[0] = s_in[lon, :, ch:2 * ch]
    cols1 = col_copies(0)
    cols_t = col_copies(1)
    pl.semaphore_wait(barrier, nd - 1)
    for c in cols1:
        c.start()

    loads[2].wait()

    def mask_target(i):
        target[0, i] = (target[0, i].astype(F32) * mask[at(i)]).astype(BF16)
    loop(0, lon, mask_target)

    halves = []
    for h in range(2):
        half = mask[h * cells // 2:(h + 1) * cells // 2]
        halves.append(jnp.broadcast_to(jnp.sum(half, axis=0, keepdims=True), (8, ch)))
    rows1[z] = jnp.concatenate(
        [s_in[i + 1, lat - 16:, ch:2 * ch].astype(F32)[15:] for i in range(lon)]
        + [target[0, i, lat - 16:].astype(F32)[15:] for i in range(lon)] + halves, axis=0
    ).astype(BF16)
    heads[1] = target[0, 0]
    tails[1] = target[0, lon - 1]

    send_rows(0, rows1)
    for c in cols_t:
        c.start()

    for i in (0, lon + 1):
        s_in[i] = jnp.zeros((lat, 3 * ch), BF16)

    def window(s, f):
        return s[pl.ds(f, lon)].reshape(cells, 3 * ch)

    def conv(s, w, out, order=(0, 1, 2)):
        part_lon = lon // 2

        def half(h):
            acc = jnp.zeros((part_lon * lat, ch), F32)
            for f in range(3):
                piece = s[pl.ds(h * part_lon + order[f], part_lon)].reshape(part_lon * lat, 3 * ch)
                acc += jnp.dot(piece, w[f], preferred_element_type=F32)
            out[pl.ds(pl.multiple_of(h * part_lon * lat, part_lon * lat), part_lon * lat)] = acc
        loop(0, 2, half)

    def fold_part(rows, w):
        acc = jnp.zeros((2 * lon, ch), F32)
        for f in range(3):
            piece = jnp.concatenate(rows[f:f + lon] + [jnp.zeros((lon, ch), F32)], axis=0)
            acc += jnp.dot(piece.astype(BF16), w[f, 2 * ch:3 * ch, :], preferred_element_type=F32)
        return acc

    def north(v, row):
        return v + jnp.where(row_id == lat - 1, row, 0.0)

    loads[3].wait()
    conv(s_in, w_in, first)
    for load in loads[4:]:
        load.wait()

    for c in cols1:
        c.wait_recv()
    recv_rows(0, rows1)

    opposite = nz - 1 - z
    beyond = lax.rem(nz - z, nz)
    before = lax.rem(2 * nz - 2 - z, nz)

    def ghosts(buf, start):
        facing = buf[opposite].astype(F32)
        left = buf[beyond].astype(F32)[start:start + 1]
        right = buf[before].astype(F32)[start + lon - 1:start + lon]
        return [left] + [facing[start + lon - 1 - i:start + lon - i] for i in range(lon)] + [right]

    ghost_in = ghosts(rows1, 0)
    for i, v in ((0, wests[0].astype(F32)), (lon + 1, easts[0].astype(F32))):
        put(s_in, i, shift_down(v), 0)
        put(s_in, i, v, 1)
        put(s_in, i, shift_up(v, ghost_in[i]), 2)
    from_west = jnp.dot(s_in[0], w_in[0], preferred_element_type=F32)
    from_east = jnp.dot(s_in[lon + 1], w_in[2], preferred_element_type=F32)
    fold[0] = fold_part([zero_row] + ghost_in[1:lon + 1] + [zero_row], w_in)
    for i in range(lon + 2):
        ghost_f[i] = ghost_in[i]
    first[at(0)] += from_west
    first[at(lon - 1)] += from_east

    def first_lon(i, sums):
        v = north(first[at(i)], fold[0, pl.ds(i, 1)])
        v = v.astype(BF16).astype(F32)
        first[at(i)] = v
        held = v * mask[at(i)]
        return sums[0] + held, sums[1] + held * v
    zeros = jnp.zeros((lat, ch), F32)
    sum_1, sum_2 = lax.fori_loop(0, lon, first_lon, (zeros, zeros))
    stats[0, me, 0:1] = jnp.sum(sum_1, axis=0, keepdims=True)
    stats[0, me, 1:2] = jnp.sum(sum_2, axis=0, keepdims=True)
    send_stats(0)

    def turn(f):
        for t in range(3):
            w = w_out[f, t * ch:(t + 1) * ch, :].astype(F32)
            w_back[f, t * ch:(t + 1) * ch, :] = w.T.astype(BF16)
    loop(0, 3, turn)

    count = zero_row
    for k in range(nz):
        packet = rows1[k].astype(F32)
        count = count + packet[16:17] + packet[24:25]
    count = count * float(nb)
    scale = lax.rsqrt(count)

    def scaled(v):
        return (v * scale).astype(BF16).astype(F32)

    for c in cols_t:
        c.wait_recv()
    def base_dout(i, v):
        put(s_dout, i, shift_up(v, zero_row), 0)
        put(s_dout, i, v, 1)
        put(s_dout, i, shift_down(v), 2)

    def lanes(k):
        return pl.ds(pl.multiple_of(k * 2 * lat, 2 * lat), 2 * lat)

    def dout_pair(k):
        pair = [scaled(target[0, 2 * k + t].astype(F32)) for t in range(2)]
        for t in range(2):
            base_dout(2 * k + t + 1, pair[t])
        dout_t[:, lanes(k)] = jnp.concatenate(pair, axis=0).T.astype(BF16)
    loop(0, lon // 2, dout_pair)
    base_dout(0, scaled(wests[1].astype(F32)))
    base_dout(lon + 1, scaled(easts[1].astype(F32)))
    ghost_dout = [scaled(v) for v in ghosts(rows1, lon)]
    north_d = [s_dout[i + 1, lat - 16:, ch:2 * ch].astype(F32)[15:] for i in range(lon)]
    north_t[...] = jnp.concatenate(
        north_d + [jnp.zeros((ch - lon, ch), F32)], axis=0).T.astype(BF16)
    conv(s_dout, w_back, dact, (2, 1, 0))
    fold[1] = fold_part(ghost_dout, w_back)

    def finish_lon(i):
        dact[at(i)] = north(dact[at(i)], fold[1, pl.ds(i, 1)]) * mask[at(i)]
        v = s_in[i + 1, :, ch:2 * ch].astype(F32)
        put(s_in, i + 1, shift_up(v, ghost_f[i + 1]), 2)
    loop(0, lon, finish_lon)

    acc = recv_stats(0)
    mean = acc[0:1] / count
    var = acc[1:2] / count - mean * mean
    inverse = lax.rsqrt(var + 1e-05)
    gains = gain[...]
    offsets = offset[...]

    def act_lon(i, sums):
        xhat = (first[at(i)] - mean) * inverse
        act, slope = gelu_parts(gains * xhat + offsets)
        d = dact[at(i)] * slope
        dpre[at(i)] = d
        base(s_act, i + 1, (act * mask[at(i)]).astype(BF16).astype(F32))
        return sums[0] + d, sums[1] + d * xhat
    sum_1, sum_2 = lax.fori_loop(0, lon, act_lon, (zeros, zeros))
    sum_off = jnp.sum(sum_1, axis=0, keepdims=True)
    sum_gain = jnp.sum(sum_2, axis=0, keepdims=True)
    stats[1, me, 0:1] = sum_off
    stats[1, me, 1:2] = sum_gain
    send_stats(1)
    heads[2] = s_act[1, :, ch:2 * ch]
    tails[2] = s_act[lon, :, ch:2 * ch]
    last = [s_act[i + 1, lat - 16:, ch:2 * ch].astype(F32)[15:] for i in range(lon)]
    rows2[z] = jnp.concatenate(last + [jnp.zeros((lon, ch), F32)], axis=0).astype(BF16)
    cols2 = col_copies(2)
    for c in cols2:
        c.start()
    send_rows(1, rows2)

    for i in (0, lon + 1):
        s_act[i] = jnp.zeros((lat, 3 * ch), BF16)

    def own_a(f):
        acc_a[f] = jnp.dot(dout_t[...], window(s_act, f), preferred_element_type=F32)
    loop(0, 3, own_a)

    for c in cols2:
        c.wait_recv()
    recv_rows(1, rows2)
    ghost_act = ghosts(rows2, 0)
    for i in range(lon + 2):
        ghost_a[i] = ghost_act[i]
    for i, v in ((0, wests[2].astype(F32)), (lon + 1, easts[2].astype(F32))):
        put(s_act, i, shift_down(v), 0)
        put(s_act, i, v, 1)
        put(s_act, i, shift_up(v, ghost_act[i]), 2)
    blank = jnp.zeros((lat, 3 * ch), BF16)
    acc_a[0] += jnp.dot(dout_t[:, 0:2 * lat], jnp.concatenate([s_act[0], blank], axis=0),
                        preferred_element_type=F32)
    acc_a[2] += jnp.dot(dout_t[:, cells - 2 * lat:],
                        jnp.concatenate([blank, s_act[lon + 1]], axis=0),
                        preferred_element_type=F32)
    inner = [zero_row] + ghost_act[1:lon + 1] + [zero_row]
    for f in range(3):
        piece = jnp.concatenate(inner[f:f + lon] + [jnp.zeros((ch - lon, ch), F32)], axis=0)
        acc_a[f, :, 2 * ch:] += jnp.dot(north_t[...], piece.astype(BF16),
                                        preferred_element_type=F32)

    share = ch // nb
    live = 9 * share
    padded = units * 16 * nz

    def rows_of(f):
        return pl.ds(pl.multiple_of(3 * f * share, 16), 3 * share)

    def part_copy(which, f, part, peers, slot, peer):
        return copy(part.at[peer, rows_of(f)], peers.at[slot, rows_of(f)],
                    part_sems.at[which, 0, f, peer], part_sems.at[which, 1, f, slot], z, peer)

    def send_part(which, f, g, part, peers):
        for t in range(3):
            row = pl.ds(pl.multiple_of((3 * f + t) * share, 16), share)
            for k in range(nb):
                part[k, row, :] = g[k * share:(k + 1) * share, t * ch:(t + 1) * ch].astype(BF16)

        def one(k):
            peer = lax.rem(b + k, nb)
            part_copy(which, f, part, peers, b, peer).start()
        over(nb, one)

    def ring_copy(which, mine, ring, slot, peer):
        return copy(mine.at[peer], ring.at[slot], ring_sems.at[which, 0, peer],
                    ring_sems.at[which, 1, slot], peer, b)

    def full_copy(which, full, slot, peer):
        return copy(full.at[slot], full.at[slot], full_sems.at[which, 0, peer],
                    full_sems.at[which, 1, slot], peer, b)

    def after_part(which, part, peers, mine, ring):
        acc = part[b].astype(F32)
        for k in range(1, nb):
            src = lax.rem(b + k, nb)
            for f in range(3):
                part_copy(which, f, part, peers, src, src).wait_recv()
            acc = acc + peers[src].astype(F32)
        if padded > live:
            acc = jnp.concatenate([acc, jnp.zeros((padded - live, ch), F32)], axis=0)
        for k in range(nz):
            mine[k] = acc[k * units * 16:(k + 1) * units * 16].astype(BF16)

        def one(k):
            peer = lax.rem(z + k, nz)
            ring_copy(which, mine, ring, z, peer).start()
        over(nz, one)

    def after_ring(which, mine, ring, full):
        acc = mine[z].astype(F32)
        for k in range(1, nz):
            src = lax.rem(z + k, nz)
            ring_copy(which, mine, ring, src, src).wait_recv()
            acc = acc + ring[src].astype(F32)
        full[z] = acc.astype(BF16)

        def one(k):
            full_copy(which, full, z, lax.rem(z + k, nz)).start()
        over(nz, one)

    def after_full(which, full, out):
        def one(k):
            src = lax.rem(z + k, nz)
            full_copy(which, full, src, src).wait_recv()
        over(nz, one)
        out[...] = full[...].reshape(padded, ch)[0:live].astype(F32)

    def drain(which, part, peers, mine, ring, full):
        for f in range(3):
            def one_b(k):
                peer = lax.rem(b + k, nb)
                part_copy(which, f, part, peers, b, peer).wait_send()
            over(nb, one_b)

        def one_z(k):
            peer = lax.rem(z + k, nz)
            ring_copy(which, mine, ring, z, peer).wait_send()
            full_copy(which, full, z, peer).wait_send()
        over(nz, one_z)

    loop(0, 3, lambda f: send_part(0, f, acc_a[f], part_a, peer_a))

    acc = recv_stats(1)
    off_total = acc[0:1]
    gain_total = acc[1:2]
    offset_gradient[...] = off_total
    gain_gradient[...] = gain_total
    stores[3].start()
    stores[4].start()
    scale_in = gains * inverse
    off_mean = off_total / count
    gain_mean = gain_total / count

    def dfirst_pair(k):
        pieces = []
        for j in (2 * k, 2 * k + 1):
            xhat = (first[at(j)] - mean) * inverse
            pieces.append(mask[at(j)] * scale_in * (dpre[at(j)] - (off_mean + xhat * gain_mean)))
        dout_t[:, lanes(k)] = jnp.concatenate(pieces, axis=0).T.astype(BF16)
    loop(0, lon // 2, dfirst_pair)

    def tap_b(f):
        g = jnp.dot(dout_t[...], window(s_in, f), preferred_element_type=F32)
        send_part(1, f, g, part_b, peer_b)
    loop(0, 3, tap_b)
    after_part(0, part_a, peer_a, mine_a, ring_a)

    def finish_act(i):
        v = s_act[i + 1, :, ch:2 * ch].astype(F32)
        put(s_act, i + 1, shift_up(v, ghost_a[i + 1]), 2)
    loop(0, lon, finish_act)
    conv(s_act, w_out, dact)

    def out_lon(i):
        output[0, i] = (dact[at(i)] * mask[at(i)]).astype(BF16)
    loop(0, lon, out_lon)
    stores[0].start()

    after_ring(0, mine_a, ring_a, full_a)
    after_part(1, part_b, peer_b, mine_b, ring_b)
    after_ring(1, mine_b, ring_b, full_b)
    after_full(0, full_a, grad_out)
    stores[2].start()
    after_full(1, full_b, grad_in)
    stores[1].start()

    for c in cols1 + cols_t + cols2:
        c.wait_send()
    drain_rows(0, rows1)
    drain_rows(1, rows2)
    drain_stats(0)
    drain_stats(1)
    drain(0, part_a, peer_a, mine_a, ring_a, full_a)
    drain(1, part_b, peer_b, mine_b, ring_b, full_b)
    for store in stores:
        store.wait()


def writer(*refs):
    sources, results, held, sems = refs[:5], refs[5:10], refs[10:15], refs[15]
    loads = [pltpu.make_async_copy(sources[k], held[k], sems.at[0, k]) for k in range(5)]
    stores = [pltpu.make_async_copy(held[k], results[k], sems.at[1, k]) for k in range(5)]
    for c in loads:
        c.start()
    for load, store in zip(loads, stores):
        load.wait()
        store.start()
    for c in stores:
        c.wait()


def body(nz, nb, fields, land, conv_in, conv_out, gain, offset, target):
    lon, lat, ch = fields.shape[1:]
    nd = nz * nb
    share = ch // nb
    units = -(-(9 * share // 16) // nz)
    padded = units * 16 * nz
    vm = pltpu.VMEM
    reduction = [
        vm((nb, 9 * share, ch), BF16),
        vm((nb, 9 * share, ch), BF16),
        vm((nz, units * 16, ch), BF16),
        vm((nz, units * 16, ch), BF16),
        vm((nz, units * 16, ch), BF16),
    ]
    dma = pltpu.SemaphoreType.DMA
    scratch = [
        vm(fields.shape, BF16),
        vm((9 * share, ch), F32),
        vm((9 * share, ch), F32),
        vm((1, ch), F32),
        vm((1, ch), F32),
        vm(fields.shape, BF16),
        vm(land.shape, jnp.int32),
        vm((3, 3 * ch, ch), BF16),
        vm((3, 3 * ch, ch), BF16),
        vm((1, ch), F32),
        vm((1, ch), F32),
        vm(target.shape, BF16),
        vm((lon * lat, ch), F32),
        vm((lon * lat, ch), F32),
        vm((lon * lat, ch), F32),
        vm((lon * lat, ch), F32),
        vm((lon + 2, lat, 3 * ch), BF16),
        vm((lon + 2, lat, 3 * ch), BF16),
        vm((lon + 2, lat, 3 * ch), BF16),
        vm((3, 3 * ch, ch), BF16),
        vm((ch, lon * lat), BF16),
        vm((nz, 32, ch), BF16),
        vm((nz, 16, ch), BF16),
        vm((3, lat, ch), BF16), vm((3, lat, ch), BF16),
        vm((3, lat, ch), BF16), vm((3, lat, ch), BF16),
        vm((2, nd, 2, ch), F32),
        vm((lon + 2, 1, ch), F32),
        vm((lon + 2, 1, ch), F32),
        vm((lon + 2, 1, ch), F32),
        vm((2, 2 * lon, ch), F32),
        vm((3, ch, 3 * ch), F32),
        vm((ch, ch), BF16),
        *reduction,
        *reduction,
        dma((7,)),
        dma((5,)),
        dma((2, 2, nz)),
        dma((3, 2, 2)),
        dma((2, 2, nd)),
        dma((2, 2, 3, nb)),
        dma((2, 2, nz)),
        dma((2, 2, nz)),
    ]
    anywhere = pl.BlockSpec(memory_space=pl.ANY)
    limit = 62 * 1024 * 1024
    results = pl.pallas_call(
        functools.partial(kernel, nz, nb, lon, lat, ch, units),
        out_shape=(
            jax.ShapeDtypeStruct(fields.shape, BF16),
            jax.ShapeDtypeStruct((9 * share, ch), F32),
            jax.ShapeDtypeStruct((9 * share, ch), F32),
            jax.ShapeDtypeStruct((1, ch), F32),
            jax.ShapeDtypeStruct((1, ch), F32),
        ),
        in_specs=[anywhere] * 7,
        out_specs=(anywhere,) * 5,
        scratch_shapes=scratch,
        compiler_params=pltpu.CompilerParams(
            collective_id=0, has_side_effects=True, vmem_limit_bytes=limit
        ),
    )(
        fields, land,
        conv_in.reshape(3, 3 * ch, ch), conv_out.reshape(3, 3 * ch, ch),
        gain.reshape(1, ch), offset.reshape(1, ch), target,
    )

    out, grad_in, grad_out, gain_gradient, offset_gradient = pl.pallas_call(
        writer,
        out_shape=tuple(jax.ShapeDtypeStruct(r.shape, r.dtype) for r in results),
        in_specs=[anywhere] * 5,
        out_specs=(anywhere,) * 5,
        scratch_shapes=[vm(r.shape, r.dtype) for r in results] + [dma((2, 5))],
        compiler_params=pltpu.CompilerParams(vmem_limit_bytes=limit),
    )(*results)

    def taps(g):
        return g.reshape(9, share, ch).transpose(0, 2, 1)

    return (out, taps(grad_in), taps(grad_out),
            gain_gradient.reshape(ch), offset_gradient.reshape(ch))


def solution(mesh):
    in_specs = (
        P(("groups", "batch"), "space", None, None),
        P("space", None),
        P(),
        P(),
        P(),
        P(),
        P(("groups", "batch"), "space", None, None),
    )
    out_specs = (
        P(("groups", "batch"), "space", None, None),
        P("groups", None, "batch"),
        P("groups", None, "batch"),
        P("groups"),
        P("groups"),
    )
    step = functools.partial(body, mesh.shape["space"], mesh.shape["batch"])
    return jax.shard_map(step, mesh=mesh, in_specs=in_specs, out_specs=out_specs, check_vma=False)
```

```python
import functools

import jax
import jax.numpy as jnp
from jax import lax
from jax.experimental import pallas as pl
from jax.experimental.pallas import tpu as pltpu
from jax.sharding import PartitionSpec as P

F32 = jnp.float32
BF16 = jnp.bfloat16


def gelu_parts(value):
    inner = 0.7978845608 * (value + 0.044715 * value * value * value)
    hyper = jnp.tanh(inner)
    act = 0.5 * value * (1.0 + hyper)
    slope = 0.5 * (1.0 + hyper) + 0.5 * value * (1.0 - hyper * hyper) * 0.7978845608 * (
        1.0 + 3.0 * 0.044715 * value * value
    )
    return act, slope


def kernel(
    nz, nb, lon, lat, ch, units,
    fields_h, land_h, w_in_h, w_out_h, gain_h, offset_h, target_h,
    output_h, grad_in_h, grad_out_h, gain_gradient_h, offset_gradient_h,
    output, grad_in, grad_out, gain_gradient, offset_gradient,
    fields, land, w_in, w_out, gain, offset, target,
    mask, first, dact, dpre, s_in, s_act, s_dout, w_back, dout_t,
    rows1, rows2, heads, tails, wests, easts,
    stats, ghost_f, ghost_d, ghost_a, fold,
    acc_a, north_t,
    part_a, pair_a, half_a, cross_a, mine_a, ring_a, full_a,
    part_b, pair_b, half_b, cross_b, mine_b, ring_b, full_b,
    load_sems, store_sems, row_sems, col_sems, stat_sems, pair_sems, cross_sems, ring_sems, full_sems,
):
    nd = nz * nb
    nx = nb // 2
    cells = lon * lat
    z = lax.axis_index("space")
    b = lax.axis_index("batch")
    me = z * nb + b
    core = lax.rem(b, 2)
    col = b // 2
    other = 1 - core

    def device(zz, bb):
        return {"space": zz, "batch": bb}

    def copy(src, dst, send, recv, zz, bb):
        return pltpu.make_async_remote_copy(
            src_ref=src, dst_ref=dst, send_sem=send, recv_sem=recv,
            device_id=device(zz, bb), device_id_type=pl.DeviceIdType.MESH,
        )

    def over(count, fn):
        if count <= 4:
            for k in range(1, count):
                fn(k)
            return

        def step(k, carry):
            fn(k)
            return carry
        lax.fori_loop(1, count, step, 0)

    def row_copy(which, buf, slot, zz):
        return copy(buf.at[slot], buf.at[slot], row_sems.at[which, 0, zz],
                    row_sems.at[which, 1, slot], zz, b)

    def send_rows(which, buf):
        over(nz, lambda k: row_copy(which, buf, z, lax.rem(z + k, nz)).start())

    def recv_rows(which, buf):
        def one(k):
            src = lax.rem(z + k, nz)
            row_copy(which, buf, src, src).wait_recv()
        over(nz, one)

    def drain_rows(which, buf):
        over(nz, lambda k: row_copy(which, buf, z, lax.rem(z + k, nz)).wait_send())

    up = lax.rem(z + 1, nz)
    down = lax.rem(z + nz - 1, nz)

    def col_copies(which):
        return (
            copy(heads.at[which], easts.at[which], col_sems.at[which, 0, 0], col_sems.at[which, 1, 0], down, b),
            copy(tails.at[which], wests.at[which], col_sems.at[which, 0, 1], col_sems.at[which, 1, 1], up, b),
        )

    def stat_copy(which, slot, peer):
        return copy(stats.at[which, slot], stats.at[which, slot], stat_sems.at[which, 0, peer],
                    stat_sems.at[which, 1, slot], peer // nb, lax.rem(peer, nb))

    def send_stats(which):
        over(nd, lambda k: stat_copy(which, me, lax.rem(me + k, nd)).start())

    def recv_stats(which):
        def one(k):
            src = lax.rem(me + k, nd)
            stat_copy(which, src, src).wait_recv()
        over(nd, one)
        acc = stats[which, 0]
        for k in range(1, nd):
            acc = acc + stats[which, k]
        return acc

    def drain_stats(which):
        over(nd, lambda k: stat_copy(which, me, lax.rem(me + k, nd)).wait_send())

    loads = [
        pltpu.make_async_copy(src, dst, load_sems.at[k])
        for k, (src, dst) in enumerate((
            (land_h, land), (fields_h, fields), (target_h, target), (w_in_h, w_in),
            (w_out_h, w_out), (gain_h, gain), (offset_h, offset)))
    ]
    for load in loads:
        load.start()
    stores = [
        pltpu.make_async_copy(src, dst, store_sems.at[k])
        for k, (src, dst) in enumerate((
            (output, output_h), (grad_in, grad_in_h), (grad_out, grad_out_h),
            (gain_gradient, gain_gradient_h), (offset_gradient, offset_gradient_h)))
    ]

    barrier = pltpu.get_barrier_semaphore()

    def greet(k):
        peer = lax.rem(me + k, nd)
        pl.semaphore_signal(barrier, inc=1, device_id=device(peer // nb, lax.rem(peer, nb)),
                            device_id_type=pl.DeviceIdType.MESH)
    over(nd, greet)

    row_id = lax.broadcasted_iota(jnp.int32, (lat, ch), 0)
    zero_row = jnp.zeros((1, ch), F32)

    loads[0].wait()
    land_f = land[...].astype(F32)
    diagonal = lax.broadcasted_iota(jnp.int32, (lat, lat), 0) == lax.broadcasted_iota(
        jnp.int32, (lat, lat), 1)
    spread = jnp.concatenate(
        [jnp.where(diagonal, land_f[i:i + 1, :], 0.0) for i in range(lon)], axis=0)
    mask[...] = jnp.dot(spread.astype(BF16), jnp.ones((lat, ch), BF16), preferred_element_type=F32)

    def at(i):
        return pl.ds(pl.multiple_of(i * lat, lat), lat)

    def loop(start, stop, fn):
        def step(i, carry):
            fn(i)
            return carry
        lax.fori_loop(start, stop, step, 0)

    def shift_up(v, ghost):
        return jnp.concatenate([v[1:], ghost], axis=0)

    def shift_down(v):
        return jnp.concatenate([zero_row, v[:-1]], axis=0)

    def put(s, i, v, lane):
        s[i, :, lane * ch:(lane + 1) * ch] = v.astype(BF16)

    loads[1].wait()
    def base(s, i, v):
        put(s, i, shift_down(v), 0)
        put(s, i, v, 1)
        put(s, i, shift_up(v, zero_row), 2)

    def mask_lon(i):
        base(s_in, i + 1, fields[0, i].astype(F32) * mask[at(i)])
    loop(0, lon, mask_lon)
    heads[0] = s_in[1, :, ch:2 * ch]
    tails[0] = s_in[lon, :, ch:2 * ch]
    cols1 = col_copies(0)
    cols_t = col_copies(1)
    pl.semaphore_wait(barrier, nd - 1)
    for c in cols1:
        c.start()

    loads[2].wait()

    def mask_target(i):
        target[0, i] = (target[0, i].astype(F32) * mask[at(i)]).astype(BF16)
    loop(0, lon, mask_target)

    halves = []
    for h in range(2):
        half = mask[h * cells // 2:(h + 1) * cells // 2]
        halves.append(jnp.broadcast_to(jnp.sum(half, axis=0, keepdims=True), (8, ch)))
    rows1[z] = jnp.concatenate(
        [s_in[i + 1, lat - 16:, ch:2 * ch].astype(F32)[15:] for i in range(lon)]
        + [target[0, i, lat - 16:].astype(F32)[15:] for i in range(lon)] + halves, axis=0
    ).astype(BF16)
    heads[1] = target[0, 0]
    tails[1] = target[0, lon - 1]

    send_rows(0, rows1)
    for c in cols_t:
        c.start()

    for i in (0, lon + 1):
        s_in[i] = jnp.zeros((lat, 3 * ch), BF16)

    def window(s, f):
        return s[pl.ds(f, lon)].reshape(cells, 3 * ch)

    def conv_half(s, w, out, h, order=(0, 1, 2)):
        part_lon = lon // 2
        acc = jnp.zeros((part_lon * lat, ch), F32)
        for f in range(3):
            piece = s[pl.ds(h * part_lon + order[f], part_lon)].reshape(part_lon * lat, 3 * ch)
            acc += jnp.dot(piece, w[f], preferred_element_type=F32)
        out[pl.ds(pl.multiple_of(h * part_lon * lat, part_lon * lat), part_lon * lat)] = acc

    def conv(s, w, out, order=(0, 1, 2)):
        loop(0, 2, lambda h: conv_half(s, w, out, h, order))

    def fold_part(rows, w):
        acc = jnp.zeros((2 * lon, ch), F32)
        for f in range(3):
            piece = jnp.concatenate(rows[f:f + lon] + [jnp.zeros((lon, ch), F32)], axis=0)
            acc += jnp.dot(piece.astype(BF16), w[f, 2 * ch:3 * ch, :], preferred_element_type=F32)
        return acc

    def north(v, row):
        return v + jnp.where(row_id == lat - 1, row, 0.0)

    loads[3].wait()
    conv(s_in, w_in, first)
    for load in loads[4:]:
        load.wait()

    for c in cols1:
        c.wait_recv()
    recv_rows(0, rows1)

    opposite = nz - 1 - z
    beyond = lax.rem(nz - z, nz)
    before = lax.rem(2 * nz - 2 - z, nz)

    def ghosts(buf, start):
        facing = buf[opposite].astype(F32)
        left = buf[beyond].astype(F32)[start:start + 1]
        right = buf[before].astype(F32)[start + lon - 1:start + lon]
        return [left] + [facing[start + lon - 1 - i:start + lon - i] for i in range(lon)] + [right]

    ghost_in = ghosts(rows1, 0)
    for i, v in ((0, wests[0].astype(F32)), (lon + 1, easts[0].astype(F32))):
        put(s_in, i, shift_down(v), 0)
        put(s_in, i, v, 1)
        put(s_in, i, shift_up(v, ghost_in[i]), 2)
    from_west = jnp.dot(s_in[0], w_in[0], preferred_element_type=F32)
    from_east = jnp.dot(s_in[lon + 1], w_in[2], preferred_element_type=F32)
    fold[0] = fold_part([zero_row] + ghost_in[1:lon + 1] + [zero_row], w_in)
    for i in range(lon + 2):
        ghost_f[i] = ghost_in[i]
    first[at(0)] += from_west
    first[at(lon - 1)] += from_east

    def first_lon(i, sums):
        v = north(first[at(i)], fold[0, pl.ds(i, 1)])
        v = v.astype(BF16).astype(F32)
        first[at(i)] = v
        held = v * mask[at(i)]
        return sums[0] + held, sums[1] + held * v
    zeros = jnp.zeros((lat, ch), F32)
    sum_1, sum_2 = lax.fori_loop(0, lon, first_lon, (zeros, zeros))
    stats[0, me, 0:1] = jnp.sum(sum_1, axis=0, keepdims=True)
    stats[0, me, 1:2] = jnp.sum(sum_2, axis=0, keepdims=True)
    send_stats(0)

    def turn(f):
        for t in range(3):
            w = w_out[f, t * ch:(t + 1) * ch, :].astype(F32)
            w_back[f, t * ch:(t + 1) * ch, :] = w.T.astype(BF16)
    loop(0, 3, turn)

    count = zero_row
    for k in range(nz):
        packet = rows1[k].astype(F32)
        count = count + packet[16:17] + packet[24:25]
    count = count * float(nb)
    scale = lax.rsqrt(count)

    def scaled(v):
        return (v * scale).astype(BF16).astype(F32)

    for c in cols_t:
        c.wait_recv()
    def base_dout(i, v):
        put(s_dout, i, shift_up(v, zero_row), 0)
        put(s_dout, i, v, 1)
        put(s_dout, i, shift_down(v), 2)

    def lanes(k):
        return pl.ds(pl.multiple_of(k * 2 * lat, 2 * lat), 2 * lat)

    def dout_pair(k):
        pair = [scaled(target[0, 2 * k + t].astype(F32)) for t in range(2)]
        for t in range(2):
            base_dout(2 * k + t + 1, pair[t])
        dout_t[:, lanes(k)] = jnp.concatenate(pair, axis=0).T.astype(BF16)
    loop(0, lon // 2, dout_pair)
    base_dout(0, scaled(wests[1].astype(F32)))
    base_dout(lon + 1, scaled(easts[1].astype(F32)))
    ghost_dout = [scaled(v) for v in ghosts(rows1, lon)]
    north_d = [s_dout[i + 1, lat - 16:, ch:2 * ch].astype(F32)[15:] for i in range(lon)]
    north_t[...] = jnp.concatenate(
        north_d + [jnp.zeros((ch - lon, ch), F32)], axis=0).T.astype(BF16)
    conv(s_dout, w_back, dact, (2, 1, 0))
    fold[1] = fold_part(ghost_dout, w_back)

    def finish_lon(i):
        dact[at(i)] = north(dact[at(i)], fold[1, pl.ds(i, 1)]) * mask[at(i)]
        v = s_in[i + 1, :, ch:2 * ch].astype(F32)
        put(s_in, i + 1, shift_up(v, ghost_f[i + 1]), 2)
    loop(0, lon, finish_lon)

    acc = recv_stats(0)
    mean = acc[0:1] / count
    var = acc[1:2] / count - mean * mean
    inverse = lax.rsqrt(var + 1e-05)
    gains = gain[...]
    offsets = offset[...]

    def act_lon(i, sums):
        xhat = (first[at(i)] - mean) * inverse
        act, slope = gelu_parts(gains * xhat + offsets)
        d = dact[at(i)] * slope
        dpre[at(i)] = d
        base(s_act, i + 1, (act * mask[at(i)]).astype(BF16).astype(F32))
        return sums[0] + d, sums[1] + d * xhat
    sum_1, sum_2 = lax.fori_loop(0, lon, act_lon, (zeros, zeros))
    sum_off = jnp.sum(sum_1, axis=0, keepdims=True)
    sum_gain = jnp.sum(sum_2, axis=0, keepdims=True)
    stats[1, me, 0:1] = sum_off
    stats[1, me, 1:2] = sum_gain
    send_stats(1)
    heads[2] = s_act[1, :, ch:2 * ch]
    tails[2] = s_act[lon, :, ch:2 * ch]
    last = [s_act[i + 1, lat - 16:, ch:2 * ch].astype(F32)[15:] for i in range(lon)]
    rows2[z] = jnp.concatenate(last + [jnp.zeros((lon, ch), F32)], axis=0).astype(BF16)
    cols2 = col_copies(2)
    for c in cols2:
        c.start()
    send_rows(1, rows2)

    for i in (0, lon + 1):
        s_act[i] = jnp.zeros((lat, 3 * ch), BF16)

    def own_a(f):
        acc_a[f] = jnp.dot(dout_t[...], window(s_act, f), preferred_element_type=F32)
    loop(0, 3, own_a)

    for c in cols2:
        c.wait_recv()
    recv_rows(1, rows2)
    ghost_act = ghosts(rows2, 0)
    for i in range(lon + 2):
        ghost_a[i] = ghost_act[i]
    for i, v in ((0, wests[2].astype(F32)), (lon + 1, easts[2].astype(F32))):
        put(s_act, i, shift_down(v), 0)
        put(s_act, i, v, 1)
        put(s_act, i, shift_up(v, ghost_act[i]), 2)
    blank = jnp.zeros((lat, 3 * ch), BF16)
    acc_a[0] += jnp.dot(dout_t[:, 0:2 * lat], jnp.concatenate([s_act[0], blank], axis=0),
                        preferred_element_type=F32)
    acc_a[2] += jnp.dot(dout_t[:, cells - 2 * lat:],
                        jnp.concatenate([blank, s_act[lon + 1]], axis=0),
                        preferred_element_type=F32)
    inner = [zero_row] + ghost_act[1:lon + 1] + [zero_row]
    for f in range(3):
        piece = jnp.concatenate(inner[f:f + lon] + [jnp.zeros((ch - lon, ch), F32)], axis=0)
        acc_a[f, :, 2 * ch:] += jnp.dot(north_t[...], piece.astype(BF16),
                                        preferred_element_type=F32)

    share = ch // nb
    live = 9 * share
    padded = units * 16 * nz

    def rows_of(f):
        return pl.ds(pl.multiple_of(3 * f * share, 16), 3 * share)

    def pair_copy(which, f, part, pair):
        return copy(part.at[other, :, rows_of(f)], pair.at[:, rows_of(f)],
                    pair_sems.at[which, 0, f], pair_sems.at[which, 1, f], z, 2 * col + other)

    def cross_copy(which, f, half, cross, slot, peer, x):
        return copy(half.at[peer, rows_of(f)], cross.at[slot, rows_of(f)],
                    cross_sems.at[which, 0, f, peer], cross_sems.at[which, 1, f, slot],
                    z, 2 * x + core)

    def send_part(which, f, g, part, pair):
        for t in range(3):
            row = pl.ds(pl.multiple_of((3 * f + t) * share, 16), share)
            for k in range(nb):
                part[k % 2, k // 2, row, :] = (
                    g[k * share:(k + 1) * share, t * ch:(t + 1) * ch].astype(BF16))
        pair_copy(which, f, part, pair).start()

    def ring_copy(which, mine, ring, slot, peer):
        return copy(mine.at[peer], ring.at[slot], ring_sems.at[which, 0, peer],
                    ring_sems.at[which, 1, slot], peer, b)

    def full_copy(which, full, slot, peer):
        return copy(full.at[slot], full.at[slot], full_sems.at[which, 0, peer],
                    full_sems.at[which, 1, slot], peer, b)

    def after_pair(which, part, pair, half, cross):
        def one_f(f):
            pair_copy(which, f, part, pair).wait_recv()

            def summed(x):
                return (part[core, x, rows_of(f)].astype(F32)
                        + pair[x, rows_of(f)].astype(F32)).astype(BF16)

            def one(k):
                x = lax.rem(col + k, nx)
                half[x, rows_of(f)] = summed(x)
                cross_copy(which, f, half, cross, col, x, x).start()
            over(nx, one)
            half[col, rows_of(f)] = summed(col)
        loop(0, 3, one_f)

    def after_cross(which, half, cross, mine, ring):
        acc = half[col].astype(F32)
        for k in range(1, nx):
            x = lax.rem(col + k, nx)
            for f in range(3):
                cross_copy(which, f, half, cross, x, x, x).wait_recv()
            acc = acc + cross[x].astype(F32)
        if padded > live:
            acc = jnp.concatenate([acc, jnp.zeros((padded - live, ch), F32)], axis=0)
        for k in range(nz):
            mine[k] = acc[k * units * 16:(k + 1) * units * 16].astype(BF16)

        def one(k):
            peer = lax.rem(z + k, nz)
            ring_copy(which, mine, ring, z, peer).start()
        over(nz, one)

    def after_ring(which, mine, ring, full):
        acc = mine[z].astype(F32)
        for k in range(1, nz):
            src = lax.rem(z + k, nz)
            ring_copy(which, mine, ring, src, src).wait_recv()
            acc = acc + ring[src].astype(F32)
        full[z] = acc.astype(BF16)

        def one(k):
            full_copy(which, full, z, lax.rem(z + k, nz)).start()
        over(nz, one)

    def after_full(which, full, out):
        def one(k):
            src = lax.rem(z + k, nz)
            full_copy(which, full, src, src).wait_recv()
        over(nz, one)
        out[...] = full[...].reshape(padded, ch)[0:live].astype(F32)

    def drain(which, part, pair, half, cross, mine, ring, full):
        for f in range(3):
            pair_copy(which, f, part, pair).wait_send()

            def one_x(k):
                x = lax.rem(col + k, nx)
                cross_copy(which, f, half, cross, col, x, x).wait_send()
            over(nx, one_x)

        def one_z(k):
            peer = lax.rem(z + k, nz)
            ring_copy(which, mine, ring, z, peer).wait_send()
            full_copy(which, full, z, peer).wait_send()
        over(nz, one_z)

    loop(0, 3, lambda f: send_part(0, f, acc_a[f], part_a, pair_a))

    acc = recv_stats(1)
    off_total = acc[0:1]
    gain_total = acc[1:2]
    offset_gradient[...] = off_total
    gain_gradient[...] = gain_total
    stores[3].start()
    stores[4].start()
    scale_in = gains * inverse
    off_mean = off_total / count
    gain_mean = gain_total / count

    def dfirst_pair(k):
        pieces = []
        for j in (2 * k, 2 * k + 1):
            xhat = (first[at(j)] - mean) * inverse
            pieces.append(mask[at(j)] * scale_in * (dpre[at(j)] - (off_mean + xhat * gain_mean)))
        dout_t[:, lanes(k)] = jnp.concatenate(pieces, axis=0).T.astype(BF16)
    loop(0, lon // 2, dfirst_pair)
    after_pair(0, part_a, pair_a, half_a, cross_a)

    def tap_b(f):
        g = jnp.dot(dout_t[...], window(s_in, f), preferred_element_type=F32)
        send_part(1, f, g, part_b, pair_b)
    loop(0, 3, tap_b)

    def finish_act(i):
        v = s_act[i + 1, :, ch:2 * ch].astype(F32)
        put(s_act, i + 1, shift_up(v, ghost_a[i + 1]), 2)
    loop(0, lon, finish_act)
    after_pair(1, part_b, pair_b, half_b, cross_b)
    conv_half(s_act, w_out, dact, 0)
    after_cross(0, half_a, cross_a, mine_a, ring_a)
    conv_half(s_act, w_out, dact, 1)
    after_cross(1, half_b, cross_b, mine_b, ring_b)

    def out_lon(i):
        output[0, i] = (dact[at(i)] * mask[at(i)]).astype(BF16)
    loop(0, lon, out_lon)
    stores[0].start()
    after_ring(0, mine_a, ring_a, full_a)
    after_ring(1, mine_b, ring_b, full_b)
    after_full(0, full_a, grad_out)
    stores[2].start()
    after_full(1, full_b, grad_in)
    stores[1].start()

    for c in cols1 + cols_t + cols2:
        c.wait_send()
    drain_rows(0, rows1)
    drain_rows(1, rows2)
    drain_stats(0)
    drain_stats(1)
    drain(0, part_a, pair_a, half_a, cross_a, mine_a, ring_a, full_a)
    drain(1, part_b, pair_b, half_b, cross_b, mine_b, ring_b, full_b)
    for store in stores:
        store.wait()


def writer(*refs):
    sources, results, held, sems = refs[:5], refs[5:10], refs[10:15], refs[15]
    loads = [pltpu.make_async_copy(sources[k], held[k], sems.at[0, k]) for k in range(5)]
    stores = [pltpu.make_async_copy(held[k], results[k], sems.at[1, k]) for k in range(5)]
    for c in loads:
        c.start()
    for load, store in zip(loads, stores):
        load.wait()
        store.start()
    for c in stores:
        c.wait()


def body(nz, nb, fields, land, conv_in, conv_out, gain, offset, target):
    lon, lat, ch = fields.shape[1:]
    nd = nz * nb
    nx = nb // 2
    share = ch // nb
    units = -(-(9 * share // 16) // nz)
    padded = units * 16 * nz
    vm = pltpu.VMEM
    reduction = [
        vm((2, nx, 9 * share, ch), BF16),
        vm((nx, 9 * share, ch), BF16),
        vm((nx, 9 * share, ch), BF16),
        vm((nx, 9 * share, ch), BF16),
        vm((nz, units * 16, ch), BF16),
        vm((nz, units * 16, ch), BF16),
        vm((nz, units * 16, ch), BF16),
    ]
    dma = pltpu.SemaphoreType.DMA
    scratch = [
        vm(fields.shape, BF16),
        vm((9 * share, ch), F32),
        vm((9 * share, ch), F32),
        vm((1, ch), F32),
        vm((1, ch), F32),
        vm(fields.shape, BF16),
        vm(land.shape, jnp.int32),
        vm((3, 3 * ch, ch), BF16),
        vm((3, 3 * ch, ch), BF16),
        vm((1, ch), F32),
        vm((1, ch), F32),
        vm(target.shape, BF16),
        vm((lon * lat, ch), F32),
        vm((lon * lat, ch), F32),
        vm((lon * lat, ch), F32),
        vm((lon * lat, ch), F32),
        vm((lon + 2, lat, 3 * ch), BF16),
        vm((lon + 2, lat, 3 * ch), BF16),
        vm((lon + 2, lat, 3 * ch), BF16),
        vm((3, 3 * ch, ch), BF16),
        vm((ch, lon * lat), BF16),
        vm((nz, 32, ch), BF16),
        vm((nz, 16, ch), BF16),
        vm((3, lat, ch), BF16), vm((3, lat, ch), BF16),
        vm((3, lat, ch), BF16), vm((3, lat, ch), BF16),
        vm((2, nd, 2, ch), F32),
        vm((lon + 2, 1, ch), F32),
        vm((lon + 2, 1, ch), F32),
        vm((lon + 2, 1, ch), F32),
        vm((2, 2 * lon, ch), F32),
        vm((3, ch, 3 * ch), F32),
        vm((ch, ch), BF16),
        *reduction,
        *reduction,
        dma((7,)),
        dma((5,)),
        dma((2, 2, nz)),
        dma((3, 2, 2)),
        dma((2, 2, nd)),
        dma((2, 2, 3)),
        dma((2, 2, 3, nx)),
        dma((2, 2, nz)),
        dma((2, 2, nz)),
    ]
    anywhere = pl.BlockSpec(memory_space=pl.ANY)
    limit = 62 * 1024 * 1024
    results = pl.pallas_call(
        functools.partial(kernel, nz, nb, lon, lat, ch, units),
        out_shape=(
            jax.ShapeDtypeStruct(fields.shape, BF16),
            jax.ShapeDtypeStruct((9 * share, ch), F32),
            jax.ShapeDtypeStruct((9 * share, ch), F32),
            jax.ShapeDtypeStruct((1, ch), F32),
            jax.ShapeDtypeStruct((1, ch), F32),
        ),
        in_specs=[anywhere] * 7,
        out_specs=(anywhere,) * 5,
        scratch_shapes=scratch,
        compiler_params=pltpu.CompilerParams(
            collective_id=0, has_side_effects=True, vmem_limit_bytes=limit
        ),
    )(
        fields, land,
        conv_in.reshape(3, 3 * ch, ch), conv_out.reshape(3, 3 * ch, ch),
        gain.reshape(1, ch), offset.reshape(1, ch), target,
    )

    out, grad_in, grad_out, gain_gradient, offset_gradient = pl.pallas_call(
        writer,
        out_shape=tuple(jax.ShapeDtypeStruct(r.shape, r.dtype) for r in results),
        in_specs=[anywhere] * 5,
        out_specs=(anywhere,) * 5,
        scratch_shapes=[vm(r.shape, r.dtype) for r in results] + [dma((2, 5))],
        compiler_params=pltpu.CompilerParams(vmem_limit_bytes=limit),
    )(*results)

    def taps(g):
        return g.reshape(9, share, ch).transpose(0, 2, 1)

    return (out, taps(grad_in), taps(grad_out),
            gain_gradient.reshape(ch), offset_gradient.reshape(ch))


def solution(mesh):
    in_specs = (
        P(("groups", "batch"), "space", None, None),
        P("space", None),
        P(),
        P(),
        P(),
        P(),
        P(("groups", "batch"), "space", None, None),
    )
    out_specs = (
        P(("groups", "batch"), "space", None, None),
        P("groups", None, "batch"),
        P("groups", None, "batch"),
        P("groups"),
        P("groups"),
    )
    step = functools.partial(body, mesh.shape["space"], mesh.shape["batch"])
    return jax.shard_map(step, mesh=mesh, in_specs=in_specs, out_specs=out_specs, check_vma=False)
```

```python
import functools

import jax
import jax.numpy as jnp
from jax import lax
from jax.experimental import pallas as pl
from jax.experimental.pallas import tpu as pltpu
from jax.sharding import PartitionSpec as P

F32 = jnp.float32
BF16 = jnp.bfloat16


def gelu_parts(value):
    inner = 0.7978845608 * (value + 0.044715 * value * value * value)
    hyper = jnp.tanh(inner)
    act = 0.5 * value * (1.0 + hyper)
    slope = 0.5 * (1.0 + hyper) + 0.5 * value * (1.0 - hyper * hyper) * 0.7978845608 * (
        1.0 + 3.0 * 0.044715 * value * value
    )
    return act, slope


def kernel(
    nz, nb, lon, lat, ch, depth,
    fields_h, land_h, w_in_h, w_out_h, gain_h, offset_h, target_h,
    output_h, grad_in_h, grad_out_h, gain_gradient_h, offset_gradient_h,
    output, grad_in, grad_out, gain_gradient, offset_gradient,
    fields, land, w_in, w_out, gain, offset, target,
    mask, first, dact, dpre, s_in, s_act, s_dout, w_back, dout_t,
    rows1, rows2, heads, tails, wests, easts,
    stats, ghost_f, ghost_d, ghost_a, fold,
    acc_a, north_t,
    part_a, pair_a, half_a, cross_a, mine_a, next_a, ring_a, full_a,
    part_b, pair_b, half_b, cross_b, mine_b, next_b, ring_b, full_b,
    load_sems, store_sems, row_sems, col_sems, stat_sems, pair_sems, cross_sems, next_sems, ring_sems, full_sems,
):
    nd = nz * nb
    nx = nb // 2
    cells = lon * lat
    z = lax.axis_index("space")
    b = lax.axis_index("batch")
    me = z * nb + b
    core = lax.rem(b, 2)
    col = b // 2
    other = 1 - core
    nh = nz // 2
    side = lax.rem(z, 2)
    duo = z // 2
    facing_z = 2 * duo + 1 - side

    def device(zz, bb):
        return {"space": zz, "batch": bb}

    def copy(src, dst, send, recv, zz, bb):
        return pltpu.make_async_remote_copy(
            src_ref=src, dst_ref=dst, send_sem=send, recv_sem=recv,
            device_id=device(zz, bb), device_id_type=pl.DeviceIdType.MESH,
        )

    def over(count, fn):
        if count <= 4:
            for k in range(1, count):
                fn(k)
            return

        def step(k, carry):
            fn(k)
            return carry
        lax.fori_loop(1, count, step, 0)

    def row_copy(which, buf, slot, zz):
        return copy(buf.at[slot], buf.at[slot], row_sems.at[which, 0, zz],
                    row_sems.at[which, 1, slot], zz, b)

    def send_rows(which, buf):
        over(nz, lambda k: row_copy(which, buf, z, lax.rem(z + k, nz)).start())

    def recv_rows(which, buf):
        def one(k):
            src = lax.rem(z + k, nz)
            row_copy(which, buf, src, src).wait_recv()
        over(nz, one)

    def drain_rows(which, buf):
        over(nz, lambda k: row_copy(which, buf, z, lax.rem(z + k, nz)).wait_send())

    up = lax.rem(z + 1, nz)
    down = lax.rem(z + nz - 1, nz)

    def col_copies(which):
        return (
            copy(heads.at[which], easts.at[which], col_sems.at[which, 0, 0], col_sems.at[which, 1, 0], down, b),
            copy(tails.at[which], wests.at[which], col_sems.at[which, 0, 1], col_sems.at[which, 1, 1], up, b),
        )

    def stat_copy(which, slot, peer):
        return copy(stats.at[which, slot], stats.at[which, slot], stat_sems.at[which, 0, peer],
                    stat_sems.at[which, 1, slot], peer // nb, lax.rem(peer, nb))

    def send_stats(which):
        over(nd, lambda k: stat_copy(which, me, lax.rem(me + k, nd)).start())

    def recv_stats(which):
        def one(k):
            src = lax.rem(me + k, nd)
            stat_copy(which, src, src).wait_recv()
        over(nd, one)
        acc = stats[which, 0]
        for k in range(1, nd):
            acc = acc + stats[which, k]
        return acc

    def drain_stats(which):
        over(nd, lambda k: stat_copy(which, me, lax.rem(me + k, nd)).wait_send())

    loads = [
        pltpu.make_async_copy(src, dst, load_sems.at[k])
        for k, (src, dst) in enumerate((
            (land_h, land), (fields_h, fields), (target_h, target), (w_in_h, w_in),
            (w_out_h, w_out), (gain_h, gain), (offset_h, offset)))
    ]
    for load in loads:
        load.start()
    stores = [
        pltpu.make_async_copy(src, dst, store_sems.at[k])
        for k, (src, dst) in enumerate((
            (output, output_h), (grad_in, grad_in_h), (grad_out, grad_out_h),
            (gain_gradient, gain_gradient_h), (offset_gradient, offset_gradient_h)))
    ]

    barrier = pltpu.get_barrier_semaphore()

    def greet(k):
        peer = lax.rem(me + k, nd)
        pl.semaphore_signal(barrier, inc=1, device_id=device(peer // nb, lax.rem(peer, nb)),
                            device_id_type=pl.DeviceIdType.MESH)
    over(nd, greet)

    row_id = lax.broadcasted_iota(jnp.int32, (lat, ch), 0)
    zero_row = jnp.zeros((1, ch), F32)

    loads[0].wait()
    land_f = land[...].astype(F32)
    diagonal = lax.broadcasted_iota(jnp.int32, (lat, lat), 0) == lax.broadcasted_iota(
        jnp.int32, (lat, lat), 1)
    spread = jnp.concatenate(
        [jnp.where(diagonal, land_f[i:i + 1, :], 0.0) for i in range(lon)], axis=0)
    mask[...] = jnp.dot(spread.astype(BF16), jnp.ones((lat, ch), BF16), preferred_element_type=F32)

    def at(i):
        return pl.ds(pl.multiple_of(i * lat, lat), lat)

    def loop(start, stop, fn):
        def step(i, carry):
            fn(i)
            return carry
        lax.fori_loop(start, stop, step, 0)

    def shift_up(v, ghost):
        return jnp.concatenate([v[1:], ghost], axis=0)

    def shift_down(v):
        return jnp.concatenate([zero_row, v[:-1]], axis=0)

    def put(s, i, v, lane):
        s[i, :, lane * ch:(lane + 1) * ch] = v.astype(BF16)

    loads[1].wait()
    def base(s, i, v):
        put(s, i, shift_down(v), 0)
        put(s, i, v, 1)
        put(s, i, shift_up(v, zero_row), 2)

    def mask_lon(i):
        base(s_in, i + 1, fields[0, i].astype(F32) * mask[at(i)])
    loop(0, lon, mask_lon)
    heads[0] = s_in[1, :, ch:2 * ch]
    tails[0] = s_in[lon, :, ch:2 * ch]
    cols1 = col_copies(0)
    cols_t = col_copies(1)
    pl.semaphore_wait(barrier, nd - 1)
    for c in cols1:
        c.start()

    loads[2].wait()

    def mask_target(i):
        target[0, i] = (target[0, i].astype(F32) * mask[at(i)]).astype(BF16)
    loop(0, lon, mask_target)

    halves = []
    for h in range(2):
        half = mask[h * cells // 2:(h + 1) * cells // 2]
        halves.append(jnp.broadcast_to(jnp.sum(half, axis=0, keepdims=True), (8, ch)))
    rows1[z] = jnp.concatenate(
        [s_in[i + 1, lat - 16:, ch:2 * ch].astype(F32)[15:] for i in range(lon)]
        + [target[0, i, lat - 16:].astype(F32)[15:] for i in range(lon)] + halves, axis=0
    ).astype(BF16)
    heads[1] = target[0, 0]
    tails[1] = target[0, lon - 1]

    send_rows(0, rows1)
    for c in cols_t:
        c.start()

    for i in (0, lon + 1):
        s_in[i] = jnp.zeros((lat, 3 * ch), BF16)

    def window(s, f):
        return s[pl.ds(f, lon)].reshape(cells, 3 * ch)

    def conv_half(s, w, out, h, order=(0, 1, 2)):
        part_lon = lon // 2
        acc = jnp.zeros((part_lon * lat, ch), F32)
        for f in range(3):
            piece = s[pl.ds(h * part_lon + order[f], part_lon)].reshape(part_lon * lat, 3 * ch)
            acc += jnp.dot(piece, w[f], preferred_element_type=F32)
        out[pl.ds(pl.multiple_of(h * part_lon * lat, part_lon * lat), part_lon * lat)] = acc

    def conv(s, w, out, order=(0, 1, 2)):
        loop(0, 2, lambda h: conv_half(s, w, out, h, order))

    def fold_part(rows, w):
        acc = jnp.zeros((2 * lon, ch), F32)
        for f in range(3):
            piece = jnp.concatenate(rows[f:f + lon] + [jnp.zeros((lon, ch), F32)], axis=0)
            acc += jnp.dot(piece.astype(BF16), w[f, 2 * ch:3 * ch, :], preferred_element_type=F32)
        return acc

    def north(v, row):
        return v + jnp.where(row_id == lat - 1, row, 0.0)

    loads[3].wait()
    conv(s_in, w_in, first)
    for load in loads[4:]:
        load.wait()

    for c in cols1:
        c.wait_recv()
    recv_rows(0, rows1)

    opposite = nz - 1 - z
    beyond = lax.rem(nz - z, nz)
    before = lax.rem(2 * nz - 2 - z, nz)

    def ghosts(buf, start):
        facing = buf[opposite].astype(F32)
        left = buf[beyond].astype(F32)[start:start + 1]
        right = buf[before].astype(F32)[start + lon - 1:start + lon]
        return [left] + [facing[start + lon - 1 - i:start + lon - i] for i in range(lon)] + [right]

    ghost_in = ghosts(rows1, 0)
    for i, v in ((0, wests[0].astype(F32)), (lon + 1, easts[0].astype(F32))):
        put(s_in, i, shift_down(v), 0)
        put(s_in, i, v, 1)
        put(s_in, i, shift_up(v, ghost_in[i]), 2)
    from_west = jnp.dot(s_in[0], w_in[0], preferred_element_type=F32)
    from_east = jnp.dot(s_in[lon + 1], w_in[2], preferred_element_type=F32)
    fold[0] = fold_part([zero_row] + ghost_in[1:lon + 1] + [zero_row], w_in)
    for i in range(lon + 2):
        ghost_f[i] = ghost_in[i]
    first[at(0)] += from_west
    first[at(lon - 1)] += from_east

    def first_lon(i, sums):
        v = north(first[at(i)], fold[0, pl.ds(i, 1)])
        v = v.astype(BF16).astype(F32)
        first[at(i)] = v
        held = v * mask[at(i)]
        return sums[0] + held, sums[1] + held * v
    zeros = jnp.zeros((lat, ch), F32)
    sum_1, sum_2 = lax.fori_loop(0, lon, first_lon, (zeros, zeros))
    stats[0, me, 0:1] = jnp.sum(sum_1, axis=0, keepdims=True)
    stats[0, me, 1:2] = jnp.sum(sum_2, axis=0, keepdims=True)
    send_stats(0)

    def turn(f):
        for t in range(3):
            w = w_out[f, t * ch:(t + 1) * ch, :].astype(F32)
            w_back[f, t * ch:(t + 1) * ch, :] = w.T.astype(BF16)
    loop(0, 3, turn)

    count = zero_row
    for k in range(nz):
        packet = rows1[k].astype(F32)
        count = count + packet[16:17] + packet[24:25]
    count = count * float(nb)
    scale = lax.rsqrt(count)

    def scaled(v):
        return (v * scale).astype(BF16).astype(F32)

    for c in cols_t:
        c.wait_recv()
    def base_dout(i, v):
        put(s_dout, i, shift_up(v, zero_row), 0)
        put(s_dout, i, v, 1)
        put(s_dout, i, shift_down(v), 2)

    def lanes(k):
        return pl.ds(pl.multiple_of(k * 2 * lat, 2 * lat), 2 * lat)

    def dout_pair(k):
        pair = [scaled(target[0, 2 * k + t].astype(F32)) for t in range(2)]
        for t in range(2):
            base_dout(2 * k + t + 1, pair[t])
        dout_t[:, lanes(k)] = jnp.concatenate(pair, axis=0).T.astype(BF16)
    loop(0, lon // 2, dout_pair)
    base_dout(0, scaled(wests[1].astype(F32)))
    base_dout(lon + 1, scaled(easts[1].astype(F32)))
    ghost_dout = [scaled(v) for v in ghosts(rows1, lon)]
    north_d = [s_dout[i + 1, lat - 16:, ch:2 * ch].astype(F32)[15:] for i in range(lon)]
    north_t[...] = jnp.concatenate(
        north_d + [jnp.zeros((ch - lon, ch), F32)], axis=0).T.astype(BF16)
    conv(s_dout, w_back, dact, (2, 1, 0))
    fold[1] = fold_part(ghost_dout, w_back)

    def finish_lon(i):
        dact[at(i)] = north(dact[at(i)], fold[1, pl.ds(i, 1)]) * mask[at(i)]
        v = s_in[i + 1, :, ch:2 * ch].astype(F32)
        put(s_in, i + 1, shift_up(v, ghost_f[i + 1]), 2)
    loop(0, lon, finish_lon)

    acc = recv_stats(0)
    mean = acc[0:1] / count
    var = acc[1:2] / count - mean * mean
    inverse = lax.rsqrt(var + 1e-05)
    gains = gain[...]
    offsets = offset[...]

    def act_lon(i, sums):
        xhat = (first[at(i)] - mean) * inverse
        act, slope = gelu_parts(gains * xhat + offsets)
        d = dact[at(i)] * slope
        dpre[at(i)] = d
        base(s_act, i + 1, (act * mask[at(i)]).astype(BF16).astype(F32))
        return sums[0] + d, sums[1] + d * xhat
    sum_1, sum_2 = lax.fori_loop(0, lon, act_lon, (zeros, zeros))
    sum_off = jnp.sum(sum_1, axis=0, keepdims=True)
    sum_gain = jnp.sum(sum_2, axis=0, keepdims=True)
    stats[1, me, 0:1] = sum_off
    stats[1, me, 1:2] = sum_gain
    send_stats(1)
    heads[2] = s_act[1, :, ch:2 * ch]
    tails[2] = s_act[lon, :, ch:2 * ch]
    last = [s_act[i + 1, lat - 16:, ch:2 * ch].astype(F32)[15:] for i in range(lon)]
    rows2[z] = jnp.concatenate(last + [jnp.zeros((lon, ch), F32)], axis=0).astype(BF16)
    cols2 = col_copies(2)
    for c in cols2:
        c.start()
    send_rows(1, rows2)

    for i in (0, lon + 1):
        s_act[i] = jnp.zeros((lat, 3 * ch), BF16)

    def own_a(f):
        acc_a[f] = jnp.dot(dout_t[...], window(s_act, f), preferred_element_type=F32)
    loop(0, 3, own_a)

    for c in cols2:
        c.wait_recv()
    recv_rows(1, rows2)
    ghost_act = ghosts(rows2, 0)
    for i in range(lon + 2):
        ghost_a[i] = ghost_act[i]
    for i, v in ((0, wests[2].astype(F32)), (lon + 1, easts[2].astype(F32))):
        put(s_act, i, shift_down(v), 0)
        put(s_act, i, v, 1)
        put(s_act, i, shift_up(v, ghost_act[i]), 2)
    blank = jnp.zeros((lat, 3 * ch), BF16)
    acc_a[0] += jnp.dot(dout_t[:, 0:2 * lat], jnp.concatenate([s_act[0], blank], axis=0),
                        preferred_element_type=F32)
    acc_a[2] += jnp.dot(dout_t[:, cells - 2 * lat:],
                        jnp.concatenate([blank, s_act[lon + 1]], axis=0),
                        preferred_element_type=F32)
    inner = [zero_row] + ghost_act[1:lon + 1] + [zero_row]
    for f in range(3):
        piece = jnp.concatenate(inner[f:f + lon] + [jnp.zeros((ch - lon, ch), F32)], axis=0)
        acc_a[f, :, 2 * ch:] += jnp.dot(north_t[...], piece.astype(BF16),
                                        preferred_element_type=F32)

    share = ch // nb
    live = 9 * share
    padded = 2 * depth

    def rows_of(f):
        return pl.ds(pl.multiple_of(3 * f * share, 16), 3 * share)

    def pair_copy(which, f, part, pair):
        return copy(part.at[other, :, rows_of(f)], pair.at[:, rows_of(f)],
                    pair_sems.at[which, 0, f], pair_sems.at[which, 1, f], z, 2 * col + other)

    def cross_copy(which, f, half, cross, slot, peer, x):
        return copy(half.at[peer, rows_of(f)], cross.at[slot, rows_of(f)],
                    cross_sems.at[which, 0, f, peer], cross_sems.at[which, 1, f, slot],
                    z, 2 * x + core)

    def send_part(which, f, g, part, pair):
        for t in range(3):
            row = pl.ds(pl.multiple_of((3 * f + t) * share, 16), share)
            for k in range(nb):
                part[k % 2, k // 2, row, :] = (
                    g[k * share:(k + 1) * share, t * ch:(t + 1) * ch].astype(BF16))
        pair_copy(which, f, part, pair).start()

    def next_copy(which, mine, near):
        return copy(mine.at[1 - side], near, next_sems.at[which, 0], next_sems.at[which, 1],
                    facing_z, b)

    def ring_copy(which, ring, slot, peer):
        return copy(ring.at[slot], ring.at[slot], ring_sems.at[which, 0, peer],
                    ring_sems.at[which, 1, slot], 2 * peer + side, b)

    def full_copy(which, full, half):
        return copy(full.at[half], full.at[half], full_sems.at[which, 0], full_sems.at[which, 1],
                    facing_z, b)

    def after_pair(which, part, pair, half, cross):
        def one_f(f):
            pair_copy(which, f, part, pair).wait_recv()

            def summed(x):
                return (part[core, x, rows_of(f)].astype(F32)
                        + pair[x, rows_of(f)].astype(F32)).astype(BF16)

            def one(k):
                x = lax.rem(col + k, nx)
                half[x, rows_of(f)] = summed(x)
                cross_copy(which, f, half, cross, col, x, x).start()
            over(nx, one)
            half[col, rows_of(f)] = summed(col)
        loop(0, 3, one_f)

    def after_cross(which, half, cross, mine, near):
        acc = half[col].astype(F32)
        for k in range(1, nx):
            x = lax.rem(col + k, nx)
            for f in range(3):
                cross_copy(which, f, half, cross, x, x, x).wait_recv()
            acc = acc + cross[x].astype(F32)
        if padded > live:
            acc = jnp.concatenate([acc, jnp.zeros((padded - live, ch), F32)], axis=0)
        for k in range(2):
            mine[k] = acc[k * depth:(k + 1) * depth].astype(BF16)
        next_copy(which, mine, near).start()

    def after_next(which, mine, near, ring):
        next_copy(which, mine, near).wait_recv()
        ring[duo] = (mine[side].astype(F32) + near[...].astype(F32)).astype(BF16)
        over(nh, lambda k: ring_copy(which, ring, duo, lax.rem(duo + k, nh)).start())

    def after_ring(which, ring, full):
        def one(k):
            src = lax.rem(duo + k, nh)
            ring_copy(which, ring, src, src).wait_recv()
        over(nh, one)
        acc = ring[0].astype(F32)
        for k in range(1, nh):
            acc = acc + ring[k].astype(F32)
        full[side] = acc.astype(BF16)
        full_copy(which, full, side).start()

    def after_full(which, full, out):
        full_copy(which, full, 1 - side).wait_recv()
        out[...] = full[...].reshape(padded, ch)[0:live].astype(F32)

    def drain(which, part, pair, half, cross, mine, near, ring, full):
        for f in range(3):
            pair_copy(which, f, part, pair).wait_send()

            def one_x(k):
                x = lax.rem(col + k, nx)
                cross_copy(which, f, half, cross, col, x, x).wait_send()
            over(nx, one_x)

        next_copy(which, mine, near).wait_send()
        over(nh, lambda k: ring_copy(which, ring, duo, lax.rem(duo + k, nh)).wait_send())
        full_copy(which, full, side).wait_send()

    loop(0, 3, lambda f: send_part(0, f, acc_a[f], part_a, pair_a))

    acc = recv_stats(1)
    off_total = acc[0:1]
    gain_total = acc[1:2]
    offset_gradient[...] = off_total
    gain_gradient[...] = gain_total
    stores[3].start()
    stores[4].start()
    scale_in = gains * inverse
    off_mean = off_total / count
    gain_mean = gain_total / count

    def dfirst_pair(k):
        pieces = []
        for j in (2 * k, 2 * k + 1):
            xhat = (first[at(j)] - mean) * inverse
            pieces.append(mask[at(j)] * scale_in * (dpre[at(j)] - (off_mean + xhat * gain_mean)))
        dout_t[:, lanes(k)] = jnp.concatenate(pieces, axis=0).T.astype(BF16)
    loop(0, lon // 2, dfirst_pair)
    after_pair(0, part_a, pair_a, half_a, cross_a)

    def tap_b(f):
        g = jnp.dot(dout_t[...], window(s_in, f), preferred_element_type=F32)
        send_part(1, f, g, part_b, pair_b)
    loop(0, 3, tap_b)

    def finish_act(i):
        v = s_act[i + 1, :, ch:2 * ch].astype(F32)
        put(s_act, i + 1, shift_up(v, ghost_a[i + 1]), 2)
    loop(0, lon, finish_act)
    after_pair(1, part_b, pair_b, half_b, cross_b)
    conv_half(s_act, w_out, dact, 0)
    after_cross(0, half_a, cross_a, mine_a, next_a)
    conv_half(s_act, w_out, dact, 1)
    after_cross(1, half_b, cross_b, mine_b, next_b)

    def out_lon(i):
        output[0, i] = (dact[at(i)] * mask[at(i)]).astype(BF16)
    loop(0, lon, out_lon)
    stores[0].start()
    after_next(0, mine_a, next_a, ring_a)
    after_next(1, mine_b, next_b, ring_b)
    after_ring(0, ring_a, full_a)
    after_ring(1, ring_b, full_b)
    after_full(0, full_a, grad_out)
    stores[2].start()
    after_full(1, full_b, grad_in)
    stores[1].start()

    for c in cols1 + cols_t + cols2:
        c.wait_send()
    drain_rows(0, rows1)
    drain_rows(1, rows2)
    drain_stats(0)
    drain_stats(1)
    drain(0, part_a, pair_a, half_a, cross_a, mine_a, next_a, ring_a, full_a)
    drain(1, part_b, pair_b, half_b, cross_b, mine_b, next_b, ring_b, full_b)
    for store in stores:
        store.wait()


def writer(*refs):
    sources, results, held, sems = refs[:5], refs[5:10], refs[10:15], refs[15]
    loads = [pltpu.make_async_copy(sources[k], held[k], sems.at[0, k]) for k in range(5)]
    stores = [pltpu.make_async_copy(held[k], results[k], sems.at[1, k]) for k in range(5)]
    for c in loads:
        c.start()
    for load, store in zip(loads, stores):
        load.wait()
        store.start()
    for c in stores:
        c.wait()


def body(nz, nb, fields, land, conv_in, conv_out, gain, offset, target):
    lon, lat, ch = fields.shape[1:]
    nd = nz * nb
    nx = nb // 2
    share = ch // nb
    depth = -(-9 * share // 32) * 16
    vm = pltpu.VMEM
    reduction = [
        vm((2, nx, 9 * share, ch), BF16),
        vm((nx, 9 * share, ch), BF16),
        vm((nx, 9 * share, ch), BF16),
        vm((nx, 9 * share, ch), BF16),
        vm((2, depth, ch), BF16),
        vm((depth, ch), BF16),
        vm((nz // 2, depth, ch), BF16),
        vm((2, depth, ch), BF16),
    ]
    dma = pltpu.SemaphoreType.DMA
    scratch = [
        vm(fields.shape, BF16),
        vm((9 * share, ch), F32),
        vm((9 * share, ch), F32),
        vm((1, ch), F32),
        vm((1, ch), F32),
        vm(fields.shape, BF16),
        vm(land.shape, jnp.int32),
        vm((3, 3 * ch, ch), BF16),
        vm((3, 3 * ch, ch), BF16),
        vm((1, ch), F32),
        vm((1, ch), F32),
        vm(target.shape, BF16),
        vm((lon * lat, ch), F32),
        vm((lon * lat, ch), F32),
        vm((lon * lat, ch), F32),
        vm((lon * lat, ch), F32),
        vm((lon + 2, lat, 3 * ch), BF16),
        vm((lon + 2, lat, 3 * ch), BF16),
        vm((lon + 2, lat, 3 * ch), BF16),
        vm((3, 3 * ch, ch), BF16),
        vm((ch, lon * lat), BF16),
        vm((nz, 32, ch), BF16),
        vm((nz, 16, ch), BF16),
        vm((3, lat, ch), BF16), vm((3, lat, ch), BF16),
        vm((3, lat, ch), BF16), vm((3, lat, ch), BF16),
        vm((2, nd, 2, ch), F32),
        vm((lon + 2, 1, ch), F32),
        vm((lon + 2, 1, ch), F32),
        vm((lon + 2, 1, ch), F32),
        vm((2, 2 * lon, ch), F32),
        vm((3, ch, 3 * ch), F32),
        vm((ch, ch), BF16),
        *reduction,
        *reduction,
        dma((7,)),
        dma((5,)),
        dma((2, 2, nz)),
        dma((3, 2, 2)),
        dma((2, 2, nd)),
        dma((2, 2, 3)),
        dma((2, 2, 3, nx)),
        dma((2, 2)),
        dma((2, 2, nz // 2)),
        dma((2, 2)),
    ]
    anywhere = pl.BlockSpec(memory_space=pl.ANY)
    limit = 62 * 1024 * 1024
    results = pl.pallas_call(
        functools.partial(kernel, nz, nb, lon, lat, ch, depth),
        out_shape=(
            jax.ShapeDtypeStruct(fields.shape, BF16),
            jax.ShapeDtypeStruct((9 * share, ch), F32),
            jax.ShapeDtypeStruct((9 * share, ch), F32),
            jax.ShapeDtypeStruct((1, ch), F32),
            jax.ShapeDtypeStruct((1, ch), F32),
        ),
        in_specs=[anywhere] * 7,
        out_specs=(anywhere,) * 5,
        scratch_shapes=scratch,
        compiler_params=pltpu.CompilerParams(
            collective_id=0, has_side_effects=True, vmem_limit_bytes=limit
        ),
    )(
        fields, land,
        conv_in.reshape(3, 3 * ch, ch), conv_out.reshape(3, 3 * ch, ch),
        gain.reshape(1, ch), offset.reshape(1, ch), target,
    )

    out, grad_in, grad_out, gain_gradient, offset_gradient = pl.pallas_call(
        writer,
        out_shape=tuple(jax.ShapeDtypeStruct(r.shape, r.dtype) for r in results),
        in_specs=[anywhere] * 5,
        out_specs=(anywhere,) * 5,
        scratch_shapes=[vm(r.shape, r.dtype) for r in results] + [dma((2, 5))],
        compiler_params=pltpu.CompilerParams(vmem_limit_bytes=limit),
    )(*results)

    def taps(g):
        return g.reshape(9, share, ch).transpose(0, 2, 1)

    return (out, taps(grad_in), taps(grad_out),
            gain_gradient.reshape(ch), offset_gradient.reshape(ch))


def solution(mesh):
    in_specs = (
        P(("groups", "batch"), "space", None, None),
        P("space", None),
        P(),
        P(),
        P(),
        P(),
        P(("groups", "batch"), "space", None, None),
    )
    out_specs = (
        P(("groups", "batch"), "space", None, None),
        P("groups", None, "batch"),
        P("groups", None, "batch"),
        P("groups"),
        P("groups"),
    )
    step = functools.partial(body, mesh.shape["space"], mesh.shape["batch"])
    return jax.shard_map(step, mesh=mesh, in_specs=in_specs, out_specs=out_specs, check_vma=False)
```

```python
import functools

import jax
import jax.numpy as jnp
from jax import lax
from jax.experimental import pallas as pl
from jax.experimental.pallas import tpu as pltpu
from jax.sharding import PartitionSpec as P

F32 = jnp.float32
BF16 = jnp.bfloat16


def gelu_parts(value):
    inner = 0.7978845608 * (value + 0.044715 * value * value * value)
    hyper = jnp.tanh(inner)
    act = 0.5 * value * (1.0 + hyper)
    slope = 0.5 * (1.0 + hyper) + 0.5 * value * (1.0 - hyper * hyper) * 0.7978845608 * (
        1.0 + 3.0 * 0.044715 * value * value
    )
    return act, slope


def kernel(
    nz, nb, lon, lat, ch, units,
    fields_h, land_h, w_in_h, w_out_h, gain_h, offset_h, target_h,
    output_h, grad_in_h, grad_out_h, gain_gradient_h, offset_gradient_h,
    output, grad_in, grad_out, gain_gradient, offset_gradient,
    fields, land, w_in, w_out, gain, offset, target,
    mask, first, dact, dpre, s_in, s_act, s_dout, w_back, dout_t,
    rows1, rows2, heads, tails, wests, easts,
    stats, ghost_f, ghost_d, ghost_a, fold,
    acc_a, north_t,
    part_a, pair_a, half_a, cross_a, mine_a, ring_a, full_a,
    part_b, pair_b, half_b, cross_b, mine_b, ring_b, full_b,
    load_sems, store_sems, row_sems, col_sems, stat_sems, pair_sems, cross_sems, ring_sems, full_sems,
):
    nd = nz * nb
    nx = nb // 2
    cells = lon * lat
    z = lax.axis_index("space")
    b = lax.axis_index("batch")
    me = z * nb + b
    core = lax.rem(b, 2)
    col = b // 2
    other = 1 - core

    def device(zz, bb):
        return {"space": zz, "batch": bb}

    def copy(src, dst, send, recv, zz, bb):
        return pltpu.make_async_remote_copy(
            src_ref=src, dst_ref=dst, send_sem=send, recv_sem=recv,
            device_id=device(zz, bb), device_id_type=pl.DeviceIdType.MESH,
        )

    def over(count, fn):
        if count <= 4:
            for k in range(1, count):
                fn(k)
            return

        def step(k, carry):
            fn(k)
            return carry
        lax.fori_loop(1, count, step, 0)

    def row_copy(which, buf, slot, zz):
        return copy(buf.at[slot], buf.at[slot], row_sems.at[which, 0, zz],
                    row_sems.at[which, 1, slot], zz, b)

    def send_rows(which, buf):
        over(nz, lambda k: row_copy(which, buf, z, lax.rem(z + k, nz)).start())

    def recv_rows(which, buf):
        def one(k):
            src = lax.rem(z + k, nz)
            row_copy(which, buf, src, src).wait_recv()
        over(nz, one)

    def drain_rows(which, buf):
        over(nz, lambda k: row_copy(which, buf, z, lax.rem(z + k, nz)).wait_send())

    up = lax.rem(z + 1, nz)
    down = lax.rem(z + nz - 1, nz)

    def col_copies(which):
        return (
            copy(heads.at[which], easts.at[which], col_sems.at[which, 0, 0], col_sems.at[which, 1, 0], down, b),
            copy(tails.at[which], wests.at[which], col_sems.at[which, 0, 1], col_sems.at[which, 1, 1], up, b),
        )

    def stat_copy(which, slot, peer):
        return copy(stats.at[which, slot], stats.at[which, slot], stat_sems.at[which, 0, peer],
                    stat_sems.at[which, 1, slot], peer // nb, lax.rem(peer, nb))

    def send_stats(which):
        over(nd, lambda k: stat_copy(which, me, lax.rem(me + k, nd)).start())

    def recv_stats(which):
        def one(k):
            src = lax.rem(me + k, nd)
            stat_copy(which, src, src).wait_recv()
        over(nd, one)
        acc = stats[which, 0]
        for k in range(1, nd):
            acc = acc + stats[which, k]
        return acc

    def drain_stats(which):
        over(nd, lambda k: stat_copy(which, me, lax.rem(me + k, nd)).wait_send())

    loads = [
        pltpu.make_async_copy(src, dst, load_sems.at[k])
        for k, (src, dst) in enumerate((
            (land_h, land), (fields_h, fields), (target_h, target), (w_in_h, w_in),
            (w_out_h, w_out), (gain_h, gain), (offset_h, offset)))
    ]
    for load in loads:
        load.start()
    stores = [
        pltpu.make_async_copy(src, dst, store_sems.at[k])
        for k, (src, dst) in enumerate((
            (output, output_h), (grad_in, grad_in_h), (grad_out, grad_out_h),
            (gain_gradient, gain_gradient_h), (offset_gradient, offset_gradient_h)))
    ]

    barrier = pltpu.get_barrier_semaphore()

    def greet(k):
        peer = lax.rem(me + k, nd)
        pl.semaphore_signal(barrier, inc=1, device_id=device(peer // nb, lax.rem(peer, nb)),
                            device_id_type=pl.DeviceIdType.MESH)
    over(nd, greet)

    row_id = lax.broadcasted_iota(jnp.int32, (lat, ch), 0)
    zero_row = jnp.zeros((1, ch), F32)

    loads[0].wait()
    land_f = land[...].astype(F32)
    diagonal = lax.broadcasted_iota(jnp.int32, (lat, lat), 0) == lax.broadcasted_iota(
        jnp.int32, (lat, lat), 1)
    spread = jnp.concatenate(
        [jnp.where(diagonal, land_f[i:i + 1, :], 0.0) for i in range(lon)], axis=0)
    mask[...] = jnp.dot(spread.astype(BF16), jnp.ones((lat, ch), BF16), preferred_element_type=F32)

    def at(i):
        return pl.ds(pl.multiple_of(i * lat, lat), lat)

    def loop(start, stop, fn):
        def step(i, carry):
            fn(i)
            return carry
        lax.fori_loop(start, stop, step, 0)

    def shift_up(v, ghost):
        return jnp.concatenate([v[1:], ghost], axis=0)

    def shift_down(v):
        return jnp.concatenate([zero_row, v[:-1]], axis=0)

    def put(s, i, v, lane):
        s[i, :, lane * ch:(lane + 1) * ch] = v.astype(BF16)

    loads[1].wait()
    def base(s, i, v):
        put(s, i, shift_down(v), 0)
        put(s, i, v, 1)
        put(s, i, shift_up(v, zero_row), 2)

    def mask_lon(i):
        base(s_in, i + 1, fields[0, i].astype(F32) * mask[at(i)])
    loop(0, lon, mask_lon)
    heads[0] = s_in[1, :, ch:2 * ch]
    tails[0] = s_in[lon, :, ch:2 * ch]
    cols1 = col_copies(0)
    cols_t = col_copies(1)
    pl.semaphore_wait(barrier, nd - 1)
    for c in cols1:
        c.start()

    loads[2].wait()

    def mask_target(i):
        target[0, i] = (target[0, i].astype(F32) * mask[at(i)]).astype(BF16)
    loop(0, lon, mask_target)

    halves = []
    for h in range(2):
        half = mask[h * cells // 2:(h + 1) * cells // 2]
        halves.append(jnp.broadcast_to(jnp.sum(half, axis=0, keepdims=True), (8, ch)))
    rows1[z] = jnp.concatenate(
        [s_in[i + 1, lat - 16:, ch:2 * ch].astype(F32)[15:] for i in range(lon)]
        + [target[0, i, lat - 16:].astype(F32)[15:] for i in range(lon)] + halves, axis=0
    ).astype(BF16)
    heads[1] = target[0, 0]
    tails[1] = target[0, lon - 1]

    send_rows(0, rows1)
    for c in cols_t:
        c.start()

    for i in (0, lon + 1):
        s_in[i] = jnp.zeros((lat, 3 * ch), BF16)

    def window(s, f):
        return s[pl.ds(f, lon)].reshape(cells, 3 * ch)

    def conv_half(s, w, out, h, order=(0, 1, 2)):
        part_lon = lon // 2
        acc = jnp.zeros((part_lon * lat, ch), F32)
        for f in range(3):
            piece = s[pl.ds(h * part_lon + order[f], part_lon)].reshape(part_lon * lat, 3 * ch)
            acc += jnp.dot(piece, w[f], preferred_element_type=F32)
        out[pl.ds(pl.multiple_of(h * part_lon * lat, part_lon * lat), part_lon * lat)] = acc

    def conv(s, w, out, order=(0, 1, 2)):
        loop(0, 2, lambda h: conv_half(s, w, out, h, order))

    def fold_part(rows, w):
        acc = jnp.zeros((2 * lon, ch), F32)
        for f in range(3):
            piece = jnp.concatenate(rows[f:f + lon] + [jnp.zeros((lon, ch), F32)], axis=0)
            acc += jnp.dot(piece.astype(BF16), w[f, 2 * ch:3 * ch, :], preferred_element_type=F32)
        return acc

    def north(v, row):
        return v + jnp.where(row_id == lat - 1, row, 0.0)

    loads[3].wait()
    conv(s_in, w_in, first)
    for load in loads[4:]:
        load.wait()

    for c in cols1:
        c.wait_recv()
    recv_rows(0, rows1)

    opposite = nz - 1 - z
    beyond = lax.rem(nz - z, nz)
    before = lax.rem(2 * nz - 2 - z, nz)

    def ghosts(buf, start):
        facing = buf[opposite].astype(F32)
        left = buf[beyond].astype(F32)[start:start + 1]
        right = buf[before].astype(F32)[start + lon - 1:start + lon]
        return [left] + [facing[start + lon - 1 - i:start + lon - i] for i in range(lon)] + [right]

    ghost_in = ghosts(rows1, 0)
    for i, v in ((0, wests[0].astype(F32)), (lon + 1, easts[0].astype(F32))):
        put(s_in, i, shift_down(v), 0)
        put(s_in, i, v, 1)
        put(s_in, i, shift_up(v, ghost_in[i]), 2)
    from_west = jnp.dot(s_in[0], w_in[0], preferred_element_type=F32)
    from_east = jnp.dot(s_in[lon + 1], w_in[2], preferred_element_type=F32)
    fold[0] = fold_part([zero_row] + ghost_in[1:lon + 1] + [zero_row], w_in)
    for i in range(lon + 2):
        ghost_f[i] = ghost_in[i]
    first[at(0)] += from_west
    first[at(lon - 1)] += from_east

    def first_lon(i, sums):
        v = north(first[at(i)], fold[0, pl.ds(i, 1)])
        v = v.astype(BF16).astype(F32)
        first[at(i)] = v
        held = v * mask[at(i)]
        return sums[0] + held, sums[1] + held * v
    zeros = jnp.zeros((lat, ch), F32)
    sum_1, sum_2 = lax.fori_loop(0, lon, first_lon, (zeros, zeros))
    stats[0, me, 0:1] = jnp.sum(sum_1, axis=0, keepdims=True)
    stats[0, me, 1:2] = jnp.sum(sum_2, axis=0, keepdims=True)
    send_stats(0)

    def turn(f):
        for t in range(3):
            w = w_out[f, t * ch:(t + 1) * ch, :].astype(F32)
            w_back[f, t * ch:(t + 1) * ch, :] = w.T.astype(BF16)
    loop(0, 3, turn)

    count = zero_row
    for k in range(nz):
        packet = rows1[k].astype(F32)
        count = count + packet[16:17] + packet[24:25]
    count = count * float(nb)
    scale = lax.rsqrt(count)

    def scaled(v):
        return (v * scale).astype(BF16).astype(F32)

    for c in cols_t:
        c.wait_recv()
    def base_dout(i, v):
        put(s_dout, i, shift_up(v, zero_row), 0)
        put(s_dout, i, v, 1)
        put(s_dout, i, shift_down(v), 2)

    def lanes(k):
        return pl.ds(pl.multiple_of(k * 2 * lat, 2 * lat), 2 * lat)

    def dout_pair(k):
        pair = [scaled(target[0, 2 * k + t].astype(F32)) for t in range(2)]
        for t in range(2):
            base_dout(2 * k + t + 1, pair[t])
        dout_t[:, lanes(k)] = jnp.concatenate(pair, axis=0).T.astype(BF16)
    loop(0, lon // 2, dout_pair)
    base_dout(0, scaled(wests[1].astype(F32)))
    base_dout(lon + 1, scaled(easts[1].astype(F32)))
    ghost_dout = [scaled(v) for v in ghosts(rows1, lon)]
    north_d = [s_dout[i + 1, lat - 16:, ch:2 * ch].astype(F32)[15:] for i in range(lon)]
    north_t[...] = jnp.concatenate(
        north_d + [jnp.zeros((ch - lon, ch), F32)], axis=0).T.astype(BF16)
    conv(s_dout, w_back, dact, (2, 1, 0))
    fold[1] = fold_part(ghost_dout, w_back)

    def finish_lon(i):
        dact[at(i)] = north(dact[at(i)], fold[1, pl.ds(i, 1)]) * mask[at(i)]
        v = s_in[i + 1, :, ch:2 * ch].astype(F32)
        put(s_in, i + 1, shift_up(v, ghost_f[i + 1]), 2)
    loop(0, lon, finish_lon)

    acc = recv_stats(0)
    mean = acc[0:1] / count
    var = acc[1:2] / count - mean * mean
    inverse = lax.rsqrt(var + 1e-05)
    gains = gain[...]
    offsets = offset[...]

    def act_lon(i, sums):
        xhat = (first[at(i)] - mean) * inverse
        act, slope = gelu_parts(gains * xhat + offsets)
        d = dact[at(i)] * slope
        dpre[at(i)] = d
        base(s_act, i + 1, (act * mask[at(i)]).astype(BF16).astype(F32))
        return sums[0] + d, sums[1] + d * xhat
    sum_1, sum_2 = lax.fori_loop(0, lon, act_lon, (zeros, zeros))
    sum_off = jnp.sum(sum_1, axis=0, keepdims=True)
    sum_gain = jnp.sum(sum_2, axis=0, keepdims=True)
    stats[1, me, 0:1] = sum_off
    stats[1, me, 1:2] = sum_gain
    send_stats(1)
    heads[2] = s_act[1, :, ch:2 * ch]
    tails[2] = s_act[lon, :, ch:2 * ch]
    last = [s_act[i + 1, lat - 16:, ch:2 * ch].astype(F32)[15:] for i in range(lon)]
    rows2[z] = jnp.concatenate(last + [jnp.zeros((lon, ch), F32)], axis=0).astype(BF16)
    cols2 = col_copies(2)
    for c in cols2:
        c.start()
    send_rows(1, rows2)

    for i in (0, lon + 1):
        s_act[i] = jnp.zeros((lat, 3 * ch), BF16)

    def own_a(f):
        acc_a[f] = jnp.dot(dout_t[...], window(s_act, f), preferred_element_type=F32)
    loop(0, 3, own_a)

    for c in cols2:
        c.wait_recv()
    recv_rows(1, rows2)
    ghost_act = ghosts(rows2, 0)
    for i in range(lon + 2):
        ghost_a[i] = ghost_act[i]
    for i, v in ((0, wests[2].astype(F32)), (lon + 1, easts[2].astype(F32))):
        put(s_act, i, shift_down(v), 0)
        put(s_act, i, v, 1)
        put(s_act, i, shift_up(v, ghost_act[i]), 2)
    blank = jnp.zeros((lat, 3 * ch), BF16)
    acc_a[0] += jnp.dot(dout_t[:, 0:2 * lat], jnp.concatenate([s_act[0], blank], axis=0),
                        preferred_element_type=F32)
    acc_a[2] += jnp.dot(dout_t[:, cells - 2 * lat:],
                        jnp.concatenate([blank, s_act[lon + 1]], axis=0),
                        preferred_element_type=F32)
    inner = [zero_row] + ghost_act[1:lon + 1] + [zero_row]
    for f in range(3):
        piece = jnp.concatenate(inner[f:f + lon] + [jnp.zeros((ch - lon, ch), F32)], axis=0)
        acc_a[f, :, 2 * ch:] += jnp.dot(north_t[...], piece.astype(BF16),
                                        preferred_element_type=F32)

    share = ch // nb
    live = 9 * share
    padded = units * 16 * nz

    def rows_of(f):
        return pl.ds(pl.multiple_of(3 * f * share, 16), 3 * share)

    def pair_copy(which, f, part, pair):
        return copy(part.at[other, :, rows_of(f)], pair.at[:, rows_of(f)],
                    pair_sems.at[which, 0, f], pair_sems.at[which, 1, f], z, 2 * col + other)

    def cross_copy(which, f, half, cross, slot, peer, x):
        return copy(half.at[peer, rows_of(f)], cross.at[slot, rows_of(f)],
                    cross_sems.at[which, 0, f, peer], cross_sems.at[which, 1, f, slot],
                    z, 2 * x + core)

    def send_part(which, f, g, part, pair):
        for t in range(3):
            row = pl.ds(pl.multiple_of((3 * f + t) * share, 16), share)
            for k in range(nb):
                part[k % 2, k // 2, row, :] = (
                    g[k * share:(k + 1) * share, t * ch:(t + 1) * ch].astype(BF16))
        pair_copy(which, f, part, pair).start()

    def ring_copy(which, mine, ring, slot, peer):
        return copy(mine.at[peer], ring.at[slot], ring_sems.at[which, 0, peer],
                    ring_sems.at[which, 1, slot], peer, b)

    def full_copy(which, full, slot, peer):
        return copy(full.at[slot], full.at[slot], full_sems.at[which, 0, peer],
                    full_sems.at[which, 1, slot], peer, b)

    def after_pair(which, part, pair, half, cross):
        def one_f(f):
            pair_copy(which, f, part, pair).wait_recv()

            def summed(x):
                return (part[core, x, rows_of(f)].astype(F32)
                        + pair[x, rows_of(f)].astype(F32)).astype(BF16)

            def one(k):
                x = lax.rem(col + k, nx)
                half[x, rows_of(f)] = summed(x)
                cross_copy(which, f, half, cross, col, x, x).start()
            over(nx, one)
            half[col, rows_of(f)] = summed(col)
        loop(0, 3, one_f)

    def after_cross(which, half, cross, mine, ring):
        acc = half[col].astype(F32)
        for k in range(1, nx):
            x = lax.rem(col + k, nx)
            for f in range(3):
                cross_copy(which, f, half, cross, x, x, x).wait_recv()
            acc = acc + cross[x].astype(F32)
        if padded > live:
            acc = jnp.concatenate([acc, jnp.zeros((padded - live, ch), F32)], axis=0)
        for k in range(nz):
            mine[k] = acc[k * units * 16:(k + 1) * units * 16].astype(BF16)

        def one(k):
            peer = lax.rem(z + k, nz)
            ring_copy(which, mine, ring, z, peer).start()
        over(nz, one)

    def after_ring(which, mine, ring, full):
        acc = mine[z].astype(F32)
        for k in range(1, nz):
            src = lax.rem(z + k, nz)
            ring_copy(which, mine, ring, src, src).wait_recv()
            acc = acc + ring[src].astype(F32)
        full[z] = acc.astype(BF16)

        def one(k):
            full_copy(which, full, z, lax.rem(z + k, nz)).start()
        over(nz, one)

    def after_full(which, full, out):
        def one(k):
            src = lax.rem(z + k, nz)
            full_copy(which, full, src, src).wait_recv()
        over(nz, one)
        out[...] = full[...].reshape(padded, ch)[0:live].astype(F32)

    def drain(which, part, pair, half, cross, mine, ring, full):
        for f in range(3):
            pair_copy(which, f, part, pair).wait_send()

            def one_x(k):
                x = lax.rem(col + k, nx)
                cross_copy(which, f, half, cross, col, x, x).wait_send()
            over(nx, one_x)

        def one_z(k):
            peer = lax.rem(z + k, nz)
            ring_copy(which, mine, ring, z, peer).wait_send()
            full_copy(which, full, z, peer).wait_send()
        over(nz, one_z)

    loop(0, 3, lambda f: send_part(0, f, acc_a[f], part_a, pair_a))

    acc = recv_stats(1)
    off_total = acc[0:1]
    gain_total = acc[1:2]
    offset_gradient[...] = off_total
    gain_gradient[...] = gain_total
    stores[3].start()
    stores[4].start()
    scale_in = gains * inverse
    off_mean = off_total / count
    gain_mean = gain_total / count

    def dfirst_pair(k):
        pieces = []
        for j in (2 * k, 2 * k + 1):
            xhat = (first[at(j)] - mean) * inverse
            pieces.append(mask[at(j)] * scale_in * (dpre[at(j)] - (off_mean + xhat * gain_mean)))
        dout_t[:, lanes(k)] = jnp.concatenate(pieces, axis=0).T.astype(BF16)
    loop(0, lon // 2, dfirst_pair)
    after_pair(0, part_a, pair_a, half_a, cross_a)

    def tap_b(f):
        g = jnp.dot(dout_t[...], window(s_in, f), preferred_element_type=F32)
        send_part(1, f, g, part_b, pair_b)
    loop(0, 3, tap_b)

    after_pair(1, part_b, pair_b, half_b, cross_b)
    after_cross(0, half_a, cross_a, mine_a, ring_a)
    after_cross(1, half_b, cross_b, mine_b, ring_b)

    def finish_act(i):
        v = s_act[i + 1, :, ch:2 * ch].astype(F32)
        put(s_act, i + 1, shift_up(v, ghost_a[i + 1]), 2)
    loop(0, lon, finish_act)
    conv(s_act, w_out, dact)

    def out_lon(i):
        output[0, i] = (dact[at(i)] * mask[at(i)]).astype(BF16)
    loop(0, lon, out_lon)
    stores[0].start()
    after_ring(0, mine_a, ring_a, full_a)
    after_ring(1, mine_b, ring_b, full_b)
    after_full(0, full_a, grad_out)
    stores[2].start()
    after_full(1, full_b, grad_in)
    stores[1].start()

    for c in cols1 + cols_t + cols2:
        c.wait_send()
    drain_rows(0, rows1)
    drain_rows(1, rows2)
    drain_stats(0)
    drain_stats(1)
    drain(0, part_a, pair_a, half_a, cross_a, mine_a, ring_a, full_a)
    drain(1, part_b, pair_b, half_b, cross_b, mine_b, ring_b, full_b)
    for store in stores:
        store.wait()


def writer(*refs):
    sources, results, held, sems = refs[:5], refs[5:10], refs[10:15], refs[15]
    loads = [pltpu.make_async_copy(sources[k], held[k], sems.at[0, k]) for k in range(5)]
    stores = [pltpu.make_async_copy(held[k], results[k], sems.at[1, k]) for k in range(5)]
    for c in loads:
        c.start()
    for load, store in zip(loads, stores):
        load.wait()
        store.start()
    for c in stores:
        c.wait()


def body(nz, nb, fields, land, conv_in, conv_out, gain, offset, target):
    lon, lat, ch = fields.shape[1:]
    nd = nz * nb
    nx = nb // 2
    share = ch // nb
    units = -(-(9 * share // 16) // nz)
    padded = units * 16 * nz
    vm = pltpu.VMEM
    reduction = [
        vm((2, nx, 9 * share, ch), BF16),
        vm((nx, 9 * share, ch), BF16),
        vm((nx, 9 * share, ch), BF16),
        vm((nx, 9 * share, ch), BF16),
        vm((nz, units * 16, ch), BF16),
        vm((nz, units * 16, ch), BF16),
        vm((nz, units * 16, ch), BF16),
    ]
    dma = pltpu.SemaphoreType.DMA
    scratch = [
        vm(fields.shape, BF16),
        vm((9 * share, ch), F32),
        vm((9 * share, ch), F32),
        vm((1, ch), F32),
        vm((1, ch), F32),
        vm(fields.shape, BF16),
        vm(land.shape, jnp.int32),
        vm((3, 3 * ch, ch), BF16),
        vm((3, 3 * ch, ch), BF16),
        vm((1, ch), F32),
        vm((1, ch), F32),
        vm(target.shape, BF16),
        vm((lon * lat, ch), F32),
        vm((lon * lat, ch), F32),
        vm((lon * lat, ch), F32),
        vm((lon * lat, ch), F32),
        vm((lon + 2, lat, 3 * ch), BF16),
        vm((lon + 2, lat, 3 * ch), BF16),
        vm((lon + 2, lat, 3 * ch), BF16),
        vm((3, 3 * ch, ch), BF16),
        vm((ch, lon * lat), BF16),
        vm((nz, 32, ch), BF16),
        vm((nz, 16, ch), BF16),
        vm((3, lat, ch), BF16), vm((3, lat, ch), BF16),
        vm((3, lat, ch), BF16), vm((3, lat, ch), BF16),
        vm((2, nd, 2, ch), F32),
        vm((lon + 2, 1, ch), F32),
        vm((lon + 2, 1, ch), F32),
        vm((lon + 2, 1, ch), F32),
        vm((2, 2 * lon, ch), F32),
        vm((3, ch, 3 * ch), F32),
        vm((ch, ch), BF16),
        *reduction,
        *reduction,
        dma((7,)),
        dma((5,)),
        dma((2, 2, nz)),
        dma((3, 2, 2)),
        dma((2, 2, nd)),
        dma((2, 2, 3)),
        dma((2, 2, 3, nx)),
        dma((2, 2, nz)),
        dma((2, 2, nz)),
    ]
    anywhere = pl.BlockSpec(memory_space=pl.ANY)
    limit = 62 * 1024 * 1024
    results = pl.pallas_call(
        functools.partial(kernel, nz, nb, lon, lat, ch, units),
        out_shape=(
            jax.ShapeDtypeStruct(fields.shape, BF16),
            jax.ShapeDtypeStruct((9 * share, ch), F32),
            jax.ShapeDtypeStruct((9 * share, ch), F32),
            jax.ShapeDtypeStruct((1, ch), F32),
            jax.ShapeDtypeStruct((1, ch), F32),
        ),
        in_specs=[anywhere] * 7,
        out_specs=(anywhere,) * 5,
        scratch_shapes=scratch,
        compiler_params=pltpu.CompilerParams(
            collective_id=0, has_side_effects=True, vmem_limit_bytes=limit
        ),
    )(
        fields, land,
        conv_in.reshape(3, 3 * ch, ch), conv_out.reshape(3, 3 * ch, ch),
        gain.reshape(1, ch), offset.reshape(1, ch), target,
    )

    out, grad_in, grad_out, gain_gradient, offset_gradient = pl.pallas_call(
        writer,
        out_shape=tuple(jax.ShapeDtypeStruct(r.shape, r.dtype) for r in results),
        in_specs=[anywhere] * 5,
        out_specs=(anywhere,) * 5,
        scratch_shapes=[vm(r.shape, r.dtype) for r in results] + [dma((2, 5))],
        compiler_params=pltpu.CompilerParams(vmem_limit_bytes=limit),
    )(*results)

    def taps(g):
        return g.reshape(9, share, ch).transpose(0, 2, 1)

    return (out, taps(grad_in), taps(grad_out),
            gain_gradient.reshape(ch), offset_gradient.reshape(ch))


def solution(mesh):
    in_specs = (
        P(("groups", "batch"), "space", None, None),
        P("space", None),
        P(),
        P(),
        P(),
        P(),
        P(("groups", "batch"), "space", None, None),
    )
    out_specs = (
        P(("groups", "batch"), "space", None, None),
        P("groups", None, "batch"),
        P("groups", None, "batch"),
        P("groups"),
        P("groups"),
    )
    step = functools.partial(body, mesh.shape["space"], mesh.shape["batch"])
    return jax.shard_map(step, mesh=mesh, in_specs=in_specs, out_specs=out_specs, check_vma=False)
```
